32 devices in a mesh: lat: 4 (over y, x), ord: 8 (over z, core).
Axes of the slice: x: 2, y: 2, z: 4, core: 2. Of those that a mesh axis runs over, the one named last changes fastest.
Arguments:
- field: bfloat16 [32, 64, 256], P(('lat', 'ord')), may hold values from -6 to 6
- tap_mask: int32 [32, 8, 15], P(('lat', 'ord')), may hold values 0 or 1
- tap_weight: float32 [32, 8, 15], P(('lat', 'ord')), may hold values from -1.4 to 1.4
- basis_mix: bfloat16 [8, 256, 256], replicated, may hold values from -0.125 to 0.125
- order_slots: int32 [32], replicated, may hold values from 0 to 31, each once
- degree_gain: float32 [32, 256], replicated, may hold values from 0.3 to 3
- spectral_mix: bfloat16 [2, 256, 256], replicated, may hold values from -0.25 to 0.25
Outputs:
- spectrum: bfloat16 [32, 32, 2, 256], P('lat', 'ord')
The draws below stay inside these ranges and needn't reach their ends.
Inputs may be any that keep to these rules, and one draw needn't show every extreme that they name: `order_slots`: each order 0 to 31 stands in exactly one slot.
All inputs are finite; a program needn't handle non-finite values. No bound on the sum of `tap_mask` on one device may be relied on, other than what follows from the above.
Results may differ from the reference program's by a relative error of at most 0.0095.
Values may be sent and summed in bfloat16 or wider, within the bound.
A program may use at most 64 MiB of HBM per device.

```python
import math
import jax
import jax.numpy as jnp
from jax import lax

C = 256
NB = 8
TAPS = 15
NLAT = 32
NLON = 64
M = 32


def place_ends(array, key, low, top_value):
    place = [jax.random.randint(jax.random.fold_in(key, axis), (), 0, length) for axis, length in enumerate(array.shape)]
    widest = array.shape.index(max(array.shape))
    beside = place[:widest] + [(place[widest] + 1) % array.shape[widest]] + place[widest + 1:]
    return array.at[tuple(place)].set(low).at[tuple(beside)].set(top_value)


def levels(key, dims, cuts, low, largest):
    def one(position, parts):
        heights = jax.random.uniform(jax.random.fold_in(jax.random.fold_in(key, 6), position), (parts,), jnp.float32, low / len(cuts), largest / len(cuts))
        return jnp.repeat(jnp.exp(heights), dims[position] // parts).reshape((-1,) + (1,) * (len(dims) - position - 1))

    loudness = one(*cuts[0])
    for cut in cuts[1:]:
        loudness = loudness * one(*cut)
    return loudness


def scatter_about(rng, dims, spread, limit, cuts=(), held_as=jnp.bfloat16):
    values = jax.random.normal(rng, dims, jnp.float32) * spread
    if len(cuts) > 0:
        values = levels(rng, dims, cuts, -0.22, 0.18) * values
    return jnp.clip(values, min=-limit, max=limit).astype(held_as)


def setup_inputs(seed: int = 0) -> dict:
    key_list = jax.random.split(jax.random.key(seed), 8)
    field = scatter_about(key_list[0], (NLAT, NLON, C), 1.0, 6.0, ((0, 32),))
    tap_mask = place_ends((jax.random.randint(key_list[1], (NLAT, NB, TAPS), 0, 3) < 2).astype(jnp.int32), jax.random.fold_in(key_list[1], 1), 0, 1)
    tap_weight = scatter_about(key_list[2], (NLAT, NB, TAPS), 0.35, 1.4, ((0, 32),), jnp.float32)
    basis_mix = scatter_about(key_list[3], (NB, C, C), (NB * C) ** -0.5, 0.125)
    order_slots = jax.random.permutation(key_list[4], M).astype(jnp.int32)
    degree_gain = jnp.clip(jnp.exp(jax.random.uniform(key_list[5], (NLAT, C), jnp.float32, math.log(0.3), math.log(3.0))), 0.3, 3.0)
    spectral_mix = scatter_about(key_list[6], (2, C, C), (2 * C) ** -0.5, 0.25)
    return {"field": field, "tap_mask": tap_mask, "tap_weight": tap_weight, "basis_mix": basis_mix, "order_slots": order_slots, "degree_gain": degree_gain, "spectral_mix": spectral_mix}


def fourier_table(order_slots, n_lon):
    orders = order_slots.astype(jnp.int32)
    points = jnp.arange(n_lon, dtype=jnp.int32)
    phase_int = orders[:, None] * points[None, :] % n_lon
    angles = phase_int.astype(jnp.float32) * (2.0 * math.pi / n_lon)
    factor = 1.0 / math.sqrt(n_lon)
    stacked = jnp.stack([jnp.cos(angles) * factor, -jnp.sin(angles) * factor], axis=1)
    return stacked.reshape(2 * orders.shape[0], n_lon).astype(jnp.bfloat16)

def latitude_table(orders, wavenumbers, lat_rows, n_lat):
    phase_int = wavenumbers[None, :, None] * (2 * lat_rows[None, None, :] + 1) % (4 * n_lat)
    angles = phase_int.astype(jnp.float32) * (math.pi / (2 * n_lat))
    factor = math.sqrt(2.0 / n_lat)
    is_even = (orders % 2 == 0)[:, None, None]
    return (jnp.where(is_even, jnp.cos(angles), jnp.sin(angles)) * factor).astype(jnp.bfloat16)

def disco(lat_rows, filters, out_rows):
    running = None
    for lat_step in range(3):
        cycle_rows = lat_rows[lat_step:lat_step + out_rows].astype(jnp.float32)
        for lon_step in range(5):
            shifted = jnp.roll(cycle_rows, 2 - lon_step, axis=1)
            tap_vals = filters[:, :, 5 * lat_step + lon_step]
            tap_term = tap_vals[:, None, :, None] * shifted[:, :, None, :]
            running = tap_term if running is None else running + tap_term
    return running.astype(jnp.bfloat16)

def mixing(spectral_mix):
    real_part = spectral_mix[0]
    imag_part = spectral_mix[1]
    top_rows = jnp.concatenate([real_part, imag_part], axis=1)
    bottom_rows = jnp.concatenate([-imag_part, real_part], axis=1)
    return jnp.concatenate([top_rows, bottom_rows], axis=0)

def reference(field, tap_mask, tap_weight, basis_mix, order_slots, degree_gain, spectral_mix):
    n_lat, n_lon, channels = field.shape
    basis_count = basis_mix.shape[0]
    n_orders = order_slots.shape[0]
    filters = tap_mask.astype(jnp.float32) * tap_weight
    padded = jnp.pad(field, ((1, 1), (0, 0), (0, 0)))
    weights = basis_mix.reshape(basis_count * channels, channels)
    dft_table = fourier_table(order_slots, n_lon).astype(jnp.float32)
    row_block = 16

    def one_block(block_index):
        offset = block_index * row_block
        lat_rows = lax.dynamic_slice_in_dim(padded, offset, row_block + 2, 0)
        filter_rows = lax.dynamic_slice_in_dim(filters, offset, row_block, 0)
        tap_sums = disco(lat_rows, filter_rows, row_block)
        grid_rows = jnp.dot(tap_sums.reshape(row_block * n_lon, basis_count * channels), weights, preferred_element_type=jnp.float32).astype(jnp.bfloat16)
        grid_rows = grid_rows.reshape(row_block, n_lon, channels).astype(jnp.float32)
        spectra = jnp.einsum('fj,rjc->rfc', dft_table, grid_rows)
        return spectra.astype(jnp.bfloat16)
    fourier = lax.map(one_block, jnp.arange(n_lat // row_block, dtype=jnp.int32))
    fourier = fourier.reshape(n_lat, n_orders, 2, channels)
    wavenumbers = jnp.arange(n_lat, dtype=jnp.int32)
    mix_matrix = mixing(spectral_mix)

    def one_slot(slot_index):
        order_one = lax.dynamic_slice_in_dim(order_slots, slot_index, 1)
        lat_basis = latitude_table(order_one, wavenumbers, wavenumbers, n_lat)[0]
        column = lax.dynamic_index_in_dim(fourier, slot_index, 1, keepdims=False)
        coefficients = jnp.dot(lat_basis, column.reshape(n_lat, 2 * channels), preferred_element_type=jnp.float32)
        scaled = (coefficients.reshape(n_lat, 2, channels) * degree_gain[:, None, :]).astype(jnp.bfloat16)
        return jnp.dot(scaled.reshape(n_lat, 2 * channels), mix_matrix, preferred_element_type=jnp.float32).astype(jnp.bfloat16)
    result = lax.map(one_slot, jnp.arange(n_orders, dtype=jnp.int32))
    return jnp.transpose(result, (1, 0, 2)).reshape(n_lat, n_orders, 2, channels)
```

```python
import functools
import math

import jax
import jax.numpy as jnp
from jax import lax
from jax.experimental import pallas as pl
from jax.experimental.pallas import tpu as pltpu
from jax.sharding import PartitionSpec as P

MESH = pl.DeviceIdType.MESH
F32 = jnp.float32
BF16 = jnp.bfloat16
SLAB = 8
COLUMNS = 256
LANES = 128


def log2(n):
    assert n & (n - 1) == 0
    return n.bit_length() - 1


def cosine(phase_int, period):
    q = phase_int & (period - 1)
    r = jnp.minimum(q, period - q)
    x = (period // 4 - r).astype(F32) * (2.0 * math.pi / period)
    x2 = x * x
    total = jnp.full_like(x, -1.0 / math.factorial(11))
    for power, sign in ((9, 1.0), (7, -1.0), (5, 1.0), (3, -1.0), (1, 1.0)):
        total = total * x2 + sign / math.factorial(power)
    return total * x


def iota(shape, dim):
    return lax.broadcasted_iota(jnp.int32, shape, dim)


def repeat(count, body):
    if count == 1:
        body(0)
    else:
        pl.loop(0, count)(body)


def kernel(
    dims,
    mask_hbm, weight_hbm, slots_hbm, field_hbm, basis_hbm, gain_hbm, spectral_hbm,
    out_ref,
    mask_ref, weight_ref, slots_ref, slots_smem, field, basis, gain, spectral, table, filt, sent, held, lat_tab, left, mixed,
    local_sem, filt_send, filt_recv, all_send, all_recv,
):
    n_lat_dev, n_ord_dev, n_lat, n_lon, n_orders, channels, basis_count = dims
    lat_id = lax.axis_index("lat")
    ord_id = lax.axis_index("ord")
    row_id = lat_id * n_ord_dev + ord_id
    slots_here = n_orders // n_ord_dev
    waves = n_lat // n_lat_dev
    per_slab = min(SLAB // 2, slots_here)
    width = 2 * per_slab
    groups = slots_here // per_slab
    count = n_lat_dev * n_ord_dev
    ord_mask = n_ord_dev - 1
    ord_bits = log2(n_ord_dev)
    lat_rows = min(n_lat, COLUMNS // width)
    parts = n_lat // lat_rows
    cols = lat_rows * width
    out_rows = waves * width

    def each_target(body):
        if count <= 64:
            for step in sorted(range(1, count), key=lambda step: (-(step & ord_mask), -step)):
                body((lat_id ^ (step >> ord_bits), ord_id ^ (step & ord_mask)))
        else:
            def one(step):
                body((lat_id ^ (step >> ord_bits), ord_id ^ (step & ord_mask)))

            pl.loop(1, count)(one)

    slots_copy = pltpu.make_async_copy(slots_hbm, slots_ref, local_sem.at[0])
    field_copy = pltpu.make_async_copy(field_hbm, field, local_sem.at[1])
    mask_copy = pltpu.make_async_copy(mask_hbm, mask_ref, local_sem.at[2])
    weight_copy = pltpu.make_async_copy(weight_hbm, weight_ref, local_sem.at[3])
    smem_copy = pltpu.make_async_copy(slots_hbm, slots_smem, local_sem.at[4])
    gain_copy = pltpu.make_async_copy(
        gain_hbm.at[pl.ds(pl.multiple_of(lat_id * waves, waves), waves)], gain, local_sem.at[5]
    )
    spectral_copy = pltpu.make_async_copy(spectral_hbm, spectral, local_sem.at[6])
    basis_copy = pltpu.make_async_copy(basis_hbm, basis, local_sem.at[7])
    slots_copy.start()
    field_copy.start()
    mask_copy.start()
    weight_copy.start()
    smem_copy.start()
    basis_copy.start()
    gain_copy.start()
    spectral_copy.start()

    barrier = pltpu.get_barrier_semaphore()

    def greet(target):
        pl.semaphore_signal(barrier, inc=1, device_id=target, device_id_type=MESH)

    each_target(greet)

    filt[0] = jnp.zeros((1, LANES), F32)
    filt[n_lat + 1] = jnp.zeros((1, LANES), F32)

    slots_copy.wait()
    orders = slots_ref[...]
    block_rows = table.shape[0]

    def dft_block(start):
        row = iota((block_rows, 1), 0) + start
        found = iota((block_rows, n_orders), 1) == row >> 1
        order = jnp.sum(jnp.where(found, orders.astype(F32), 0.0), axis=1, keepdims=True).astype(jnp.int32)
        phase = order * iota((block_rows, n_lon), 1) + (n_lon // 4) * (row & 1)
        table[...] = (cosine(phase, n_lon) * (1.0 / math.sqrt(n_lon))).astype(BF16)

    single_dft = block_rows == 2 * n_orders
    if single_dft:
        dft_block(0)
    slabs = block_rows // width

    mask_copy.wait()
    weight_copy.wait()
    taps = mask_ref[0].astype(F32) * weight_ref[0]
    tap_count = taps.shape[1]
    lane = iota((basis_count, LANES), 1)
    spread = jnp.zeros((basis_count, LANES), F32)
    for tap in range(tap_count):
        spread = jnp.where(lane // basis_count == tap, taps[:, tap:tap + 1], spread)
    spread = jnp.where(lane % basis_count == iota((basis_count, LANES), 0), spread, 0.0)
    filt[row_id + 1] = jnp.sum(spread, axis=0, keepdims=True)

    field_copy.wait()

    def transform(block):
        if not single_dft:
            dft_block(block * block_rows)
        rows = jnp.dot(table[...], field[0], preferred_element_type=F32).astype(BF16)
        sent[pl.ds(block * slabs, slabs)] = rows.reshape(slabs, width, channels)

    repeat(2 * n_orders // block_rows, transform)

    pl.semaphore_wait(barrier, count - 1)

    def send(target):
        pltpu.make_async_remote_copy(
            src_ref=filt.at[row_id + 1], dst_ref=filt.at[row_id + 1],
            send_sem=filt_send.at[0], recv_sem=filt_recv.at[0],
            device_id=target, device_id_type=MESH,
        ).start()
        pltpu.make_async_remote_copy(
            src_ref=sent.at[pl.ds(target[1] * groups, groups)], dst_ref=held.at[:, row_id],
            send_sem=all_send.at[0], recv_sem=all_recv.at[0],
            device_id=target, device_id_type=MESH,
        ).start()

    each_target(send)
    held[:, row_id] = sent[pl.ds(ord_id * groups, groups)]

    smem_copy.wait()

    def lane_orders(group):
        place = (iota((1, cols), 1) & (width - 1)) >> 1
        order = jnp.zeros((1, cols), jnp.int32)
        for slot in range(per_slab):
            order = jnp.where(place == slot, slots_smem[0, ord_id * slots_here + group * per_slab + slot], order)
        return order

    def lat_tables(group, part):
        order = lane_orders(group)
        col = iota((1, cols), 1)
        row = iota((out_rows, 1), 0)
        wave = (row >> log2(width)) + lat_id * waves
        same = ((row & (width - 1)) >> 1) == ((col & (width - 1)) >> 1)
        for step in range(3):
            lat = (col >> log2(width)) + part * lat_rows + 1 - step
            phase = wave * (2 * lat + 1) + jnp.where((order & 1) == 0, 0, 3 * n_lat)
            value = cosine(phase, 4 * n_lat) * math.sqrt(2.0 / n_lat)
            lat_tab[step] = jnp.where(same, value, 0.0)

    def tap_factors(group):
        order = lane_orders(group)
        row = iota((16, cols), 0)
        lon_step = (row & 7) - 2
        part_of = iota((16, cols), 1) & 1
        phase = order * lon_step + (n_lon // 4) * (part_of - (row >> 3))
        return cosine(phase, n_lon)

    single_lat = groups == 1 and parts == 1
    if single_lat:
        lat_tables(0, 0)
        factors = tap_factors(0)

    gain_copy.wait()
    spectral_copy.wait()
    basis_copy.wait()
    filt_arrivals = pltpu.make_async_remote_copy(
        src_ref=filt.at[pl.ds(0, count - 1)], dst_ref=filt.at[pl.ds(0, count - 1)],
        send_sem=filt_send.at[0], recv_sem=filt_recv.at[0],
        device_id=(lat_id, ord_id ^ 1), device_id_type=MESH,
    )
    arrivals = pltpu.make_async_remote_copy(
        src_ref=held.at[:, pl.ds(0, count - 1)], dst_ref=held.at[:, pl.ds(0, count - 1)],
        send_sem=all_send.at[0], recv_sem=all_recv.at[0],
        device_id=(lat_id, ord_id ^ 1), device_id_type=MESH,
    )
    filt_arrivals.wait_recv()

    def build_left(part, factors):
        window = filt[pl.ds(part * lat_rows, lat_rows + 2)].reshape(lat_rows + 2, LANES)
        high = window.astype(BF16)
        low = (window - high.astype(F32)).astype(BF16)
        both = jnp.concatenate([high.astype(F32), low.astype(F32)], axis=0).T.astype(BF16)
        row = iota((lat_rows + 2, cols), 0)
        lat = iota((lat_rows + 2, cols), 1) >> log2(width)
        real, imag = [], []
        for step in range(3):
            chosen = (row == lat + 2 - step).astype(F32)
            chosen = jnp.concatenate([chosen, chosen], axis=0).astype(BF16)
            first = 5 * step * basis_count
            wide = jnp.dot(both[first:first + 5 * basis_count], chosen, preferred_element_type=F32)
            sums = [None, None]
            for lon_step in range(5):
                values = wide[lon_step * basis_count:(lon_step + 1) * basis_count]
                for which in range(2):
                    term = values * factors[8 * which + lon_step:8 * which + lon_step + 1]
                    sums[which] = term if sums[which] is None else sums[which] + term
            real.append(sums[0])
            imag.append(sums[1])
        even = (iota((width, cols), 0) & 1) == 0
        for b in range(basis_count):
            total = None
            for step in range(3):
                turn = jnp.where(even, real[step][b:b + 1], imag[step][b:b + 1])
                term = lat_tab[step].reshape(waves, width, cols) * turn[None]
                total = term if total is None else total + term
            left[pl.ds(b * out_rows, out_rows)] = total.reshape(out_rows, cols).astype(BF16)

    def latitude(group, part):
        rows = held[group, pl.ds(part * lat_rows, lat_rows)].reshape(cols, channels)
        return jnp.dot(left[...], rows, preferred_element_type=F32)

    def finish(group):
        if single_lat:
            total = latitude(group, 0)
        else:
            factors_here = tap_factors(group)
            mixed[...] = jnp.zeros(mixed.shape, F32)

            def add(part):
                lat_tables(group, part)
                build_left(part, factors_here)
                mixed[...] += latitude(group, part)

            pl.loop(0, parts)(add)
            total = mixed[...]
        total = total.astype(BF16)
        flat = jnp.concatenate([total[b * out_rows:(b + 1) * out_rows] for b in range(basis_count)], axis=1)
        coefficients = jnp.dot(flat, basis[...].reshape(basis_count * channels, channels), preferred_element_type=F32)
        scaled = (coefficients.reshape(waves, width, channels) * gain[...][:, None, :]).astype(BF16)
        scaled = scaled.reshape(out_rows, channels)
        straight = jnp.dot(scaled, spectral[0], preferred_element_type=F32)
        turned = jnp.dot(scaled, spectral[1], preferred_element_type=F32).reshape(waves, width, channels)
        even = (iota((1, width, channels), 1) & 1) == 0
        turned = jnp.where(even, -pltpu.roll(turned, width - 1, 1), pltpu.roll(turned, 1, 1))
        out_ref[group] = (straight + turned.reshape(out_rows, channels)).astype(BF16)

    if single_lat:
        build_left(0, factors)
    arrivals.wait_recv()
    repeat(groups, finish)
    filt_arrivals.wait_send()
    arrivals.wait_send()


def per_device(field, tap_mask, tap_weight, basis_mix, order_slots, degree_gain, spectral_mix):
    rows_here, n_lon, channels = field.shape
    assert rows_here == 1
    basis_count = basis_mix.shape[0]
    n_lat = degree_gain.shape[0]
    n_orders = order_slots.shape[0]
    n_lat_dev = lax.axis_size("lat")
    n_ord_dev = lax.axis_size("ord")
    slots_here = n_orders // n_ord_dev
    waves = n_lat // n_lat_dev
    per_slab = min(SLAB // 2, slots_here)
    width = 2 * per_slab
    groups = slots_here // per_slab
    lat_rows = min(n_lat, COLUMNS // width)
    block_rows = min(2 * n_orders, 64)
    out_rows = waves * width
    single = groups == 1 and lat_rows == n_lat
    dims = (n_lat_dev, n_ord_dev, n_lat, n_lon, n_orders, channels, basis_count)
    vmem = pl.BlockSpec(memory_space=pltpu.VMEM)
    hbm = pl.BlockSpec(memory_space=pltpu.HBM)
    result = pl.pallas_call(
        functools.partial(kernel, dims),
        out_shape=pltpu.VMEM((groups, out_rows, channels), BF16),
        in_specs=[hbm] * 7,
        out_specs=vmem,
        scratch_shapes=[
            pltpu.VMEM(tap_mask.shape, jnp.int32),
            pltpu.VMEM(tap_weight.shape, F32),
            pltpu.VMEM((1, n_orders), jnp.int32),
            pltpu.SMEM((1, n_orders), jnp.int32),
            pltpu.VMEM((1, n_lon, channels), BF16),
            pltpu.VMEM((basis_count, channels, channels), BF16),
            pltpu.VMEM((waves, channels), F32),
            pltpu.VMEM((2, channels, channels), BF16),
            pltpu.VMEM((block_rows, n_lon), BF16),
            pltpu.VMEM((n_lat + 2, 1, LANES), F32),
            pltpu.VMEM((n_ord_dev * groups, width, channels), BF16),
            pltpu.VMEM((groups, n_lat, width, channels), BF16),
            pltpu.VMEM((3, out_rows, lat_rows * width), F32),
            pltpu.VMEM((basis_count * out_rows, lat_rows * width), BF16),
            pltpu.VMEM((8, LANES) if single else (basis_count * out_rows, channels), F32),
            pltpu.SemaphoreType.DMA((8,)),
            pltpu.SemaphoreType.DMA((1,)),
            pltpu.SemaphoreType.DMA((1,)),
            pltpu.SemaphoreType.DMA((1,)),
            pltpu.SemaphoreType.DMA((1,)),
        ],
        compiler_params=pltpu.CompilerParams(
            collective_id=0, has_side_effects=True, vmem_limit_bytes=63 * 1024 * 1024
        ),
    )(*[pltpu.with_memory_space_constraint(x, pltpu.HBM) for x in (tap_mask, tap_weight, order_slots.reshape(1, n_orders), field, basis_mix, degree_gain, spectral_mix)])
    result = result.reshape(groups, waves, per_slab, 2, channels)
    return jnp.swapaxes(result, 0, 1).reshape(waves, slots_here, 2, channels)


def solution(mesh):
    in_specs = (
        P(("lat", "ord"), None, None),
        P(("lat", "ord"), None, None),
        P(("lat", "ord"), None, None),
        P(),
        P(),
        P(),
        P(),
    )
    out_specs = P("lat", "ord", None, None)
    return jax.shard_map(
        per_device, mesh=mesh, in_specs=in_specs, out_specs=out_specs, check_vma=False
    )
```

```python
import functools
import math

import jax
import jax.numpy as jnp
from jax import lax
from jax.experimental import pallas as pl
from jax.experimental.pallas import tpu as pltpu
from jax.sharding import PartitionSpec as P

MESH = pl.DeviceIdType.MESH
F32 = jnp.float32
BF16 = jnp.bfloat16
SLAB = 8
COLUMNS = 256
LANES = 128


def log2(n):
    assert n & (n - 1) == 0
    return n.bit_length() - 1


def cosine(phase_int, period):
    q = phase_int & (period - 1)
    r = jnp.minimum(q, period - q)
    x = (period // 4 - r).astype(F32) * (2.0 * math.pi / period)
    x2 = x * x
    total = jnp.full_like(x, -1.0 / math.factorial(11))
    for power, sign in ((9, 1.0), (7, -1.0), (5, 1.0), (3, -1.0), (1, 1.0)):
        total = total * x2 + sign / math.factorial(power)
    return total * x


def iota(shape, dim):
    return lax.broadcasted_iota(jnp.int32, shape, dim)


def repeat(count, body):
    if count == 1:
        body(0)
    else:
        pl.loop(0, count)(body)


def kernel(
    dims,
    mask_hbm, weight_hbm, slots_hbm, field_hbm, basis_hbm, gain_hbm, spectral_hbm,
    out_ref,
    mask_ref, weight_ref, slots_ref, slots_smem, field, basis, gain, spectral, table, filt, sent, held, lat_tab, left, mixed,
    local_sem, filt_send, filt_recv, row_send, row_recv, band_send, band_recv,
):
    n_lat_dev, n_ord_dev, n_lat, n_lon, n_orders, channels, basis_count = dims
    lat_id = lax.axis_index("lat")
    ord_id = lax.axis_index("ord")
    row_id = lat_id * n_ord_dev + ord_id
    slots_here = n_orders // n_ord_dev
    waves = n_lat // n_lat_dev
    per_slab = min(SLAB // 2, slots_here)
    width = 2 * per_slab
    groups = slots_here // per_slab
    lat_rows = min(n_lat, COLUMNS // width)
    parts = n_lat // lat_rows
    cols = lat_rows * width
    out_rows = waves * width

    def steps(first, last, body):
        if last - first <= 32:
            for step in range(first, last):
                body(step)
        else:
            pl.loop(first, last)(body)

    def ord_peer(step):
        return (lat_id, ord_id ^ step)

    def lat_peer(step):
        return (lat_id ^ step, ord_id)

    slots_copy = pltpu.make_async_copy(slots_hbm, slots_ref, local_sem.at[0])
    field_copy = pltpu.make_async_copy(field_hbm, field, local_sem.at[1])
    mask_copy = pltpu.make_async_copy(mask_hbm, mask_ref, local_sem.at[2])
    weight_copy = pltpu.make_async_copy(weight_hbm, weight_ref, local_sem.at[3])
    smem_copy = pltpu.make_async_copy(slots_hbm, slots_smem, local_sem.at[4])
    gain_copy = pltpu.make_async_copy(
        gain_hbm.at[pl.ds(pl.multiple_of(lat_id * waves, waves), waves)], gain, local_sem.at[5]
    )
    spectral_copy = pltpu.make_async_copy(spectral_hbm, spectral, local_sem.at[6])
    basis_copy = pltpu.make_async_copy(basis_hbm, basis, local_sem.at[7])
    barrier = pltpu.get_barrier_semaphore()

    def greet(target):
        pl.semaphore_signal(barrier, inc=1, device_id=target, device_id_type=MESH)

    steps(1, n_ord_dev, lambda step: greet(ord_peer(n_ord_dev - step)))
    steps(1, n_lat_dev, lambda step: greet(lat_peer(step)))
    slots_copy.start()
    field_copy.start()
    mask_copy.start()
    weight_copy.start()
    smem_copy.start()
    basis_copy.start()
    gain_copy.start()
    spectral_copy.start()

    filt[0] = jnp.zeros((1, LANES), F32)
    filt[n_lat + 1] = jnp.zeros((1, LANES), F32)

    slots_copy.wait()
    orders = slots_ref[...]
    block_rows = table.shape[0]

    def dft_block(start):
        row = iota((block_rows, 1), 0) + start
        found = iota((block_rows, n_orders), 1) == row >> 1
        order = jnp.sum(jnp.where(found, orders.astype(F32), 0.0), axis=1, keepdims=True).astype(jnp.int32)
        phase = order * iota((block_rows, n_lon), 1) + (n_lon // 4) * (row & 1)
        table[...] = (cosine(phase, n_lon) * (1.0 / math.sqrt(n_lon))).astype(BF16)

    single_dft = block_rows == 2 * n_orders
    if single_dft:
        dft_block(0)
    slabs = block_rows // width

    mask_copy.wait()
    weight_copy.wait()
    taps = mask_ref[0].astype(F32) * weight_ref[0]
    tap_count = taps.shape[1]
    lane = iota((basis_count, LANES), 1)
    spread = jnp.zeros((basis_count, LANES), F32)
    for tap in range(tap_count):
        spread = jnp.where(lane // basis_count == tap, taps[:, tap:tap + 1], spread)
    spread = jnp.where(lane % basis_count == iota((basis_count, LANES), 0), spread, 0.0)
    filt[row_id + 1] = jnp.sum(spread, axis=0, keepdims=True)

    field_copy.wait()

    def transform(block):
        if not single_dft:
            dft_block(block * block_rows)
        rows = jnp.dot(table[...], field[0], preferred_element_type=F32).astype(BF16)
        sent[pl.ds(block * slabs, slabs)] = rows.reshape(slabs, width, channels)

    repeat(2 * n_orders // block_rows, transform)

    pl.semaphore_wait(barrier, n_ord_dev - 1 + n_lat_dev - 1)
    band = lat_id * n_ord_dev

    def filt_copy(source, which, target):
        return pltpu.make_async_remote_copy(
            src_ref=source, dst_ref=source, send_sem=filt_send.at[which], recv_sem=filt_recv.at[which],
            device_id=target, device_id_type=MESH,
        )

    def send(step):
        target = ord_peer(step)
        filt_copy(filt.at[pl.ds(row_id + 1, 1)], 0, target).start()
        pltpu.make_async_remote_copy(
            src_ref=sent.at[pl.ds(target[1] * groups, groups)], dst_ref=held.at[:, row_id],
            send_sem=row_send.at[0], recv_sem=row_recv.at[step], device_id=target, device_id_type=MESH,
        ).start()

    steps(1, n_ord_dev, lambda step: send(n_ord_dev - step))
    held[:, row_id] = sent[pl.ds(ord_id * groups, groups)]

    def row_arrival(step):
        return pltpu.make_async_remote_copy(
            src_ref=held.at[:, row_id], dst_ref=held.at[:, row_id],
            send_sem=row_send.at[0], recv_sem=row_recv.at[step], device_id=ord_peer(1), device_id_type=MESH,
        )

    def band_copy(first, rows, target):
        return pltpu.make_async_remote_copy(
            src_ref=held.at[:, pl.ds(first, rows)], dst_ref=held.at[:, pl.ds(first, rows)],
            send_sem=band_send.at[0], recv_sem=band_recv.at[0], device_id=target, device_id_type=MESH,
        )

    def hand_on(pair):
        if not isinstance(pair, int) or pair > 0:
            row_arrival(2 * pair).wait_recv()
        row_arrival(2 * pair + 1).wait_recv()
        first = band + 2 * ((ord_id >> 1) ^ pair)
        steps(1, n_lat_dev, lambda step: band_copy(first, 2, lat_peer(n_lat_dev - step)).start())

    hand_on(0)
    filt_copy(filt.at[pl.ds(0, n_ord_dev - 1)], 0, ord_peer(1)).wait_recv()
    steps(1, n_lat_dev, lambda step: filt_copy(filt.at[pl.ds(band + 1, n_ord_dev)], 1, lat_peer(n_lat_dev - step)).start())
    steps(1, n_ord_dev // 2, hand_on)

    smem_copy.wait()

    def lane_orders(group):
        place = (iota((1, cols), 1) & (width - 1)) >> 1
        order = jnp.zeros((1, cols), jnp.int32)
        for slot in range(per_slab):
            order = jnp.where(place == slot, slots_smem[0, ord_id * slots_here + group * per_slab + slot], order)
        return order

    def lat_tables(group, part):
        order = lane_orders(group)
        col = iota((1, cols), 1)
        row = iota((out_rows, 1), 0)
        wave = (row >> log2(width)) + lat_id * waves
        same = ((row & (width - 1)) >> 1) == ((col & (width - 1)) >> 1)
        for step in range(3):
            lat = (col >> log2(width)) + part * lat_rows + 1 - step
            phase = wave * (2 * lat + 1) + jnp.where((order & 1) == 0, 0, 3 * n_lat)
            value = cosine(phase, 4 * n_lat) * math.sqrt(2.0 / n_lat)
            lat_tab[step] = jnp.where(same, value, 0.0)

    def tap_factors(group):
        order = lane_orders(group)
        row = iota((16, cols), 0)
        lon_step = (row & 7) - 2
        part_of = iota((16, cols), 1) & 1
        phase = order * lon_step + (n_lon // 4) * (part_of - (row >> 3))
        return cosine(phase, n_lon)

    single_lat = groups == 1 and parts == 1
    if single_lat:
        lat_tables(0, 0)
        factors = tap_factors(0)

    gain_copy.wait()
    spectral_copy.wait()
    basis_copy.wait()
    far_rows = (n_lat_dev - 1) * n_ord_dev
    filt_copy(filt.at[pl.ds(0, far_rows)], 1, lat_peer(1)).wait_recv()

    def build_left(part, factors):
        window = filt[pl.ds(part * lat_rows, lat_rows + 2)].reshape(lat_rows + 2, LANES)
        high = window.astype(BF16)
        low = (window - high.astype(F32)).astype(BF16)
        both = jnp.concatenate([high.astype(F32), low.astype(F32)], axis=0).T.astype(BF16)
        row = iota((lat_rows + 2, cols), 0)
        lat = iota((lat_rows + 2, cols), 1) >> log2(width)
        real, imag = [], []
        for step in range(3):
            chosen = (row == lat + 2 - step).astype(F32)
            chosen = jnp.concatenate([chosen, chosen], axis=0).astype(BF16)
            first = 5 * step * basis_count
            wide = jnp.dot(both[first:first + 5 * basis_count], chosen, preferred_element_type=F32)
            sums = [None, None]
            for lon_step in range(5):
                values = wide[lon_step * basis_count:(lon_step + 1) * basis_count]
                for which in range(2):
                    term = values * factors[8 * which + lon_step:8 * which + lon_step + 1]
                    sums[which] = term if sums[which] is None else sums[which] + term
            real.append(sums[0])
            imag.append(sums[1])
        even = (iota((width, cols), 0) & 1) == 0
        for b in range(basis_count):
            total = None
            for step in range(3):
                turn = jnp.where(even, real[step][b:b + 1], imag[step][b:b + 1])
                term = lat_tab[step].reshape(waves, width, cols) * turn[None]
                total = term if total is None else total + term
            left[pl.ds(b * out_rows, out_rows)] = total.reshape(out_rows, cols).astype(BF16)

    def latitude(group, part):
        rows = held[group, pl.ds(part * lat_rows, lat_rows)].reshape(cols, channels)
        return jnp.dot(left[...], rows, preferred_element_type=F32)

    def finish(group):
        if single_lat:
            total = latitude(group, 0)
        else:
            factors_here = tap_factors(group)
            mixed[...] = jnp.zeros(mixed.shape, F32)

            def add(part):
                lat_tables(group, part)
                build_left(part, factors_here)
                mixed[...] += latitude(group, part)

            pl.loop(0, parts)(add)
            total = mixed[...]
        total = total.astype(BF16)
        flat = jnp.concatenate([total[b * out_rows:(b + 1) * out_rows] for b in range(basis_count)], axis=1)
        coefficients = jnp.dot(flat, basis[...].reshape(basis_count * channels, channels), preferred_element_type=F32)
        scaled = (coefficients.reshape(waves, width, channels) * gain[...][:, None, :]).astype(BF16)
        scaled = scaled.reshape(out_rows, channels)
        straight = jnp.dot(scaled, spectral[0], preferred_element_type=F32)
        turned = jnp.dot(scaled, spectral[1], preferred_element_type=F32).reshape(waves, width, channels)
        even = (iota((1, width, channels), 1) & 1) == 0
        turned = jnp.where(even, -pltpu.roll(turned, width - 1, 1), pltpu.roll(turned, 1, 1))
        out_ref[group] = (straight + turned.reshape(out_rows, channels)).astype(BF16)

    if single_lat:
        build_left(0, factors)
    arrivals = band_copy(0, far_rows, lat_peer(1))
    arrivals.wait_recv()
    repeat(groups, finish)
    filt_copy(filt.at[pl.ds(0, n_ord_dev - 1)], 0, ord_peer(1)).wait_send()
    filt_copy(filt.at[pl.ds(0, far_rows)], 1, lat_peer(1)).wait_send()
    pltpu.make_async_remote_copy(
        src_ref=held.at[:, pl.ds(0, n_ord_dev - 1)], dst_ref=held.at[:, pl.ds(0, n_ord_dev - 1)],
        send_sem=row_send.at[0], recv_sem=row_recv.at[0], device_id=ord_peer(1), device_id_type=MESH,
    ).wait_send()
    arrivals.wait_send()


def per_device(field, tap_mask, tap_weight, basis_mix, order_slots, degree_gain, spectral_mix):
    rows_here, n_lon, channels = field.shape
    assert rows_here == 1
    basis_count = basis_mix.shape[0]
    n_lat = degree_gain.shape[0]
    n_orders = order_slots.shape[0]
    n_lat_dev = lax.axis_size("lat")
    n_ord_dev = lax.axis_size("ord")
    slots_here = n_orders // n_ord_dev
    waves = n_lat // n_lat_dev
    per_slab = min(SLAB // 2, slots_here)
    width = 2 * per_slab
    groups = slots_here // per_slab
    lat_rows = min(n_lat, COLUMNS // width)
    block_rows = min(2 * n_orders, 64)
    out_rows = waves * width
    single = groups == 1 and lat_rows == n_lat
    dims = (n_lat_dev, n_ord_dev, n_lat, n_lon, n_orders, channels, basis_count)
    vmem = pl.BlockSpec(memory_space=pltpu.VMEM)
    hbm = pl.BlockSpec(memory_space=pltpu.HBM)
    result = pl.pallas_call(
        functools.partial(kernel, dims),
        out_shape=pltpu.VMEM((groups, out_rows, channels), BF16),
        in_specs=[hbm] * 7,
        out_specs=vmem,
        scratch_shapes=[
            pltpu.VMEM(tap_mask.shape, jnp.int32),
            pltpu.VMEM(tap_weight.shape, F32),
            pltpu.VMEM((1, n_orders), jnp.int32),
            pltpu.SMEM((1, n_orders), jnp.int32),
            pltpu.VMEM((1, n_lon, channels), BF16),
            pltpu.VMEM((basis_count, channels, channels), BF16),
            pltpu.VMEM((waves, channels), F32),
            pltpu.VMEM((2, channels, channels), BF16),
            pltpu.VMEM((block_rows, n_lon), BF16),
            pltpu.VMEM((n_lat + 2, 1, LANES), F32),
            pltpu.VMEM((n_ord_dev * groups, width, channels), BF16),
            pltpu.VMEM((groups, n_lat, width, channels), BF16),
            pltpu.VMEM((3, out_rows, lat_rows * width), F32),
            pltpu.VMEM((basis_count * out_rows, lat_rows * width), BF16),
            pltpu.VMEM((8, LANES) if single else (basis_count * out_rows, channels), F32),
            pltpu.SemaphoreType.DMA((8,)),
            pltpu.SemaphoreType.DMA((2,)),
            pltpu.SemaphoreType.DMA((2,)),
            pltpu.SemaphoreType.DMA((1,)),
            pltpu.SemaphoreType.DMA((n_ord_dev,)),
            pltpu.SemaphoreType.DMA((1,)),
            pltpu.SemaphoreType.DMA((1,)),
        ],
        compiler_params=pltpu.CompilerParams(
            collective_id=0, has_side_effects=True, vmem_limit_bytes=63 * 1024 * 1024
        ),
    )(*[pltpu.with_memory_space_constraint(x, pltpu.HBM) for x in (tap_mask, tap_weight, order_slots.reshape(1, n_orders), field, basis_mix, degree_gain, spectral_mix)])
    result = result.reshape(groups, waves, per_slab, 2, channels)
    return jnp.swapaxes(result, 0, 1).reshape(waves, slots_here, 2, channels)


def solution(mesh):
    in_specs = (
        P(("lat", "ord"), None, None),
        P(("lat", "ord"), None, None),
        P(("lat", "ord"), None, None),
        P(),
        P(),
        P(),
        P(),
    )
    out_specs = P("lat", "ord", None, None)
    return jax.shard_map(
        per_device, mesh=mesh, in_specs=in_specs, out_specs=out_specs, check_vma=False
    )
```

```python
import functools
import math

import jax
import jax.numpy as jnp
from jax import lax
from jax.experimental import pallas as pl
from jax.experimental.pallas import tpu as pltpu
from jax.sharding import PartitionSpec as P

MESH = pl.DeviceIdType.MESH
F32 = jnp.float32
BF16 = jnp.bfloat16
SLAB = 8
COLUMNS = 256
LANES = 128


def log2(n):
    assert n & (n - 1) == 0
    return n.bit_length() - 1


def cosine(phase_int, period):
    q = phase_int & (period - 1)
    r = jnp.minimum(q, period - q)
    x = (period // 4 - r).astype(F32) * (2.0 * math.pi / period)
    x2 = x * x
    total = jnp.full_like(x, -1.0 / math.factorial(11))
    for power, sign in ((9, 1.0), (7, -1.0), (5, 1.0), (3, -1.0), (1, 1.0)):
        total = total * x2 + sign / math.factorial(power)
    return total * x


def iota(shape, dim):
    return lax.broadcasted_iota(jnp.int32, shape, dim)


def repeat(count, body):
    if count == 1:
        body(0)
    else:
        pl.loop(0, count)(body)


def kernel(
    dims,
    mask_hbm, weight_hbm, slots_hbm, field_hbm, basis_hbm, gain_hbm, spectral_hbm,
    out_ref,
    mask_ref, weight_ref, slots_ref, slots_smem, field, basis, gain, spectral, table, filt, sent, held, lat_tab, left, mixed,
    local_sem, filt_send, filt_recv, all_send, all_recv, ready,
):
    n_lat_dev, n_ord_dev, n_lat, n_lon, n_orders, channels, basis_count = dims
    lat_id = lax.axis_index("lat")
    ord_id = lax.axis_index("ord")
    row_id = lat_id * n_ord_dev + ord_id
    slots_here = n_orders // n_ord_dev
    waves = n_lat // n_lat_dev
    per_slab = min(SLAB // 2, slots_here)
    width = 2 * per_slab
    groups = slots_here // per_slab
    count = n_lat_dev * n_ord_dev
    lat_rows = min(n_lat, COLUMNS // width)
    parts = n_lat // lat_rows
    cols = lat_rows * width
    out_rows = waves * width

    lat_bits = log2(n_lat_dev)
    rank = ((ord_id >> 1) * n_lat_dev + lat_id) * 2 + 1 - (ord_id & 1)
    per_ready = 1 if count <= 64 else 32

    def device(other):
        return ((other >> 1) & (n_lat_dev - 1), ((other >> (1 + lat_bits)) << 1) + 1 - (other & 1))

    slots_copy = pltpu.make_async_copy(slots_hbm, slots_ref, local_sem.at[0])
    field_copy = pltpu.make_async_copy(field_hbm, field, local_sem.at[1])
    mask_copy = pltpu.make_async_copy(mask_hbm, mask_ref, local_sem.at[2])
    weight_copy = pltpu.make_async_copy(weight_hbm, weight_ref, local_sem.at[3])
    smem_copy = pltpu.make_async_copy(slots_hbm, slots_smem, local_sem.at[4])
    gain_copy = pltpu.make_async_copy(
        gain_hbm.at[pl.ds(pl.multiple_of(lat_id * waves, waves), waves)], gain, local_sem.at[5]
    )
    spectral_copy = pltpu.make_async_copy(spectral_hbm, spectral, local_sem.at[6])
    basis_copy = pltpu.make_async_copy(basis_hbm, basis, local_sem.at[7])
    slots_copy.start()
    field_copy.start()
    mask_copy.start()
    weight_copy.start()
    barrier = pltpu.get_barrier_semaphore()

    def greet(other):
        pl.semaphore_signal(barrier, inc=1, device_id=device(other), device_id_type=MESH)

    pl.loop(rank + 1, count)(greet)
    smem_copy.start()
    basis_copy.start()
    gain_copy.start()
    spectral_copy.start()

    filt[0] = jnp.zeros((1, LANES), F32)
    filt[n_lat + 1] = jnp.zeros((1, LANES), F32)

    slots_copy.wait()
    orders = slots_ref[...]
    block_rows = table.shape[0]

    def dft_block(start):
        row = iota((block_rows, 1), 0) + start
        found = iota((block_rows, n_orders), 1) == row >> 1
        order = jnp.sum(jnp.where(found, orders.astype(F32), 0.0), axis=1, keepdims=True).astype(jnp.int32)
        phase = order * iota((block_rows, n_lon), 1) + (n_lon // 4) * (row & 1)
        table[...] = (cosine(phase, n_lon) * (1.0 / math.sqrt(n_lon))).astype(BF16)

    single_dft = block_rows == 2 * n_orders
    if single_dft:
        dft_block(0)
    slabs = block_rows // width

    mask_copy.wait()
    weight_copy.wait()
    taps = mask_ref[0].astype(F32) * weight_ref[0]
    tap_count = taps.shape[1]
    lane = iota((basis_count, LANES), 1)
    spread = jnp.zeros((basis_count, LANES), F32)
    for tap in range(tap_count):
        spread = jnp.where(lane // basis_count == tap, taps[:, tap:tap + 1], spread)
    spread = jnp.where(lane % basis_count == iota((basis_count, LANES), 0), spread, 0.0)
    filt[row_id + 1] = jnp.sum(spread, axis=0, keepdims=True)

    @pl.when(rank > 0)
    def _():
        pl.semaphore_wait(barrier, rank)

    def call(other):
        pl.semaphore_signal(ready.at[rank // per_ready], inc=1, device_id=device(other), device_id_type=MESH)

    pl.loop(0, rank)(call)
    field_copy.wait()

    def transform(block):
        if not single_dft:
            dft_block(block * block_rows)
        rows = jnp.dot(table[...], field[0], preferred_element_type=F32).astype(BF16)
        sent[pl.ds(block * slabs, slabs)] = rows.reshape(slabs, width, channels)

    repeat(2 * n_orders // block_rows, transform)

    def send(other):
        target = device(other)
        pltpu.make_async_remote_copy(
            src_ref=filt.at[row_id + 1], dst_ref=filt.at[row_id + 1],
            send_sem=filt_send.at[0], recv_sem=filt_recv.at[0],
            device_id=target, device_id_type=MESH,
        ).start()
        pltpu.make_async_remote_copy(
            src_ref=sent.at[pl.ds(target[1] * groups, groups)], dst_ref=held.at[:, row_id],
            send_sem=all_send.at[0], recv_sem=all_recv.at[0],
            device_id=target, device_id_type=MESH,
        ).start()

    pl.loop(0, rank)(send)
    held[:, row_id] = sent[pl.ds(ord_id * groups, groups)]

    smem_copy.wait()

    def lane_orders(group):
        place = (iota((1, cols), 1) & (width - 1)) >> 1
        order = jnp.zeros((1, cols), jnp.int32)
        for slot in range(per_slab):
            order = jnp.where(place == slot, slots_smem[0, ord_id * slots_here + group * per_slab + slot], order)
        return order

    def lat_tables(group, part):
        order = lane_orders(group)
        col = iota((1, cols), 1)
        row = iota((out_rows, 1), 0)
        wave = (row >> log2(width)) + lat_id * waves
        same = ((row & (width - 1)) >> 1) == ((col & (width - 1)) >> 1)
        for step in range(3):
            lat = (col >> log2(width)) + part * lat_rows + 1 - step
            phase = wave * (2 * lat + 1) + jnp.where((order & 1) == 0, 0, 3 * n_lat)
            value = cosine(phase, 4 * n_lat) * math.sqrt(2.0 / n_lat)
            lat_tab[step] = jnp.where(same, value, 0.0)

    def tap_factors(group):
        order = lane_orders(group)
        row = iota((16, cols), 0)
        lon_step = (row & 7) - 2
        part_of = iota((16, cols), 1) & 1
        phase = order * lon_step + (n_lon // 4) * (part_of - (row >> 3))
        return cosine(phase, n_lon)

    single_lat = groups == 1 and parts == 1
    if single_lat:
        lat_tables(0, 0)
        factors = tap_factors(0)

    def answer(block):
        first = jnp.maximum(rank + 1, block * per_ready)
        last = (block + 1) * per_ready
        pl.semaphore_wait(ready.at[block], last - first)
        pl.loop(first, last)(send)

    pl.loop((rank + 1) // per_ready, count // per_ready)(answer)
    gain_copy.wait()
    spectral_copy.wait()
    basis_copy.wait()
    filt_arrivals = pltpu.make_async_remote_copy(
        src_ref=filt.at[pl.ds(0, count - 1)], dst_ref=filt.at[pl.ds(0, count - 1)],
        send_sem=filt_send.at[0], recv_sem=filt_recv.at[0],
        device_id=(lat_id, ord_id ^ 1), device_id_type=MESH,
    )
    arrivals = pltpu.make_async_remote_copy(
        src_ref=held.at[:, pl.ds(0, count - 1)], dst_ref=held.at[:, pl.ds(0, count - 1)],
        send_sem=all_send.at[0], recv_sem=all_recv.at[0],
        device_id=(lat_id, ord_id ^ 1), device_id_type=MESH,
    )
    filt_arrivals.wait_recv()

    def build_left(part, factors):
        window = filt[pl.ds(part * lat_rows, lat_rows + 2)].reshape(lat_rows + 2, LANES)
        high = window.astype(BF16)
        low = (window - high.astype(F32)).astype(BF16)
        both = jnp.concatenate([high.astype(F32), low.astype(F32)], axis=0).T.astype(BF16)
        row = iota((lat_rows + 2, cols), 0)
        lat = iota((lat_rows + 2, cols), 1) >> log2(width)
        real, imag = [], []
        for step in range(3):
            chosen = (row == lat + 2 - step).astype(F32)
            chosen = jnp.concatenate([chosen, chosen], axis=0).astype(BF16)
            first = 5 * step * basis_count
            wide = jnp.dot(both[first:first + 5 * basis_count], chosen, preferred_element_type=F32)
            sums = [None, None]
            for lon_step in range(5):
                values = wide[lon_step * basis_count:(lon_step + 1) * basis_count]
                for which in range(2):
                    term = values * factors[8 * which + lon_step:8 * which + lon_step + 1]
                    sums[which] = term if sums[which] is None else sums[which] + term
            real.append(sums[0])
            imag.append(sums[1])
        even = (iota((width, cols), 0) & 1) == 0
        for b in range(basis_count):
            total = None
            for step in range(3):
                turn = jnp.where(even, real[step][b:b + 1], imag[step][b:b + 1])
                term = lat_tab[step].reshape(waves, width, cols) * turn[None]
                total = term if total is None else total + term
            left[pl.ds(b * out_rows, out_rows)] = total.reshape(out_rows, cols).astype(BF16)

    def latitude(group, part):
        rows = held[group, pl.ds(part * lat_rows, lat_rows)].reshape(cols, channels)
        return jnp.dot(left[...], rows, preferred_element_type=F32)

    def finish(group):
        if single_lat:
            total = latitude(group, 0)
        else:
            factors_here = tap_factors(group)
            mixed[...] = jnp.zeros(mixed.shape, F32)

            def add(part):
                lat_tables(group, part)
                build_left(part, factors_here)
                mixed[...] += latitude(group, part)

            pl.loop(0, parts)(add)
            total = mixed[...]
        total = total.astype(BF16)
        flat = jnp.concatenate([total[b * out_rows:(b + 1) * out_rows] for b in range(basis_count)], axis=1)
        coefficients = jnp.dot(flat, basis[...].reshape(basis_count * channels, channels), preferred_element_type=F32)
        scaled = (coefficients.reshape(waves, width, channels) * gain[...][:, None, :]).astype(BF16)
        scaled = scaled.reshape(out_rows, channels)
        straight = jnp.dot(scaled, spectral[0], preferred_element_type=F32)
        turned = jnp.dot(scaled, spectral[1], preferred_element_type=F32).reshape(waves, width, channels)
        even = (iota((1, width, channels), 1) & 1) == 0
        turned = jnp.where(even, -pltpu.roll(turned, width - 1, 1), pltpu.roll(turned, 1, 1))
        out_ref[group] = (straight + turned.reshape(out_rows, channels)).astype(BF16)

    if single_lat:
        build_left(0, factors)
    arrivals.wait_recv()
    repeat(groups, finish)
    filt_arrivals.wait_send()
    arrivals.wait_send()


def per_device(field, tap_mask, tap_weight, basis_mix, order_slots, degree_gain, spectral_mix):
    rows_here, n_lon, channels = field.shape
    assert rows_here == 1
    basis_count = basis_mix.shape[0]
    n_lat = degree_gain.shape[0]
    n_orders = order_slots.shape[0]
    n_lat_dev = lax.axis_size("lat")
    n_ord_dev = lax.axis_size("ord")
    slots_here = n_orders // n_ord_dev
    waves = n_lat // n_lat_dev
    per_slab = min(SLAB // 2, slots_here)
    width = 2 * per_slab
    groups = slots_here // per_slab
    lat_rows = min(n_lat, COLUMNS // width)
    block_rows = min(2 * n_orders, 64)
    out_rows = waves * width
    single = groups == 1 and lat_rows == n_lat
    dims = (n_lat_dev, n_ord_dev, n_lat, n_lon, n_orders, channels, basis_count)
    vmem = pl.BlockSpec(memory_space=pltpu.VMEM)
    hbm = pl.BlockSpec(memory_space=pltpu.HBM)
    result = pl.pallas_call(
        functools.partial(kernel, dims),
        out_shape=pltpu.VMEM((groups, out_rows, channels), BF16),
        in_specs=[hbm] * 7,
        out_specs=vmem,
        scratch_shapes=[
            pltpu.VMEM(tap_mask.shape, jnp.int32),
            pltpu.VMEM(tap_weight.shape, F32),
            pltpu.VMEM((1, n_orders), jnp.int32),
            pltpu.SMEM((1, n_orders), jnp.int32),
            pltpu.VMEM((1, n_lon, channels), BF16),
            pltpu.VMEM((basis_count, channels, channels), BF16),
            pltpu.VMEM((waves, channels), F32),
            pltpu.VMEM((2, channels, channels), BF16),
            pltpu.VMEM((block_rows, n_lon), BF16),
            pltpu.VMEM((n_lat + 2, 1, LANES), F32),
            pltpu.VMEM((n_ord_dev * groups, width, channels), BF16),
            pltpu.VMEM((groups, n_lat, width, channels), BF16),
            pltpu.VMEM((3, out_rows, lat_rows * width), F32),
            pltpu.VMEM((basis_count * out_rows, lat_rows * width), BF16),
            pltpu.VMEM((8, LANES) if single else (basis_count * out_rows, channels), F32),
            pltpu.SemaphoreType.DMA((8,)),
            pltpu.SemaphoreType.DMA((1,)),
            pltpu.SemaphoreType.DMA((1,)),
            pltpu.SemaphoreType.DMA((1,)),
            pltpu.SemaphoreType.DMA((1,)),
            pltpu.SemaphoreType.REGULAR((max(1, n_lat // (1 if n_lat <= 64 else 32)),)),
        ],
        compiler_params=pltpu.CompilerParams(
            collective_id=0, has_side_effects=True, vmem_limit_bytes=63 * 1024 * 1024
        ),
    )(*[pltpu.with_memory_space_constraint(x, pltpu.HBM) for x in (tap_mask, tap_weight, order_slots.reshape(1, n_orders), field, basis_mix, degree_gain, spectral_mix)])
    result = result.reshape(groups, waves, per_slab, 2, channels)
    return jnp.swapaxes(result, 0, 1).reshape(waves, slots_here, 2, channels)


def solution(mesh):
    in_specs = (
        P(("lat", "ord"), None, None),
        P(("lat", "ord"), None, None),
        P(("lat", "ord"), None, None),
        P(),
        P(),
        P(),
        P(),
    )
    out_specs = P("lat", "ord", None, None)
    return jax.shard_map(
        per_device, mesh=mesh, in_specs=in_specs, out_specs=out_specs, check_vma=False
    )
```

```python
import functools
import math

import jax
import jax.numpy as jnp
from jax import lax
from jax.experimental import pallas as pl
from jax.experimental.pallas import tpu as pltpu
from jax.sharding import PartitionSpec as P

MESH = pl.DeviceIdType.MESH
F32 = jnp.float32
BF16 = jnp.bfloat16
SLAB = 8
COLUMNS = 256
LANES = 128


def log2(n):
    assert n & (n - 1) == 0
    return n.bit_length() - 1


def cosine(phase_int, period):
    q = phase_int & (period - 1)
    r = jnp.minimum(q, period - q)
    x = (period // 4 - r).astype(F32) * (2.0 * math.pi / period)
    x2 = x * x
    total = jnp.full_like(x, -1.0 / math.factorial(11))
    for power, sign in ((9, 1.0), (7, -1.0), (5, 1.0), (3, -1.0), (1, 1.0)):
        total = total * x2 + sign / math.factorial(power)
    return total * x


def iota(shape, dim):
    return lax.broadcasted_iota(jnp.int32, shape, dim)


def repeat(count, body):
    if count == 1:
        body(0)
    else:
        pl.loop(0, count)(body)


def kernel(
    dims,
    mask_hbm, weight_hbm, slots_hbm, field_hbm, basis_hbm, gain_hbm, spectral_hbm,
    out_ref,
    mask_ref, weight_ref, slots_ref, slots_smem, field, basis, gain, spectral, table, filt, sent, held, lat_tab, left, mixed,
    local_sem, filt_send, filt_recv, all_send, all_recv, ready,
):
    n_lat_dev, n_ord_dev, n_lat, n_lon, n_orders, channels, basis_count = dims
    lat_id = lax.axis_index("lat")
    ord_id = lax.axis_index("ord")
    row_id = lat_id * n_ord_dev + ord_id
    slots_here = n_orders // n_ord_dev
    waves = n_lat // n_lat_dev
    per_slab = min(SLAB // 2, slots_here)
    width = 2 * per_slab
    groups = slots_here // per_slab
    count = n_lat_dev * n_ord_dev
    lat_rows = min(n_lat, COLUMNS // width)
    parts = n_lat // lat_rows
    cols = lat_rows * width
    out_rows = waves * width

    lat_bits = log2(n_lat_dev)
    rank = ((ord_id >> 1) * n_lat_dev + lat_id) * 2 + 1 - (ord_id & 1)
    per_ready = 1 if count <= 64 else 32

    def device(other):
        return ((other >> 1) & (n_lat_dev - 1), ((other >> (1 + lat_bits)) << 1) + 1 - (other & 1))

    slots_copy = pltpu.make_async_copy(slots_hbm, slots_ref, local_sem.at[0])
    field_copy = pltpu.make_async_copy(field_hbm, field, local_sem.at[1])
    mask_copy = pltpu.make_async_copy(mask_hbm, mask_ref, local_sem.at[2])
    weight_copy = pltpu.make_async_copy(weight_hbm, weight_ref, local_sem.at[3])
    smem_copy = pltpu.make_async_copy(slots_hbm, slots_smem, local_sem.at[4])
    gain_copy = pltpu.make_async_copy(
        gain_hbm.at[pl.ds(pl.multiple_of(lat_id * waves, waves), waves)], gain, local_sem.at[5]
    )
    spectral_copy = pltpu.make_async_copy(spectral_hbm, spectral, local_sem.at[6])
    basis_copy = pltpu.make_async_copy(basis_hbm, basis, local_sem.at[7])
    barrier = pltpu.get_barrier_semaphore()

    def greet(other):
        pl.semaphore_signal(barrier, inc=1, device_id=device(other), device_id_type=MESH)

    pl.loop(rank + 1, count)(greet)
    slots_copy.start()
    field_copy.start()
    mask_copy.start()
    weight_copy.start()
    smem_copy.start()
    basis_copy.start()
    gain_copy.start()
    spectral_copy.start()

    filt[0] = jnp.zeros((1, LANES), F32)
    filt[n_lat + 1] = jnp.zeros((1, LANES), F32)

    slots_copy.wait()
    orders = slots_ref[...]
    block_rows = table.shape[0]

    def dft_block(start):
        row = iota((block_rows, 1), 0) + start
        found = iota((block_rows, n_orders), 1) == row >> 1
        order = jnp.sum(jnp.where(found, orders.astype(F32), 0.0), axis=1, keepdims=True).astype(jnp.int32)
        phase = order * iota((block_rows, n_lon), 1) + (n_lon // 4) * (row & 1)
        table[...] = (cosine(phase, n_lon) * (1.0 / math.sqrt(n_lon))).astype(BF16)

    single_dft = block_rows == 2 * n_orders
    if single_dft:
        dft_block(0)
    slabs = block_rows // width

    mask_copy.wait()
    weight_copy.wait()
    taps = mask_ref[0].astype(F32) * weight_ref[0]
    tap_count = taps.shape[1]
    lane = iota((basis_count, LANES), 1)
    spread = jnp.zeros((basis_count, LANES), F32)
    for tap in range(tap_count):
        spread = jnp.where(lane // basis_count == tap, taps[:, tap:tap + 1], spread)
    spread = jnp.where(lane % basis_count == iota((basis_count, LANES), 0), spread, 0.0)
    filt[row_id + 1] = jnp.sum(spread, axis=0, keepdims=True)

    field_copy.wait()

    def transform(block):
        if not single_dft:
            dft_block(block * block_rows)
        rows = jnp.dot(table[...], field[0], preferred_element_type=F32).astype(BF16)
        sent[pl.ds(block * slabs, slabs)] = rows.reshape(slabs, width, channels)

    repeat(2 * n_orders // block_rows, transform)

    def send(other):
        target = device(other)
        pltpu.make_async_remote_copy(
            src_ref=filt.at[row_id + 1], dst_ref=filt.at[row_id + 1],
            send_sem=filt_send.at[0], recv_sem=filt_recv.at[0],
            device_id=target, device_id_type=MESH,
        ).start()
        pltpu.make_async_remote_copy(
            src_ref=sent.at[pl.ds(target[1] * groups, groups)], dst_ref=held.at[:, row_id],
            send_sem=all_send.at[0], recv_sem=all_recv.at[0],
            device_id=target, device_id_type=MESH,
        ).start()

    def call(other):
        pl.semaphore_signal(ready.at[rank // per_ready], inc=1, device_id=device(other), device_id_type=MESH)

    @pl.when(rank > 0)
    def _():
        pl.semaphore_wait(barrier, rank)

    pl.loop(0, jnp.minimum(rank, 2))(send)
    pl.loop(0, rank)(call)
    pl.loop(jnp.minimum(rank, 2), rank)(send)
    held[:, row_id] = sent[pl.ds(ord_id * groups, groups)]

    smem_copy.wait()

    def lane_orders(group):
        place = (iota((1, cols), 1) & (width - 1)) >> 1
        order = jnp.zeros((1, cols), jnp.int32)
        for slot in range(per_slab):
            order = jnp.where(place == slot, slots_smem[0, ord_id * slots_here + group * per_slab + slot], order)
        return order

    def lat_tables(group, part):
        order = lane_orders(group)
        col = iota((1, cols), 1)
        row = iota((out_rows, 1), 0)
        wave = (row >> log2(width)) + lat_id * waves
        same = ((row & (width - 1)) >> 1) == ((col & (width - 1)) >> 1)
        for step in range(3):
            lat = (col >> log2(width)) + part * lat_rows + 1 - step
            phase = wave * (2 * lat + 1) + jnp.where((order & 1) == 0, 0, 3 * n_lat)
            value = cosine(phase, 4 * n_lat) * math.sqrt(2.0 / n_lat)
            lat_tab[step] = jnp.where(same, value, 0.0)

    def tap_factors(group):
        order = lane_orders(group)
        row = iota((16, cols), 0)
        lon_step = (row & 7) - 2
        part_of = iota((16, cols), 1) & 1
        phase = order * lon_step + (n_lon // 4) * (part_of - (row >> 3))
        return cosine(phase, n_lon)

    single_lat = groups == 1 and parts == 1
    if single_lat:
        lat_tables(0, 0)
        factors = tap_factors(0)

    def answer(block):
        first = jnp.maximum(rank + 1, block * per_ready)
        last = (block + 1) * per_ready
        pl.semaphore_wait(ready.at[block], last - first)
        pl.loop(first, last)(send)

    pl.loop((rank + 1) // per_ready, count // per_ready)(answer)
    gain_copy.wait()
    spectral_copy.wait()
    basis_copy.wait()
    filt_arrivals = pltpu.make_async_remote_copy(
        src_ref=filt.at[pl.ds(0, count - 1)], dst_ref=filt.at[pl.ds(0, count - 1)],
        send_sem=filt_send.at[0], recv_sem=filt_recv.at[0],
        device_id=(lat_id, ord_id ^ 1), device_id_type=MESH,
    )
    arrivals = pltpu.make_async_remote_copy(
        src_ref=held.at[:, pl.ds(0, count - 1)], dst_ref=held.at[:, pl.ds(0, count - 1)],
        send_sem=all_send.at[0], recv_sem=all_recv.at[0],
        device_id=(lat_id, ord_id ^ 1), device_id_type=MESH,
    )
    filt_arrivals.wait_recv()

    def build_left(part, factors):
        window = filt[pl.ds(part * lat_rows, lat_rows + 2)].reshape(lat_rows + 2, LANES)
        high = window.astype(BF16)
        low = (window - high.astype(F32)).astype(BF16)
        both = jnp.concatenate([high.astype(F32), low.astype(F32)], axis=0).T.astype(BF16)
        row = iota((lat_rows + 2, cols), 0)
        lat = iota((lat_rows + 2, cols), 1) >> log2(width)
        real, imag = [], []
        for step in range(3):
            chosen = (row == lat + 2 - step).astype(F32)
            chosen = jnp.concatenate([chosen, chosen], axis=0).astype(BF16)
            first = 5 * step * basis_count
            wide = jnp.dot(both[first:first + 5 * basis_count], chosen, preferred_element_type=F32)
            sums = [None, None]
            for lon_step in range(5):
                values = wide[lon_step * basis_count:(lon_step + 1) * basis_count]
                for which in range(2):
                    term = values * factors[8 * which + lon_step:8 * which + lon_step + 1]
                    sums[which] = term if sums[which] is None else sums[which] + term
            real.append(sums[0])
            imag.append(sums[1])
        even = (iota((width, cols), 0) & 1) == 0
        for b in range(basis_count):
            total = None
            for step in range(3):
                turn = jnp.where(even, real[step][b:b + 1], imag[step][b:b + 1])
                term = lat_tab[step].reshape(waves, width, cols) * turn[None]
                total = term if total is None else total + term
            left[pl.ds(b * out_rows, out_rows)] = total.reshape(out_rows, cols).astype(BF16)

    def latitude(group, part):
        rows = held[group, pl.ds(part * lat_rows, lat_rows)].reshape(cols, channels)
        return jnp.dot(left[...], rows, preferred_element_type=F32)

    def finish(group):
        if single_lat:
            total = latitude(group, 0)
        else:
            factors_here = tap_factors(group)
            mixed[...] = jnp.zeros(mixed.shape, F32)

            def add(part):
                lat_tables(group, part)
                build_left(part, factors_here)
                mixed[...] += latitude(group, part)

            pl.loop(0, parts)(add)
            total = mixed[...]
        total = total.astype(BF16)
        flat = jnp.concatenate([total[b * out_rows:(b + 1) * out_rows] for b in range(basis_count)], axis=1)
        coefficients = jnp.dot(flat, basis[...].reshape(basis_count * channels, channels), preferred_element_type=F32)
        scaled = (coefficients.reshape(waves, width, channels) * gain[...][:, None, :]).astype(BF16)
        scaled = scaled.reshape(out_rows, channels)
        straight = jnp.dot(scaled, spectral[0], preferred_element_type=F32)
        turned = jnp.dot(scaled, spectral[1], preferred_element_type=F32).reshape(waves, width, channels)
        even = (iota((1, width, channels), 1) & 1) == 0
        turned = jnp.where(even, -pltpu.roll(turned, width - 1, 1), pltpu.roll(turned, 1, 1))
        out_ref[group] = (straight + turned.reshape(out_rows, channels)).astype(BF16)

    if single_lat:
        build_left(0, factors)
    arrivals.wait_recv()
    repeat(groups, finish)
    filt_arrivals.wait_send()
    arrivals.wait_send()


def per_device(field, tap_mask, tap_weight, basis_mix, order_slots, degree_gain, spectral_mix):
    rows_here, n_lon, channels = field.shape
    assert rows_here == 1
    basis_count = basis_mix.shape[0]
    n_lat = degree_gain.shape[0]
    n_orders = order_slots.shape[0]
    n_lat_dev = lax.axis_size("lat")
    n_ord_dev = lax.axis_size("ord")
    slots_here = n_orders // n_ord_dev
    waves = n_lat // n_lat_dev
    per_slab = min(SLAB // 2, slots_here)
    width = 2 * per_slab
    groups = slots_here // per_slab
    lat_rows = min(n_lat, COLUMNS // width)
    block_rows = min(2 * n_orders, 64)
    out_rows = waves * width
    single = groups == 1 and lat_rows == n_lat
    dims = (n_lat_dev, n_ord_dev, n_lat, n_lon, n_orders, channels, basis_count)
    vmem = pl.BlockSpec(memory_space=pltpu.VMEM)
    hbm = pl.BlockSpec(memory_space=pltpu.HBM)
    result = pl.pallas_call(
        functools.partial(kernel, dims),
        out_shape=pltpu.VMEM((groups, out_rows, channels), BF16),
        in_specs=[hbm] * 7,
        out_specs=vmem,
        scratch_shapes=[
            pltpu.VMEM(tap_mask.shape, jnp.int32),
            pltpu.VMEM(tap_weight.shape, F32),
            pltpu.VMEM((1, n_orders), jnp.int32),
            pltpu.SMEM((1, n_orders), jnp.int32),
            pltpu.VMEM((1, n_lon, channels), BF16),
            pltpu.VMEM((basis_count, channels, channels), BF16),
            pltpu.VMEM((waves, channels), F32),
            pltpu.VMEM((2, channels, channels), BF16),
            pltpu.VMEM((block_rows, n_lon), BF16),
            pltpu.VMEM((n_lat + 2, 1, LANES), F32),
            pltpu.VMEM((n_ord_dev * groups, width, channels), BF16),
            pltpu.VMEM((groups, n_lat, width, channels), BF16),
            pltpu.VMEM((3, out_rows, lat_rows * width), F32),
            pltpu.VMEM((basis_count * out_rows, lat_rows * width), BF16),
            pltpu.VMEM((8, LANES) if single else (basis_count * out_rows, channels), F32),
            pltpu.SemaphoreType.DMA((8,)),
            pltpu.SemaphoreType.DMA((1,)),
            pltpu.SemaphoreType.DMA((1,)),
            pltpu.SemaphoreType.DMA((1,)),
            pltpu.SemaphoreType.DMA((1,)),
            pltpu.SemaphoreType.REGULAR((max(1, n_lat // (1 if n_lat <= 64 else 32)),)),
        ],
        compiler_params=pltpu.CompilerParams(
            collective_id=0, has_side_effects=True, vmem_limit_bytes=63 * 1024 * 1024
        ),
    )(*[pltpu.with_memory_space_constraint(x, pltpu.HBM) for x in (tap_mask, tap_weight, order_slots.reshape(1, n_orders), field, basis_mix, degree_gain, spectral_mix)])
    result = result.reshape(groups, waves, per_slab, 2, channels)
    return jnp.swapaxes(result, 0, 1).reshape(waves, slots_here, 2, channels)


def solution(mesh):
    in_specs = (
        P(("lat", "ord"), None, None),
        P(("lat", "ord"), None, None),
        P(("lat", "ord"), None, None),
        P(),
        P(),
        P(),
        P(),
    )
    out_specs = P("lat", "ord", None, None)
    return jax.shard_map(
        per_device, mesh=mesh, in_specs=in_specs, out_specs=out_specs, check_vma=False
    )
```

```python
import functools
import math

import jax
import jax.numpy as jnp
from jax import lax
from jax.experimental import pallas as pl
from jax.experimental.pallas import tpu as pltpu
from jax.sharding import PartitionSpec as P

MESH = pl.DeviceIdType.MESH
F32 = jnp.float32
BF16 = jnp.bfloat16
SLAB = 8
COLUMNS = 256
LANES = 128


def log2(n):
    assert n & (n - 1) == 0
    return n.bit_length() - 1


def cosine(phase_int, period):
    q = phase_int & (period - 1)
    r = jnp.minimum(q, period - q)
    x = (period // 4 - r).astype(F32) * (2.0 * math.pi / period)
    x2 = x * x
    total = jnp.full_like(x, -1.0 / math.factorial(11))
    for power, sign in ((9, 1.0), (7, -1.0), (5, 1.0), (3, -1.0), (1, 1.0)):
        total = total * x2 + sign / math.factorial(power)
    return total * x


def iota(shape, dim):
    return lax.broadcasted_iota(jnp.int32, shape, dim)


def repeat(count, body):
    if count == 1:
        body(0)
    else:
        pl.loop(0, count)(body)


def kernel(
    dims,
    mask_hbm, weight_hbm, slots_hbm, field_hbm, basis_hbm, gain_hbm, spectral_hbm,
    out_ref,
    mask_ref, weight_ref, slots_ref, slots_smem, field, basis, gain, spectral, table, filt, sent, held, lat_tab, left, mixed,
    local_sem, filt_send, filt_recv, all_send, all_recv, ready,
):
    n_lat_dev, n_ord_dev, n_lat, n_lon, n_orders, channels, basis_count = dims
    lat_id = lax.axis_index("lat")
    ord_id = lax.axis_index("ord")
    row_id = lat_id * n_ord_dev + ord_id
    slots_here = n_orders // n_ord_dev
    waves = n_lat // n_lat_dev
    per_slab = min(SLAB // 2, slots_here)
    width = 2 * per_slab
    groups = slots_here // per_slab
    count = n_lat_dev * n_ord_dev
    lat_rows = min(n_lat, COLUMNS // width)
    parts = n_lat // lat_rows
    cols = lat_rows * width
    out_rows = waves * width

    lat_bits = log2(n_lat_dev)
    lat_mask = n_lat_dev - 1
    levels = n_ord_dev // 2
    chips = levels * n_lat_dev
    level = ord_id >> 1
    chip = level * n_lat_dev + lat_id
    leader = (ord_id & 1) == 1
    follower = (ord_id & 1) == 0
    half = levels // 2
    top = (levels - 1) * n_lat_dev
    low = level < half
    sibling = (lat_id, ord_id ^ 1)
    per_ready = 1 if chips <= 64 else n_lat_dev

    def device(other, core):
        return (other & lat_mask, ((other >> lat_bits) << 1) + core)

    def on_both(other, body):
        body(device(other, 0))
        body(device(other, 1))

    slots_copy = pltpu.make_async_copy(slots_hbm, slots_ref, local_sem.at[0])
    field_copy = pltpu.make_async_copy(field_hbm, field, local_sem.at[1])
    mask_copy = pltpu.make_async_copy(mask_hbm, mask_ref, local_sem.at[2])
    weight_copy = pltpu.make_async_copy(weight_hbm, weight_ref, local_sem.at[3])
    smem_copy = pltpu.make_async_copy(slots_hbm, slots_smem, local_sem.at[4])
    gain_copy = pltpu.make_async_copy(
        gain_hbm.at[pl.ds(pl.multiple_of(lat_id * waves, waves), waves)], gain, local_sem.at[5]
    )
    spectral_copy = pltpu.make_async_copy(spectral_hbm, spectral, local_sem.at[6])
    basis_copy = pltpu.make_async_copy(basis_hbm, basis, local_sem.at[7])
    barrier = pltpu.get_barrier_semaphore()

    def greet(target):
        pl.semaphore_signal(barrier, inc=1, device_id=target, device_id_type=MESH)

    def signal(semaphore, target):
        pl.semaphore_signal(semaphore, inc=1, device_id=target, device_id_type=MESH)

    greet(sibling)
    pl.loop(chip + 1, chips)(lambda other: greet(device(other, 1)))

    @pl.when(chip == 0)
    def _():
        pl.loop(half * n_lat_dev, chips)(lambda other: greet(device(other, 0)))

    @pl.when(level == levels - 1)
    def _():
        pl.loop(0, half * n_lat_dev)(lambda other: greet(device(other, 0)))

    slots_copy.start()
    field_copy.start()
    mask_copy.start()
    weight_copy.start()
    smem_copy.start()
    basis_copy.start()
    gain_copy.start()
    spectral_copy.start()

    filt[0] = jnp.zeros((1, LANES), F32)
    filt[n_lat + 1] = jnp.zeros((1, LANES), F32)

    slots_copy.wait()
    orders = slots_ref[...]
    block_rows = table.shape[0]

    def dft_block(start):
        row = iota((block_rows, 1), 0) + start
        found = iota((block_rows, n_orders), 1) == row >> 1
        order = jnp.sum(jnp.where(found, orders.astype(F32), 0.0), axis=1, keepdims=True).astype(jnp.int32)
        phase = order * iota((block_rows, n_lon), 1) + (n_lon // 4) * (row & 1)
        table[...] = (cosine(phase, n_lon) * (1.0 / math.sqrt(n_lon))).astype(BF16)

    single_dft = block_rows == 2 * n_orders
    if single_dft:
        dft_block(0)
    slabs = block_rows // width

    mask_copy.wait()
    weight_copy.wait()
    taps = mask_ref[0].astype(F32) * weight_ref[0]
    tap_count = taps.shape[1]
    lane = iota((basis_count, LANES), 1)
    spread = jnp.zeros((basis_count, LANES), F32)
    for tap in range(tap_count):
        spread = jnp.where(lane // basis_count == tap, taps[:, tap:tap + 1], spread)
    spread = jnp.where(lane % basis_count == iota((basis_count, LANES), 0), spread, 0.0)
    filt[row_id + 1] = jnp.sum(spread, axis=0, keepdims=True)

    def send_filters(target):
        pltpu.make_async_remote_copy(
            src_ref=filt.at[row_id + 1], dst_ref=filt.at[row_id + 1],
            send_sem=filt_send.at[0], recv_sem=filt_recv.at[0],
            device_id=target, device_id_type=MESH,
        ).start()

    def send_rows(target):
        pltpu.make_async_remote_copy(
            src_ref=sent.at[pl.ds(target[1] * groups, groups)], dst_ref=held.at[:, row_id],
            send_sem=all_send.at[0], recv_sem=all_recv.at[0],
            device_id=target, device_id_type=MESH,
        ).start()

    def send(target):
        send_filters(target)
        send_rows(target)

    early_sem, known_sem, top_sem = ready.at[chips // per_ready], ready.at[chips // per_ready + 1], ready.at[chips // per_ready + 2]

    @pl.when(jnp.logical_and(follower, jnp.logical_not(low)))
    def _():
        pl.semaphore_wait(barrier, 3)
        signal(early_sem, sibling)

    @pl.when(jnp.logical_and(leader, jnp.logical_not(low)))
    def _():
        pl.semaphore_wait(early_sem, 1)

    @pl.when(jnp.logical_not(low))
    def _():
        on_both(0, send_filters)

    field_copy.wait()

    def transform(block):
        if not single_dft:
            dft_block(block * block_rows)
        rows = jnp.dot(table[...], field[0], preferred_element_type=F32).astype(BF16)
        sent[pl.ds(block * slabs, slabs)] = rows.reshape(slabs, width, channels)

    repeat(2 * n_orders // block_rows, transform)

    @pl.when(jnp.logical_not(low))
    def _():
        on_both(0, send_rows)

    @pl.when(leader)
    def _():
        pl.semaphore_wait(barrier, 2 * chip + 1)
        signal(known_sem, sibling)
        block = chip // per_ready
        first = jnp.where(level == levels - 1, half * n_lat_dev, 0)
        pl.loop(first, chip)(lambda other: on_both(other, lambda target: signal(ready.at[block], target)))

    @pl.when(follower)
    def _():
        pl.semaphore_wait(known_sem, 1)

    pl.loop(jnp.where(low, 0, 1), chip)(lambda other: on_both(other, send))
    send(sibling)
    held[:, row_id] = sent[pl.ds(ord_id * groups, groups)]

    smem_copy.wait()

    def lane_orders(group):
        place = (iota((1, cols), 1) & (width - 1)) >> 1
        order = jnp.zeros((1, cols), jnp.int32)
        for slot in range(per_slab):
            order = jnp.where(place == slot, slots_smem[0, ord_id * slots_here + group * per_slab + slot], order)
        return order

    def lat_tables(group, part):
        order = lane_orders(group)
        col = iota((1, cols), 1)
        row = iota((out_rows, 1), 0)
        wave = (row >> log2(width)) + lat_id * waves
        same = ((row & (width - 1)) >> 1) == ((col & (width - 1)) >> 1)
        for step in range(3):
            lat = (col >> log2(width)) + part * lat_rows + 1 - step
            phase = wave * (2 * lat + 1) + jnp.where((order & 1) == 0, 0, 3 * n_lat)
            value = cosine(phase, 4 * n_lat) * math.sqrt(2.0 / n_lat)
            lat_tab[step] = jnp.where(same, value, 0.0)

    def tap_factors(group):
        order = lane_orders(group)
        row = iota((16, cols), 0)
        lon_step = (row & 7) - 2
        part_of = iota((16, cols), 1) & 1
        phase = order * lon_step + (n_lon // 4) * (part_of - (row >> 3))
        return cosine(phase, n_lon)

    single_lat = groups == 1 and parts == 1
    if single_lat:
        lat_tables(0, 0)
        factors = tap_factors(0)

    def answer(block):
        first = jnp.maximum(chip + 1, block * per_ready)
        last = (block + 1) * per_ready

        @pl.when(jnp.logical_or(jnp.logical_not(low), block < top // per_ready))
        def _():
            pl.semaphore_wait(ready.at[block], last - first)

        pl.loop(first, last)(lambda other: on_both(other, send))

    start = (chip + 1) // per_ready
    half_block, top_block = half * n_lat_dev // per_ready, top // per_ready
    pl.loop(start, half_block)(answer)

    def answer_top():
        pl.loop(jnp.maximum(start, top_block), chips // per_ready)(answer)

    def answer_rest():
        pl.loop(jnp.maximum(start, half_block), top_block)(answer)

    top_first = jnp.logical_and(low, follower)

    @pl.when(jnp.logical_not(top_first))
    def _():
        answer_rest()

    @pl.when(jnp.logical_and(follower, low))
    def _():
        pl.semaphore_wait(barrier, 2 * n_lat_dev + 1)
        signal(top_sem, sibling)

    @pl.when(jnp.logical_and(leader, low))
    def _():
        pl.semaphore_wait(top_sem, 1)

    answer_top()

    @pl.when(top_first)
    def _():
        answer_rest()

    gain_copy.wait()
    spectral_copy.wait()
    basis_copy.wait()
    filt_arrivals = pltpu.make_async_remote_copy(
        src_ref=filt.at[pl.ds(0, count - 1)], dst_ref=filt.at[pl.ds(0, count - 1)],
        send_sem=filt_send.at[0], recv_sem=filt_recv.at[0],
        device_id=(lat_id, ord_id ^ 1), device_id_type=MESH,
    )
    arrivals = pltpu.make_async_remote_copy(
        src_ref=held.at[:, pl.ds(0, count - 1)], dst_ref=held.at[:, pl.ds(0, count - 1)],
        send_sem=all_send.at[0], recv_sem=all_recv.at[0],
        device_id=(lat_id, ord_id ^ 1), device_id_type=MESH,
    )
    filt_arrivals.wait_recv()

    def build_left(part, factors):
        window = filt[pl.ds(part * lat_rows, lat_rows + 2)].reshape(lat_rows + 2, LANES)
        high = window.astype(BF16)
        low = (window - high.astype(F32)).astype(BF16)
        both = jnp.concatenate([high.astype(F32), low.astype(F32)], axis=0).T.astype(BF16)
        row = iota((lat_rows + 2, cols), 0)
        lat = iota((lat_rows + 2, cols), 1) >> log2(width)
        real, imag = [], []
        for step in range(3):
            chosen = (row == lat + 2 - step).astype(F32)
            chosen = jnp.concatenate([chosen, chosen], axis=0).astype(BF16)
            first = 5 * step * basis_count
            wide = jnp.dot(both[first:first + 5 * basis_count], chosen, preferred_element_type=F32)
            sums = [None, None]
            for lon_step in range(5):
                values = wide[lon_step * basis_count:(lon_step + 1) * basis_count]
                for which in range(2):
                    term = values * factors[8 * which + lon_step:8 * which + lon_step + 1]
                    sums[which] = term if sums[which] is None else sums[which] + term
            real.append(sums[0])
            imag.append(sums[1])
        even = (iota((width, cols), 0) & 1) == 0
        for b in range(basis_count):
            total = None
            for step in range(3):
                turn = jnp.where(even, real[step][b:b + 1], imag[step][b:b + 1])
                term = lat_tab[step].reshape(waves, width, cols) * turn[None]
                total = term if total is None else total + term
            left[pl.ds(b * out_rows, out_rows)] = total.reshape(out_rows, cols).astype(BF16)

    def latitude(group, part):
        rows = held[group, pl.ds(part * lat_rows, lat_rows)].reshape(cols, channels)
        return jnp.dot(left[...], rows, preferred_element_type=F32)

    def finish(group):
        if single_lat:
            total = latitude(group, 0)
        else:
            factors_here = tap_factors(group)
            mixed[...] = jnp.zeros(mixed.shape, F32)

            def add(part):
                lat_tables(group, part)
                build_left(part, factors_here)
                mixed[...] += latitude(group, part)

            pl.loop(0, parts)(add)
            total = mixed[...]
        total = total.astype(BF16)
        flat = jnp.concatenate([total[b * out_rows:(b + 1) * out_rows] for b in range(basis_count)], axis=1)
        coefficients = jnp.dot(flat, basis[...].reshape(basis_count * channels, channels), preferred_element_type=F32)
        scaled = (coefficients.reshape(waves, width, channels) * gain[...][:, None, :]).astype(BF16)
        scaled = scaled.reshape(out_rows, channels)
        straight = jnp.dot(scaled, spectral[0], preferred_element_type=F32)
        turned = jnp.dot(scaled, spectral[1], preferred_element_type=F32).reshape(waves, width, channels)
        even = (iota((1, width, channels), 1) & 1) == 0
        turned = jnp.where(even, -pltpu.roll(turned, width - 1, 1), pltpu.roll(turned, 1, 1))
        out_ref[group] = (straight + turned.reshape(out_rows, channels)).astype(BF16)

    if single_lat:
        build_left(0, factors)
    arrivals.wait_recv()
    repeat(groups, finish)
    filt_arrivals.wait_send()
    arrivals.wait_send()


def per_device(field, tap_mask, tap_weight, basis_mix, order_slots, degree_gain, spectral_mix):
    rows_here, n_lon, channels = field.shape
    assert rows_here == 1
    basis_count = basis_mix.shape[0]
    n_lat = degree_gain.shape[0]
    n_orders = order_slots.shape[0]
    n_lat_dev = lax.axis_size("lat")
    n_ord_dev = lax.axis_size("ord")
    slots_here = n_orders // n_ord_dev
    waves = n_lat // n_lat_dev
    per_slab = min(SLAB // 2, slots_here)
    width = 2 * per_slab
    groups = slots_here // per_slab
    lat_rows = min(n_lat, COLUMNS // width)
    block_rows = min(2 * n_orders, 64)
    out_rows = waves * width
    single = groups == 1 and lat_rows == n_lat
    dims = (n_lat_dev, n_ord_dev, n_lat, n_lon, n_orders, channels, basis_count)
    vmem = pl.BlockSpec(memory_space=pltpu.VMEM)
    hbm = pl.BlockSpec(memory_space=pltpu.HBM)
    result = pl.pallas_call(
        functools.partial(kernel, dims),
        out_shape=pltpu.VMEM((groups, out_rows, channels), BF16),
        in_specs=[hbm] * 7,
        out_specs=vmem,
        scratch_shapes=[
            pltpu.VMEM(tap_mask.shape, jnp.int32),
            pltpu.VMEM(tap_weight.shape, F32),
            pltpu.VMEM((1, n_orders), jnp.int32),
            pltpu.SMEM((1, n_orders), jnp.int32),
            pltpu.VMEM((1, n_lon, channels), BF16),
            pltpu.VMEM((basis_count, channels, channels), BF16),
            pltpu.VMEM((waves, channels), F32),
            pltpu.VMEM((2, channels, channels), BF16),
            pltpu.VMEM((block_rows, n_lon), BF16),
            pltpu.VMEM((n_lat + 2, 1, LANES), F32),
            pltpu.VMEM((n_ord_dev * groups, width, channels), BF16),
            pltpu.VMEM((groups, n_lat, width, channels), BF16),
            pltpu.VMEM((3, out_rows, lat_rows * width), F32),
            pltpu.VMEM((basis_count * out_rows, lat_rows * width), BF16),
            pltpu.VMEM((8, LANES) if single else (basis_count * out_rows, channels), F32),
            pltpu.SemaphoreType.DMA((8,)),
            pltpu.SemaphoreType.DMA((1,)),
            pltpu.SemaphoreType.DMA((1,)),
            pltpu.SemaphoreType.DMA((1,)),
            pltpu.SemaphoreType.DMA((1,)),
            pltpu.SemaphoreType.REGULAR((3 + n_lat // 2 // (1 if n_lat <= 128 else n_lat_dev),)),
        ],
        compiler_params=pltpu.CompilerParams(
            collective_id=0, has_side_effects=True, vmem_limit_bytes=63 * 1024 * 1024
        ),
    )(*[pltpu.with_memory_space_constraint(x, pltpu.HBM) for x in (tap_mask, tap_weight, order_slots.reshape(1, n_orders), field, basis_mix, degree_gain, spectral_mix)])
    result = result.reshape(groups, waves, per_slab, 2, channels)
    return jnp.swapaxes(result, 0, 1).reshape(waves, slots_here, 2, channels)


def solution(mesh):
    in_specs = (
        P(("lat", "ord"), None, None),
        P(("lat", "ord"), None, None),
        P(("lat", "ord"), None, None),
        P(),
        P(),
        P(),
        P(),
    )
    out_specs = P("lat", "ord", None, None)
    return jax.shard_map(
        per_device, mesh=mesh, in_specs=in_specs, out_specs=out_specs, check_vma=False
    )
```

```python
import functools
import math

import jax
import jax.numpy as jnp
from jax import lax
from jax.experimental import pallas as pl
from jax.experimental.pallas import tpu as pltpu
from jax.sharding import PartitionSpec as P

MESH = pl.DeviceIdType.MESH
F32 = jnp.float32
BF16 = jnp.bfloat16
SLAB = 8
COLUMNS = 256
LANES = 128


def log2(n):
    assert n & (n - 1) == 0
    return n.bit_length() - 1


def cosine(phase_int, period):
    q = phase_int & (period - 1)
    r = jnp.minimum(q, period - q)
    x = (period // 4 - r).astype(F32) * (2.0 * math.pi / period)
    x2 = x * x
    total = jnp.full_like(x, -1.0 / math.factorial(11))
    for power, sign in ((9, 1.0), (7, -1.0), (5, 1.0), (3, -1.0), (1, 1.0)):
        total = total * x2 + sign / math.factorial(power)
    return total * x


def iota(shape, dim):
    return lax.broadcasted_iota(jnp.int32, shape, dim)


def repeat(count, body):
    if count == 1:
        body(0)
    else:
        pl.loop(0, count)(body)


def kernel(
    dims,
    mask_hbm, weight_hbm, slots_hbm, field_hbm, basis_hbm, gain_hbm, spectral_hbm,
    out_ref,
    mask_ref, weight_ref, slots_ref, slots_smem, field, basis, gain, spectral, table, filt, sent, held, lat_tab, left, mixed,
    local_sem, filt_send, filt_recv, all_send, all_recv, ready,
):
    n_lat_dev, n_ord_dev, n_lat, n_lon, n_orders, channels, basis_count = dims
    lat_id = lax.axis_index("lat")
    ord_id = lax.axis_index("ord")
    row_id = lat_id * n_ord_dev + ord_id
    slots_here = n_orders // n_ord_dev
    waves = n_lat // n_lat_dev
    per_slab = min(SLAB // 2, slots_here)
    width = 2 * per_slab
    groups = slots_here // per_slab
    count = n_lat_dev * n_ord_dev
    lat_rows = min(n_lat, COLUMNS // width)
    parts = n_lat // lat_rows
    cols = lat_rows * width
    out_rows = waves * width

    lat_bits = log2(n_lat_dev)
    lat_mask = n_lat_dev - 1
    levels = n_ord_dev // 2
    chips = levels * n_lat_dev
    level = ord_id >> 1
    chip = level * n_lat_dev + lat_id
    leader = (ord_id & 1) == 1
    follower = (ord_id & 1) == 0
    half = levels // 2
    top = (levels - 1) * n_lat_dev
    low = level < half
    sibling = (lat_id, ord_id ^ 1)
    per_ready = 1 if chips <= 64 else n_lat_dev

    def device(other, core):
        return (other & lat_mask, ((other >> lat_bits) << 1) + core)

    def on_both(other, body):
        body(device(other, 1))
        body(device(other, 0))

    slots_copy = pltpu.make_async_copy(slots_hbm, slots_ref, local_sem.at[0])
    field_copy = pltpu.make_async_copy(field_hbm, field, local_sem.at[1])
    mask_copy = pltpu.make_async_copy(mask_hbm, mask_ref, local_sem.at[2])
    weight_copy = pltpu.make_async_copy(weight_hbm, weight_ref, local_sem.at[3])
    smem_copy = pltpu.make_async_copy(slots_hbm, slots_smem, local_sem.at[4])
    gain_copy = pltpu.make_async_copy(
        gain_hbm.at[pl.ds(pl.multiple_of(lat_id * waves, waves), waves)], gain, local_sem.at[5]
    )
    spectral_copy = pltpu.make_async_copy(spectral_hbm, spectral, local_sem.at[6])
    basis_copy = pltpu.make_async_copy(basis_hbm, basis, local_sem.at[7])
    barrier = pltpu.get_barrier_semaphore()

    def greet(target):
        pl.semaphore_signal(barrier, inc=1, device_id=target, device_id_type=MESH)

    def signal(semaphore, target):
        pl.semaphore_signal(semaphore, inc=1, device_id=target, device_id_type=MESH)

    mask_copy.start()
    weight_copy.start()
    slots_copy.start()
    field_copy.start()
    greet(sibling)
    pl.loop(chip + 1, chips)(lambda other: greet(device(other, 1)))

    @pl.when(chip == 0)
    def _():
        pl.loop(half * n_lat_dev, chips)(lambda other: greet(device(other, 0)))

    @pl.when(level == levels - 1)
    def _():
        pl.loop(0, half * n_lat_dev)(lambda other: greet(device(other, 0)))

    smem_copy.start()
    basis_copy.start()
    gain_copy.start()
    spectral_copy.start()

    filt[pl.ds(0, 1)] = jnp.zeros((1, LANES), F32)
    filt[pl.ds(n_lat + 1, 1)] = jnp.zeros((1, LANES), F32)

    mask_copy.wait()
    weight_copy.wait()
    taps = mask_ref[0].astype(F32) * weight_ref[0]
    tap_count = taps.shape[1]
    lane = iota((basis_count, LANES), 1)
    spread = jnp.zeros((basis_count, LANES), F32)
    for tap in range(tap_count):
        spread = jnp.where(lane // basis_count == tap, taps[:, tap:tap + 1], spread)
    spread = jnp.where(lane % basis_count == iota((basis_count, LANES), 0), spread, 0.0)
    filt[pl.ds(row_id + 1, 1)] = jnp.sum(spread, axis=0, keepdims=True)

    def send_filters(target):
        pltpu.make_async_remote_copy(
            src_ref=filt.at[pl.ds(row_id + 1, 1)], dst_ref=filt.at[pl.ds(row_id + 1, 1)],
            send_sem=filt_send.at[0], recv_sem=filt_recv.at[0],
            device_id=target, device_id_type=MESH,
        ).start()

    def send_rows(target):
        pltpu.make_async_remote_copy(
            src_ref=sent.at[pl.ds(target[1] * groups, groups)], dst_ref=held.at[:, row_id],
            send_sem=all_send.at[0], recv_sem=all_recv.at[0],
            device_id=target, device_id_type=MESH,
        ).start()

    def send(target):
        send_filters(target)
        send_rows(target)

    early_sem, known_sem, top_sem = ready.at[chips // per_ready], ready.at[chips // per_ready + 1], ready.at[chips // per_ready + 2]

    @pl.when(jnp.logical_and(follower, jnp.logical_not(low)))
    def _():
        pl.semaphore_wait(barrier, 3)
        signal(early_sem, sibling)

    @pl.when(jnp.logical_and(leader, jnp.logical_not(low)))
    def _():
        pl.semaphore_wait(early_sem, 1)

    @pl.when(jnp.logical_not(low))
    def _():
        send_filters(device(0, 0))
        send_filters(device(0, 1))

    slots_copy.wait()
    orders = slots_ref[...]
    block_rows = table.shape[0]

    def dft_block(start):
        row = iota((block_rows, 1), 0) + start
        found = iota((block_rows, n_orders), 1) == row >> 1
        order = jnp.sum(jnp.where(found, orders.astype(F32), 0.0), axis=1, keepdims=True).astype(jnp.int32)
        phase = order * iota((block_rows, n_lon), 1) + (n_lon // 4) * (row & 1)
        table[...] = (cosine(phase, n_lon) * (1.0 / math.sqrt(n_lon))).astype(BF16)

    single_dft = block_rows == 2 * n_orders
    if single_dft:
        dft_block(0)
    slabs = block_rows // width

    field_copy.wait()

    def transform(block):
        if not single_dft:
            dft_block(block * block_rows)
        rows = jnp.dot(table[...], field[0], preferred_element_type=F32).astype(BF16)
        sent[pl.ds(block * slabs, slabs)] = rows.reshape(slabs, width, channels)

    repeat(2 * n_orders // block_rows, transform)

    @pl.when(jnp.logical_not(low))
    def _():
        send_rows(device(0, 0))
        send_rows(device(0, 1))

    @pl.when(leader)
    def _():
        pl.semaphore_wait(barrier, 2 * chip + 1)
        signal(known_sem, sibling)
        block = chip // per_ready
        first = jnp.where(level == levels - 1, half * n_lat_dev, 0)
        pl.loop(first, chip)(lambda other: on_both(other, lambda target: signal(ready.at[block], target)))

    @pl.when(follower)
    def _():
        pl.semaphore_wait(known_sem, 1)

    pl.loop(jnp.where(low, 0, 1), chip)(lambda other: on_both(other, send))
    send(sibling)
    held[:, row_id] = sent[pl.ds(ord_id * groups, groups)]

    smem_copy.wait()

    def lane_orders(group):
        place = (iota((1, cols), 1) & (width - 1)) >> 1
        order = jnp.zeros((1, cols), jnp.int32)
        for slot in range(per_slab):
            order = jnp.where(place == slot, slots_smem[0, ord_id * slots_here + group * per_slab + slot], order)
        return order

    def lat_tables(group, part):
        order = lane_orders(group)
        col = iota((1, cols), 1)
        row = iota((out_rows, 1), 0)
        wave = (row >> log2(width)) + lat_id * waves
        same = ((row & (width - 1)) >> 1) == ((col & (width - 1)) >> 1)
        for step in range(3):
            lat = (col >> log2(width)) + part * lat_rows + 1 - step
            phase = wave * (2 * lat + 1) + jnp.where((order & 1) == 0, 0, 3 * n_lat)
            value = cosine(phase, 4 * n_lat) * math.sqrt(2.0 / n_lat)
            lat_tab[step] = jnp.where(same, value, 0.0)

    def tap_factors(group):
        order = lane_orders(group)
        row = iota((16, cols), 0)
        lon_step = (row & 7) - 2
        part_of = iota((16, cols), 1) & 1
        phase = order * lon_step + (n_lon // 4) * (part_of - (row >> 3))
        return cosine(phase, n_lon)

    single_lat = groups == 1 and parts == 1
    if single_lat:
        lat_tables(0, 0)
        factors = tap_factors(0)

    def answer(block):
        first = jnp.maximum(chip + 1, block * per_ready)
        last = (block + 1) * per_ready

        @pl.when(jnp.logical_or(jnp.logical_not(low), block < top // per_ready))
        def _():
            pl.semaphore_wait(ready.at[block], last - first)

        pl.loop(first, last)(lambda other: on_both(other, send))

    start = (chip + 1) // per_ready
    half_block, top_block = half * n_lat_dev // per_ready, top // per_ready
    pl.loop(start, half_block)(answer)

    def answer_top():
        pl.loop(jnp.maximum(start, top_block), chips // per_ready)(answer)

    def answer_rest():
        pl.loop(jnp.maximum(start, half_block), top_block)(answer)

    top_first = jnp.logical_and(low, follower)

    @pl.when(jnp.logical_not(top_first))
    def _():
        answer_rest()

    @pl.when(jnp.logical_and(follower, low))
    def _():
        pl.semaphore_wait(barrier, 2 * n_lat_dev + 1)
        signal(top_sem, sibling)

    @pl.when(jnp.logical_and(leader, low))
    def _():
        pl.semaphore_wait(top_sem, 1)

    answer_top()

    @pl.when(top_first)
    def _():
        answer_rest()

    gain_copy.wait()
    spectral_copy.wait()
    basis_copy.wait()
    filt_arrivals = pltpu.make_async_remote_copy(
        src_ref=filt.at[pl.ds(0, count - 1)], dst_ref=filt.at[pl.ds(0, count - 1)],
        send_sem=filt_send.at[0], recv_sem=filt_recv.at[0],
        device_id=(lat_id, ord_id ^ 1), device_id_type=MESH,
    )
    arrivals = pltpu.make_async_remote_copy(
        src_ref=held.at[:, pl.ds(0, count - 1)], dst_ref=held.at[:, pl.ds(0, count - 1)],
        send_sem=all_send.at[0], recv_sem=all_recv.at[0],
        device_id=(lat_id, ord_id ^ 1), device_id_type=MESH,
    )
    filt_arrivals.wait_recv()

    def build_left(part, factors):
        window = filt[pl.ds(part * lat_rows, lat_rows + 2)]
        high = window.astype(BF16)
        low = (window - high.astype(F32)).astype(BF16)
        both = jnp.concatenate([high.astype(F32), low.astype(F32)], axis=0).T.astype(BF16)
        row = iota((lat_rows + 2, cols), 0)
        lat = iota((lat_rows + 2, cols), 1) >> log2(width)
        real, imag = [], []
        for step in range(3):
            chosen = (row == lat + 2 - step).astype(F32)
            chosen = jnp.concatenate([chosen, chosen], axis=0).astype(BF16)
            first = 5 * step * basis_count
            wide = jnp.dot(both[first:first + 5 * basis_count], chosen, preferred_element_type=F32)
            sums = [None, None]
            for lon_step in range(5):
                values = wide[lon_step * basis_count:(lon_step + 1) * basis_count]
                for which in range(2):
                    term = values * factors[8 * which + lon_step:8 * which + lon_step + 1]
                    sums[which] = term if sums[which] is None else sums[which] + term
            real.append(sums[0])
            imag.append(sums[1])
        even = (iota((width, cols), 0) & 1) == 0
        for b in range(basis_count):
            total = None
            for step in range(3):
                turn = jnp.where(even, real[step][b:b + 1], imag[step][b:b + 1])
                term = lat_tab[step].reshape(waves, width, cols) * turn[None]
                total = term if total is None else total + term
            left[pl.ds(b * out_rows, out_rows)] = total.reshape(out_rows, cols).astype(BF16)

    def latitude(group, part):
        rows = held[group, pl.ds(part * lat_rows, lat_rows)].reshape(cols, channels)
        return jnp.dot(left[...], rows, preferred_element_type=F32)

    def finish(group):
        if single_lat:
            total = latitude(group, 0)
        else:
            factors_here = tap_factors(group)
            mixed[...] = jnp.zeros(mixed.shape, F32)

            def add(part):
                lat_tables(group, part)
                build_left(part, factors_here)
                mixed[...] += latitude(group, part)

            pl.loop(0, parts)(add)
            total = mixed[...]
        total = total.astype(BF16)
        flat = jnp.concatenate([total[b * out_rows:(b + 1) * out_rows] for b in range(basis_count)], axis=1)
        coefficients = jnp.dot(flat, basis[...].reshape(basis_count * channels, channels), preferred_element_type=F32)
        scaled = (coefficients.reshape(waves, width, channels) * gain[...][:, None, :]).astype(BF16)
        scaled = scaled.reshape(out_rows, channels)
        straight = jnp.dot(scaled, spectral[0], preferred_element_type=F32)
        turned = jnp.dot(scaled, spectral[1], preferred_element_type=F32).reshape(waves, width, channels)
        even = (iota((1, width, channels), 1) & 1) == 0
        turned = jnp.where(even, -pltpu.roll(turned, width - 1, 1), pltpu.roll(turned, 1, 1))
        out_ref[group] = (straight + turned.reshape(out_rows, channels)).astype(BF16)

    if single_lat:
        build_left(0, factors)
    arrivals.wait_recv()
    repeat(groups, finish)
    filt_arrivals.wait_send()
    arrivals.wait_send()


def per_device(field, tap_mask, tap_weight, basis_mix, order_slots, degree_gain, spectral_mix):
    rows_here, n_lon, channels = field.shape
    assert rows_here == 1
    basis_count = basis_mix.shape[0]
    n_lat = degree_gain.shape[0]
    n_orders = order_slots.shape[0]
    n_lat_dev = lax.axis_size("lat")
    n_ord_dev = lax.axis_size("ord")
    slots_here = n_orders // n_ord_dev
    waves = n_lat // n_lat_dev
    per_slab = min(SLAB // 2, slots_here)
    width = 2 * per_slab
    groups = slots_here // per_slab
    lat_rows = min(n_lat, COLUMNS // width)
    block_rows = min(2 * n_orders, 64)
    out_rows = waves * width
    single = groups == 1 and lat_rows == n_lat
    dims = (n_lat_dev, n_ord_dev, n_lat, n_lon, n_orders, channels, basis_count)
    vmem = pl.BlockSpec(memory_space=pltpu.VMEM)
    hbm = pl.BlockSpec(memory_space=pltpu.HBM)
    result = pl.pallas_call(
        functools.partial(kernel, dims),
        out_shape=pltpu.VMEM((groups, out_rows, channels), BF16),
        in_specs=[hbm] * 7,
        out_specs=vmem,
        scratch_shapes=[
            pltpu.VMEM(tap_mask.shape, jnp.int32),
            pltpu.VMEM(tap_weight.shape, F32),
            pltpu.VMEM((1, n_orders), jnp.int32),
            pltpu.SMEM((1, n_orders), jnp.int32),
            pltpu.VMEM((1, n_lon, channels), BF16),
            pltpu.VMEM((basis_count, channels, channels), BF16),
            pltpu.VMEM((waves, channels), F32),
            pltpu.VMEM((2, channels, channels), BF16),
            pltpu.VMEM((block_rows, n_lon), BF16),
            pltpu.VMEM((n_lat + 2, LANES), F32),
            pltpu.VMEM((n_ord_dev * groups, width, channels), BF16),
            pltpu.VMEM((groups, n_lat, width, channels), BF16),
            pltpu.VMEM((3, out_rows, lat_rows * width), F32),
            pltpu.VMEM((basis_count * out_rows, lat_rows * width), BF16),
            pltpu.VMEM((8, LANES) if single else (basis_count * out_rows, channels), F32),
            pltpu.SemaphoreType.DMA((8,)),
            pltpu.SemaphoreType.DMA((1,)),
            pltpu.SemaphoreType.DMA((1,)),
            pltpu.SemaphoreType.DMA((1,)),
            pltpu.SemaphoreType.DMA((1,)),
            pltpu.SemaphoreType.REGULAR((3 + n_lat // 2 // (1 if n_lat <= 128 else n_lat_dev),)),
        ],
        compiler_params=pltpu.CompilerParams(
            collective_id=0, has_side_effects=True, vmem_limit_bytes=63 * 1024 * 1024
        ),
    )(*[pltpu.with_memory_space_constraint(x, pltpu.HBM) for x in (tap_mask, tap_weight, order_slots.reshape(1, n_orders), field, basis_mix, degree_gain, spectral_mix)])
    result = result.reshape(groups, waves, per_slab, 2, channels)
    return jnp.swapaxes(result, 0, 1).reshape(waves, slots_here, 2, channels)


def solution(mesh):
    in_specs = (
        P(("lat", "ord"), None, None),
        P(("lat", "ord"), None, None),
        P(("lat", "ord"), None, None),
        P(),
        P(),
        P(),
        P(),
    )
    out_specs = P("lat", "ord", None, None)
    return jax.shard_map(
        per_device, mesh=mesh, in_specs=in_specs, out_specs=out_specs, check_vma=False
    )
```

```python
import functools
import math

import jax
import jax.numpy as jnp
from jax import lax
from jax.experimental import pallas as pl
from jax.experimental.pallas import tpu as pltpu
from jax.sharding import PartitionSpec as P

MESH = pl.DeviceIdType.MESH
F32 = jnp.float32
BF16 = jnp.bfloat16
SLAB = 8
COLUMNS = 256
LANES = 128


def log2(n):
    assert n & (n - 1) == 0
    return n.bit_length() - 1


def cosine(phase_int, period):
    q = phase_int & (period - 1)
    r = jnp.minimum(q, period - q)
    x = (period // 4 - r).astype(F32) * (2.0 * math.pi / period)
    x2 = x * x
    total = jnp.full_like(x, -1.0 / math.factorial(11))
    for power, sign in ((9, 1.0), (7, -1.0), (5, 1.0), (3, -1.0), (1, 1.0)):
        total = total * x2 + sign / math.factorial(power)
    return total * x


def iota(shape, dim):
    return lax.broadcasted_iota(jnp.int32, shape, dim)


def repeat(count, body):
    if count == 1:
        body(0)
    else:
        pl.loop(0, count)(body)


def kernel(
    dims,
    mask_hbm, weight_hbm, slots_hbm, field_hbm, basis_hbm, gain_hbm, spectral_hbm,
    out_ref,
    mask_ref, weight_ref, slots_ref, slots_smem, field, basis, gain, spectral, table, filt, sent, held, lat_tab, select, left, mixed,
    local_sem, filt_send, filt_recv, all_send, all_recv, ready,
):
    n_lat_dev, n_ord_dev, n_lat, n_lon, n_orders, channels, basis_count = dims
    lat_id = lax.axis_index("lat")
    ord_id = lax.axis_index("ord")
    row_id = lat_id * n_ord_dev + ord_id
    slots_here = n_orders // n_ord_dev
    waves = n_lat // n_lat_dev
    per_slab = min(SLAB // 2, slots_here)
    width = 2 * per_slab
    groups = slots_here // per_slab
    count = n_lat_dev * n_ord_dev
    lat_rows = min(n_lat, COLUMNS // width)
    parts = n_lat // lat_rows
    cols = lat_rows * width
    out_rows = waves * width

    lat_bits = log2(n_lat_dev)
    lat_mask = n_lat_dev - 1
    levels = n_ord_dev // 2
    chips = levels * n_lat_dev
    level = ord_id >> 1
    chip = level * n_lat_dev + lat_id
    leader = (ord_id & 1) == 1
    follower = (ord_id & 1) == 0
    half = levels // 2
    top = (levels - 1) * n_lat_dev
    low = level < half
    sibling = (lat_id, ord_id ^ 1)
    per_ready = 1 if chips <= 64 else n_lat_dev

    def device(other, core):
        return (other & lat_mask, ((other >> lat_bits) << 1) + core)

    def on_both(other, body):
        body(device(other, 1))
        body(device(other, 0))

    slots_copy = pltpu.make_async_copy(slots_hbm, slots_ref, local_sem.at[0])
    field_copy = pltpu.make_async_copy(field_hbm, field, local_sem.at[1])
    mask_copy = pltpu.make_async_copy(mask_hbm, mask_ref, local_sem.at[2])
    weight_copy = pltpu.make_async_copy(weight_hbm, weight_ref, local_sem.at[3])
    smem_copy = pltpu.make_async_copy(slots_hbm, slots_smem, local_sem.at[4])
    gain_copy = pltpu.make_async_copy(
        gain_hbm.at[pl.ds(pl.multiple_of(lat_id * waves, waves), waves)], gain, local_sem.at[5]
    )
    spectral_copy = pltpu.make_async_copy(spectral_hbm, spectral, local_sem.at[6])
    basis_copy = pltpu.make_async_copy(basis_hbm, basis, local_sem.at[7])
    barrier = pltpu.get_barrier_semaphore()

    def greet(target):
        pl.semaphore_signal(barrier, inc=1, device_id=target, device_id_type=MESH)

    def signal(semaphore, target):
        pl.semaphore_signal(semaphore, inc=1, device_id=target, device_id_type=MESH)

    mask_copy.start()
    weight_copy.start()
    slots_copy.start()
    field_copy.start()
    greet(sibling)
    pl.loop(chip + 1, chips)(lambda other: greet(device(other, 1)))

    @pl.when(chip == 0)
    def _():
        pl.loop(half * n_lat_dev, chips)(lambda other: greet(device(other, 0)))

    @pl.when(level == levels - 1)
    def _():
        pl.loop(0, half * n_lat_dev)(lambda other: greet(device(other, 0)))

    smem_copy.start()
    basis_copy.start()
    gain_copy.start()
    spectral_copy.start()

    filt[pl.ds(0, 1)] = jnp.zeros((1, LANES), F32)
    filt[pl.ds(n_lat + 1, 1)] = jnp.zeros((1, LANES), F32)

    mask_copy.wait()
    weight_copy.wait()
    taps = mask_ref[0].astype(F32) * weight_ref[0]
    tap_count = taps.shape[1]
    lane = iota((basis_count, LANES), 1)
    spread = jnp.zeros((basis_count, LANES), F32)
    for tap in range(tap_count):
        spread = jnp.where(lane // basis_count == tap, taps[:, tap:tap + 1], spread)
    spread = jnp.where(lane % basis_count == iota((basis_count, LANES), 0), spread, 0.0)
    filt[pl.ds(row_id + 1, 1)] = jnp.sum(spread, axis=0, keepdims=True)

    def send_filters(target):
        pltpu.make_async_remote_copy(
            src_ref=filt.at[pl.ds(row_id + 1, 1)], dst_ref=filt.at[pl.ds(row_id + 1, 1)],
            send_sem=filt_send.at[0], recv_sem=filt_recv.at[0],
            device_id=target, device_id_type=MESH,
        ).start()

    def send_rows(target):
        pltpu.make_async_remote_copy(
            src_ref=sent.at[pl.ds(target[1] * groups, groups)], dst_ref=held.at[:, row_id],
            send_sem=all_send.at[0], recv_sem=all_recv.at[0],
            device_id=target, device_id_type=MESH,
        ).start()

    def send(target):
        send_filters(target)
        send_rows(target)

    early_sem, known_sem, top_sem = ready.at[chips // per_ready], ready.at[chips // per_ready + 1], ready.at[chips // per_ready + 2]

    @pl.when(jnp.logical_and(follower, jnp.logical_not(low)))
    def _():
        pl.semaphore_wait(barrier, 3)
        signal(early_sem, sibling)

    @pl.when(jnp.logical_and(leader, jnp.logical_not(low)))
    def _():
        pl.semaphore_wait(early_sem, 1)

    @pl.when(jnp.logical_not(low))
    def _():
        send_filters(device(0, 0))
        send_filters(device(0, 1))

    slots_copy.wait()
    orders = slots_ref[...]
    block_rows = table.shape[0]

    def dft_block(start):
        row = iota((block_rows, 1), 0) + start
        found = iota((block_rows, n_orders), 1) == row >> 1
        order = jnp.sum(jnp.where(found, orders.astype(F32), 0.0), axis=1, keepdims=True).astype(jnp.int32)
        phase = order * iota((block_rows, n_lon), 1) + (n_lon // 4) * (row & 1)
        table[...] = (cosine(phase, n_lon) * (1.0 / math.sqrt(n_lon))).astype(BF16)

    single_dft = block_rows == 2 * n_orders
    if single_dft:
        dft_block(0)
    slabs = block_rows // width

    field_copy.wait()

    def transform(block):
        if not single_dft:
            dft_block(block * block_rows)
        rows = jnp.dot(table[...], field[0], preferred_element_type=F32).astype(BF16)
        sent[pl.ds(block * slabs, slabs)] = rows.reshape(slabs, width, channels)

    def send_first():
        @pl.when(jnp.logical_not(low))
        def _():
            send_rows(device(0, 0))
            send_rows(device(0, 1))

    def transform_rows(first, last):
        rows = jnp.dot(table[first:last], field[0], preferred_element_type=F32).astype(BF16)
        sent[first // width:last // width] = rows.reshape((last - first) // width, width, channels)

    first_rows = 4 * slots_here
    if single_dft and first_rows % 16 == 0 and first_rows < block_rows:
        transform_rows(0, first_rows)
        send_first()
        transform_rows(first_rows, block_rows)
    else:
        repeat(2 * n_orders // block_rows, transform)
        send_first()

    @pl.when(leader)
    def _():
        pl.semaphore_wait(barrier, 2 * chip + 1)
        signal(known_sem, sibling)
        block = chip // per_ready
        first = jnp.where(level == levels - 1, half * n_lat_dev, 0)
        pl.loop(first, chip)(lambda other: on_both(other, lambda target: signal(ready.at[block], target)))

    @pl.when(follower)
    def _():
        pl.semaphore_wait(known_sem, 1)

    pl.loop(jnp.where(low, 0, 1), chip)(lambda other: on_both(other, send))
    send(sibling)
    held[:, row_id] = sent[pl.ds(ord_id * groups, groups)]

    smem_copy.wait()

    def lane_orders(group):
        place = (iota((1, cols), 1) & (width - 1)) >> 1
        order = jnp.zeros((1, cols), jnp.int32)
        for slot in range(per_slab):
            order = jnp.where(place == slot, slots_smem[0, ord_id * slots_here + group * per_slab + slot], order)
        return order

    def lat_tables(group, part):
        order = lane_orders(group)
        col = iota((1, cols), 1)
        row = iota((out_rows, 1), 0)
        wave = (row >> log2(width)) + lat_id * waves
        same = ((row & (width - 1)) >> 1) == ((col & (width - 1)) >> 1)
        for step in range(3):
            lat = (col >> log2(width)) + part * lat_rows + 1 - step
            phase = wave * (2 * lat + 1) + jnp.where((order & 1) == 0, 0, 3 * n_lat)
            value = cosine(phase, 4 * n_lat) * math.sqrt(2.0 / n_lat)
            lat_tab[step] = jnp.where(same, value, 0.0)

    def tap_factors(group):
        order = lane_orders(group)
        row = iota((16, cols), 0)
        lon_step = (row & 7) - 2
        part_of = iota((16, cols), 1) & 1
        phase = order * lon_step + (n_lon // 4) * (part_of - (row >> 3))
        return cosine(phase, n_lon)

    window_row = iota((lat_rows + 2, cols), 0)
    window_lat = iota((lat_rows + 2, cols), 1) >> log2(width)
    for step in range(3):
        chosen = (window_row == window_lat + 2 - step).astype(F32)
        select[step] = jnp.concatenate([chosen, chosen], axis=0).astype(BF16)

    single_lat = groups == 1 and parts == 1
    if single_lat:
        lat_tables(0, 0)
        factors = tap_factors(0)

    def answer(block):
        first = jnp.maximum(chip + 1, block * per_ready)
        last = (block + 1) * per_ready

        @pl.when(jnp.logical_or(jnp.logical_not(low), block < top // per_ready))
        def _():
            pl.semaphore_wait(ready.at[block], last - first)

        pl.loop(first, last)(lambda other: on_both(other, send))

    start = (chip + 1) // per_ready
    half_block, top_block = half * n_lat_dev // per_ready, top // per_ready
    pl.loop(start, half_block)(answer)

    def answer_top():
        pl.loop(jnp.maximum(start, top_block), chips // per_ready)(answer)

    def answer_rest():
        pl.loop(jnp.maximum(start, half_block), top_block)(answer)

    top_first = jnp.logical_and(low, follower)

    @pl.when(jnp.logical_not(top_first))
    def _():
        answer_rest()

    @pl.when(jnp.logical_and(follower, low))
    def _():
        pl.semaphore_wait(barrier, 2 * n_lat_dev + 1)
        signal(top_sem, sibling)

    @pl.when(jnp.logical_and(leader, low))
    def _():
        pl.semaphore_wait(top_sem, 1)

    answer_top()

    @pl.when(top_first)
    def _():
        answer_rest()

    gain_copy.wait()
    spectral_copy.wait()
    basis_copy.wait()
    filt_arrivals = pltpu.make_async_remote_copy(
        src_ref=filt.at[pl.ds(0, count - 1)], dst_ref=filt.at[pl.ds(0, count - 1)],
        send_sem=filt_send.at[0], recv_sem=filt_recv.at[0],
        device_id=(lat_id, ord_id ^ 1), device_id_type=MESH,
    )
    arrivals = pltpu.make_async_remote_copy(
        src_ref=held.at[:, pl.ds(0, count - 1)], dst_ref=held.at[:, pl.ds(0, count - 1)],
        send_sem=all_send.at[0], recv_sem=all_recv.at[0],
        device_id=(lat_id, ord_id ^ 1), device_id_type=MESH,
    )
    filt_arrivals.wait_recv()

    def build_left(part, factors):
        window = filt[pl.ds(part * lat_rows, lat_rows + 2)]
        high = window.astype(BF16)
        low = (window - high.astype(F32)).astype(BF16)
        both = jnp.concatenate([high.astype(F32), low.astype(F32)], axis=0).T.astype(BF16)
        real, imag = [], []
        for step in range(3):
            first = 5 * step * basis_count
            wide = jnp.dot(both[first:first + 5 * basis_count], select[step], preferred_element_type=F32)
            sums = [None, None]
            for lon_step in range(5):
                values = wide[lon_step * basis_count:(lon_step + 1) * basis_count]
                for which in range(2):
                    term = values * factors[8 * which + lon_step:8 * which + lon_step + 1]
                    sums[which] = term if sums[which] is None else sums[which] + term
            real.append(sums[0])
            imag.append(sums[1])
        even = (iota((width, cols), 0) & 1) == 0
        for b in range(basis_count):
            total = None
            for step in range(3):
                turn = jnp.where(even, real[step][b:b + 1], imag[step][b:b + 1])
                term = lat_tab[step].reshape(waves, width, cols) * turn[None]
                total = term if total is None else total + term
            left[pl.ds(b * out_rows, out_rows)] = total.reshape(out_rows, cols).astype(BF16)

    def latitude(group, part):
        rows = held[group, pl.ds(part * lat_rows, lat_rows)].reshape(cols, channels)
        return jnp.dot(left[...], rows, preferred_element_type=F32)

    def finish(group):
        if single_lat:
            total = latitude(group, 0)
        else:
            factors_here = tap_factors(group)
            mixed[...] = jnp.zeros(mixed.shape, F32)

            def add(part):
                lat_tables(group, part)
                build_left(part, factors_here)
                mixed[...] += latitude(group, part)

            pl.loop(0, parts)(add)
            total = mixed[...]
        total = total.astype(BF16)
        flat = jnp.concatenate([total[b * out_rows:(b + 1) * out_rows] for b in range(basis_count)], axis=1)
        weights = basis[...].reshape(basis_count * channels, channels)
        coefficients = jnp.concatenate(
            [jnp.dot(flat, weights[:, first:first + LANES], preferred_element_type=F32) for first in range(0, channels, LANES)],
            axis=1,
        )
        scaled = (coefficients.reshape(waves, width, channels) * gain[...][:, None, :]).astype(BF16)
        scaled = scaled.reshape(out_rows, channels)
        straight = jnp.dot(scaled, spectral[0], preferred_element_type=F32)
        turned = jnp.dot(scaled, spectral[1], preferred_element_type=F32).reshape(waves, width, channels)
        even = (iota((1, width, channels), 1) & 1) == 0
        turned = jnp.where(even, -pltpu.roll(turned, width - 1, 1), pltpu.roll(turned, 1, 1))
        out_ref[group] = (straight + turned.reshape(out_rows, channels)).astype(BF16)

    if single_lat:
        build_left(0, factors)
    arrivals.wait_recv()
    repeat(groups, finish)
    filt_arrivals.wait_send()
    arrivals.wait_send()


def per_device(field, tap_mask, tap_weight, basis_mix, order_slots, degree_gain, spectral_mix):
    rows_here, n_lon, channels = field.shape
    assert rows_here == 1
    basis_count = basis_mix.shape[0]
    n_lat = degree_gain.shape[0]
    n_orders = order_slots.shape[0]
    n_lat_dev = lax.axis_size("lat")
    n_ord_dev = lax.axis_size("ord")
    slots_here = n_orders // n_ord_dev
    waves = n_lat // n_lat_dev
    per_slab = min(SLAB // 2, slots_here)
    width = 2 * per_slab
    groups = slots_here // per_slab
    lat_rows = min(n_lat, COLUMNS // width)
    block_rows = min(2 * n_orders, 64)
    out_rows = waves * width
    single = groups == 1 and lat_rows == n_lat
    dims = (n_lat_dev, n_ord_dev, n_lat, n_lon, n_orders, channels, basis_count)
    vmem = pl.BlockSpec(memory_space=pltpu.VMEM)
    hbm = pl.BlockSpec(memory_space=pltpu.HBM)
    result = pl.pallas_call(
        functools.partial(kernel, dims),
        out_shape=pltpu.VMEM((groups, out_rows, channels), BF16),
        in_specs=[hbm] * 7,
        out_specs=vmem,
        scratch_shapes=[
            pltpu.VMEM(tap_mask.shape, jnp.int32),
            pltpu.VMEM(tap_weight.shape, F32),
            pltpu.VMEM((1, n_orders), jnp.int32),
            pltpu.SMEM((1, n_orders), jnp.int32),
            pltpu.VMEM((1, n_lon, channels), BF16),
            pltpu.VMEM((basis_count, channels, channels), BF16),
            pltpu.VMEM((waves, channels), F32),
            pltpu.VMEM((2, channels, channels), BF16),
            pltpu.VMEM((block_rows, n_lon), BF16),
            pltpu.VMEM((n_lat + 2, LANES), F32),
            pltpu.VMEM((n_ord_dev * groups, width, channels), BF16),
            pltpu.VMEM((groups, n_lat, width, channels), BF16),
            pltpu.VMEM((3, out_rows, lat_rows * width), F32),
            pltpu.VMEM((3, 2 * (lat_rows + 2), lat_rows * width), BF16),
            pltpu.VMEM((basis_count * out_rows, lat_rows * width), BF16),
            pltpu.VMEM((8, LANES) if single else (basis_count * out_rows, channels), F32),
            pltpu.SemaphoreType.DMA((8,)),
            pltpu.SemaphoreType.DMA((1,)),
            pltpu.SemaphoreType.DMA((1,)),
            pltpu.SemaphoreType.DMA((1,)),
            pltpu.SemaphoreType.DMA((1,)),
            pltpu.SemaphoreType.REGULAR((3 + n_lat // 2 // (1 if n_lat <= 128 else n_lat_dev),)),
        ],
        compiler_params=pltpu.CompilerParams(
            collective_id=0, has_side_effects=True, vmem_limit_bytes=63 * 1024 * 1024
        ),
    )(*[pltpu.with_memory_space_constraint(x, pltpu.HBM) for x in (tap_mask, tap_weight, order_slots.reshape(1, n_orders), field, basis_mix, degree_gain, spectral_mix)])
    result = result.reshape(groups, waves, per_slab, 2, channels)
    return jnp.swapaxes(result, 0, 1).reshape(waves, slots_here, 2, channels)


def solution(mesh):
    in_specs = (
        P(("lat", "ord"), None, None),
        P(("lat", "ord"), None, None),
        P(("lat", "ord"), None, None),
        P(),
        P(),
        P(),
        P(),
    )
    out_specs = P("lat", "ord", None, None)
    return jax.shard_map(
        per_device, mesh=mesh, in_specs=in_specs, out_specs=out_specs, check_vma=False
    )
```

```python
import functools
import math

import jax
import jax.numpy as jnp
from jax import lax
from jax.experimental import pallas as pl
from jax.experimental.pallas import tpu as pltpu
from jax.sharding import PartitionSpec as P

MESH = pl.DeviceIdType.MESH
F32 = jnp.float32
BF16 = jnp.bfloat16
SLAB = 8
COLUMNS = 256
LANES = 128


def log2(n):
    assert n & (n - 1) == 0
    return n.bit_length() - 1


def cosine(phase_int, period):
    q = phase_int & (period - 1)
    r = jnp.minimum(q, period - q)
    x = (period // 4 - r).astype(F32) * (2.0 * math.pi / period)
    x2 = x * x
    total = jnp.full_like(x, -1.0 / math.factorial(11))
    for power, sign in ((9, 1.0), (7, -1.0), (5, 1.0), (3, -1.0), (1, 1.0)):
        total = total * x2 + sign / math.factorial(power)
    return total * x


def iota(shape, dim):
    return lax.broadcasted_iota(jnp.int32, shape, dim)


def repeat(count, body):
    if count == 1:
        body(0)
    else:
        pl.loop(0, count)(body)


def kernel(
    dims,
    mask_hbm, weight_hbm, slots_hbm, field_hbm, basis_hbm, gain_hbm, spectral_hbm,
    out_ref,
    mask_ref, weight_ref, slots_ref, slots_smem, field, basis, gain, spectral, table, filt, sent, held, lat_tab, select, left, mixed,
    local_sem, filt_send, filt_recv, all_send, all_recv, ready,
):
    n_lat_dev, n_ord_dev, n_lat, n_lon, n_orders, channels, basis_count = dims
    lat_id = lax.axis_index("lat")
    ord_id = lax.axis_index("ord")
    row_id = lat_id * n_ord_dev + ord_id
    slots_here = n_orders // n_ord_dev
    waves = n_lat // n_lat_dev
    per_slab = min(SLAB // 2, slots_here)
    width = 2 * per_slab
    groups = slots_here // per_slab
    count = n_lat_dev * n_ord_dev
    lat_rows = min(n_lat, COLUMNS // width)
    parts = n_lat // lat_rows
    cols = lat_rows * width
    out_rows = waves * width

    lat_bits = log2(n_lat_dev)
    lat_mask = n_lat_dev - 1
    levels = n_ord_dev // 2
    chips = levels * n_lat_dev
    level = ord_id >> 1
    chip = level * n_lat_dev + lat_id
    leader = (ord_id & 1) == 1
    follower = (ord_id & 1) == 0
    half = levels // 2
    top = (levels - 1) * n_lat_dev
    direct = levels - 1
    low = level < direct
    sibling = (lat_id, ord_id ^ 1)
    per_ready = 1 if chips <= 64 else n_lat_dev

    def device(other, core):
        return (other & lat_mask, ((other >> lat_bits) << 1) + core)

    def on_both(other, body):
        body(device(other, 1))
        body(device(other, 0))

    slots_copy = pltpu.make_async_copy(slots_hbm, slots_ref, local_sem.at[0])
    field_copy = pltpu.make_async_copy(field_hbm, field, local_sem.at[1])
    mask_copy = pltpu.make_async_copy(mask_hbm, mask_ref, local_sem.at[2])
    weight_copy = pltpu.make_async_copy(weight_hbm, weight_ref, local_sem.at[3])
    smem_copy = pltpu.make_async_copy(slots_hbm, slots_smem, local_sem.at[4])
    gain_copy = pltpu.make_async_copy(
        gain_hbm.at[pl.ds(pl.multiple_of(lat_id * waves, waves), waves)], gain, local_sem.at[5]
    )
    spectral_copy = pltpu.make_async_copy(spectral_hbm, spectral, local_sem.at[6])
    basis_copy = pltpu.make_async_copy(basis_hbm, basis, local_sem.at[7])
    barrier = pltpu.get_barrier_semaphore()

    def greet(target):
        pl.semaphore_signal(barrier, inc=1, device_id=target, device_id_type=MESH)

    def signal(semaphore, target):
        pl.semaphore_signal(semaphore, inc=1, device_id=target, device_id_type=MESH)

    mask_copy.start()
    weight_copy.start()
    slots_copy.start()
    field_copy.start()
    greet(sibling)
    pl.loop(chip + 1, chips)(lambda other: greet(device(other, 1)))

    @pl.when(chip == 0)
    def _():
        pl.loop(direct * n_lat_dev, chips)(lambda other: greet(device(other, 0)))

    @pl.when(level == levels - 1)
    def _():
        pl.loop(0, direct * n_lat_dev)(lambda other: greet(device(other, 0)))

    smem_copy.start()

    filt[pl.ds(0, 1)] = jnp.zeros((1, LANES), F32)
    filt[pl.ds(n_lat + 1, 1)] = jnp.zeros((1, LANES), F32)

    mask_copy.wait()
    weight_copy.wait()
    taps = mask_ref[0].astype(F32) * weight_ref[0]
    tap_count = taps.shape[1]
    lane = iota((basis_count, LANES), 1)
    spread = jnp.zeros((basis_count, LANES), F32)
    for tap in range(tap_count):
        spread = jnp.where(lane // basis_count == tap, taps[:, tap:tap + 1], spread)
    spread = jnp.where(lane % basis_count == iota((basis_count, LANES), 0), spread, 0.0)
    filt[pl.ds(row_id + 1, 1)] = jnp.sum(spread, axis=0, keepdims=True)

    def send_filters(target):
        pltpu.make_async_remote_copy(
            src_ref=filt.at[pl.ds(row_id + 1, 1)], dst_ref=filt.at[pl.ds(row_id + 1, 1)],
            send_sem=filt_send.at[0], recv_sem=filt_recv.at[0],
            device_id=target, device_id_type=MESH,
        ).start()

    def send_rows(target):
        pltpu.make_async_remote_copy(
            src_ref=sent.at[pl.ds(target[1] * groups, groups)], dst_ref=held.at[:, row_id],
            send_sem=all_send.at[0], recv_sem=all_recv.at[0],
            device_id=target, device_id_type=MESH,
        ).start()

    def send(target):
        send_filters(target)
        send_rows(target)

    early_sem, known_sem, top_sem = ready.at[chips // per_ready], ready.at[chips // per_ready + 1], ready.at[chips // per_ready + 2]

    @pl.when(jnp.logical_and(follower, jnp.logical_not(low)))
    def _():
        pl.semaphore_wait(barrier, 3)
        signal(early_sem, sibling)

    @pl.when(jnp.logical_and(leader, jnp.logical_not(low)))
    def _():
        pl.semaphore_wait(early_sem, 1)

    @pl.when(jnp.logical_not(low))
    def _():
        send_filters(device(0, 0))
        send_filters(device(0, 1))

    slots_copy.wait()
    orders = slots_ref[...]
    block_rows = table.shape[0]

    def dft_block(start):
        row = iota((block_rows, 1), 0) + start
        found = iota((block_rows, n_orders), 1) == row >> 1
        order = jnp.sum(jnp.where(found, orders.astype(F32), 0.0), axis=1, keepdims=True).astype(jnp.int32)
        phase = order * iota((block_rows, n_lon), 1) + (n_lon // 4) * (row & 1)
        table[...] = (cosine(phase, n_lon) * (1.0 / math.sqrt(n_lon))).astype(BF16)

    single_dft = block_rows == 2 * n_orders
    if single_dft:
        dft_block(0)
    slabs = block_rows // width

    field_copy.wait()

    def transform(block):
        if not single_dft:
            dft_block(block * block_rows)
        rows = jnp.dot(table[...], field[0], preferred_element_type=F32).astype(BF16)
        sent[pl.ds(block * slabs, slabs)] = rows.reshape(slabs, width, channels)

    def send_first():
        @pl.when(jnp.logical_not(low))
        def _():
            send_rows(device(0, 0))
            send_rows(device(0, 1))

    def transform_rows(first, last):
        rows = jnp.dot(table[first:last], field[0], preferred_element_type=F32).astype(BF16)
        sent[first // width:last // width] = rows.reshape((last - first) // width, width, channels)

    first_rows = 4 * slots_here
    if single_dft and first_rows % 16 == 0 and first_rows < block_rows:
        transform_rows(0, first_rows)
        send_first()
        transform_rows(first_rows, block_rows)
    else:
        repeat(2 * n_orders // block_rows, transform)
        send_first()

    basis_copy.start()
    gain_copy.start()
    spectral_copy.start()

    @pl.when(leader)
    def _():
        pl.semaphore_wait(barrier, 2 * chip + 1)
        signal(known_sem, sibling)
        block = chip // per_ready
        first = jnp.where(level == levels - 1, direct * n_lat_dev, 0)
        pl.loop(first, chip)(lambda other: on_both(other, lambda target: signal(ready.at[block], target)))

    @pl.when(follower)
    def _():
        pl.semaphore_wait(known_sem, 1)

    pl.loop(jnp.where(low, 0, 1), chip)(lambda other: on_both(other, send))
    send(sibling)
    held[:, row_id] = sent[pl.ds(ord_id * groups, groups)]

    smem_copy.wait()

    def lane_orders(group):
        place = (iota((1, cols), 1) & (width - 1)) >> 1
        order = jnp.zeros((1, cols), jnp.int32)
        for slot in range(per_slab):
            order = jnp.where(place == slot, slots_smem[0, ord_id * slots_here + group * per_slab + slot], order)
        return order

    def lat_tables(group, part):
        order = lane_orders(group)
        col = iota((1, cols), 1)
        row = iota((out_rows, 1), 0)
        wave = (row >> log2(width)) + lat_id * waves
        same = ((row & (width - 1)) >> 1) == ((col & (width - 1)) >> 1)
        for step in range(3):
            lat = (col >> log2(width)) + part * lat_rows + 1 - step
            phase = wave * (2 * lat + 1) + jnp.where((order & 1) == 0, 0, 3 * n_lat)
            value = cosine(phase, 4 * n_lat) * math.sqrt(2.0 / n_lat)
            lat_tab[step] = jnp.where(same, value, 0.0)

    def tap_factors(group):
        order = lane_orders(group)
        row = iota((16, cols), 0)
        lon_step = (row & 7) - 2
        part_of = iota((16, cols), 1) & 1
        phase = order * lon_step + (n_lon // 4) * (part_of - (row >> 3))
        return cosine(phase, n_lon)

    window_row = iota((lat_rows + 2, cols), 0)
    window_lat = iota((lat_rows + 2, cols), 1) >> log2(width)
    for step in range(3):
        chosen = (window_row == window_lat + 2 - step).astype(F32)
        select[step] = jnp.concatenate([chosen, chosen], axis=0).astype(BF16)

    single_lat = groups == 1 and parts == 1
    if single_lat:
        lat_tables(0, 0)
        factors = tap_factors(0)

    def answer(block):
        first = jnp.maximum(chip + 1, block * per_ready)
        last = (block + 1) * per_ready

        @pl.when(jnp.logical_or(jnp.logical_not(low), block < top // per_ready))
        def _():
            pl.semaphore_wait(ready.at[block], last - first)

        pl.loop(first, last)(lambda other: on_both(other, send))

    start = (chip + 1) // per_ready
    half_block, top_block = half * n_lat_dev // per_ready, top // per_ready
    pl.loop(start, half_block)(answer)

    def answer_top():
        pl.loop(jnp.maximum(start, top_block), chips // per_ready)(answer)

    def answer_rest():
        pl.loop(jnp.maximum(start, half_block), top_block)(answer)

    top_first = jnp.logical_and(low, follower)

    @pl.when(jnp.logical_not(top_first))
    def _():
        answer_rest()

    @pl.when(jnp.logical_and(follower, low))
    def _():
        pl.semaphore_wait(barrier, 2 * n_lat_dev + 1)
        signal(top_sem, sibling)

    @pl.when(jnp.logical_and(leader, low))
    def _():
        pl.semaphore_wait(top_sem, 1)

    answer_top()

    @pl.when(top_first)
    def _():
        answer_rest()

    gain_copy.wait()
    spectral_copy.wait()
    basis_copy.wait()
    filt_arrivals = pltpu.make_async_remote_copy(
        src_ref=filt.at[pl.ds(0, count - 1)], dst_ref=filt.at[pl.ds(0, count - 1)],
        send_sem=filt_send.at[0], recv_sem=filt_recv.at[0],
        device_id=(lat_id, ord_id ^ 1), device_id_type=MESH,
    )
    arrivals = pltpu.make_async_remote_copy(
        src_ref=held.at[:, pl.ds(0, count - 1)], dst_ref=held.at[:, pl.ds(0, count - 1)],
        send_sem=all_send.at[0], recv_sem=all_recv.at[0],
        device_id=(lat_id, ord_id ^ 1), device_id_type=MESH,
    )
    filt_arrivals.wait_recv()

    def build_left(part, factors):
        window = filt[pl.ds(part * lat_rows, lat_rows + 2)]
        high = window.astype(BF16)
        low = (window - high.astype(F32)).astype(BF16)
        both = jnp.concatenate([high.astype(F32), low.astype(F32)], axis=0).T.astype(BF16)
        real, imag = [], []
        for step in range(3):
            first = 5 * step * basis_count
            wide = jnp.dot(both[first:first + 5 * basis_count], select[step], preferred_element_type=F32)
            sums = [None, None]
            for lon_step in range(5):
                values = wide[lon_step * basis_count:(lon_step + 1) * basis_count]
                for which in range(2):
                    term = values * factors[8 * which + lon_step:8 * which + lon_step + 1]
                    sums[which] = term if sums[which] is None else sums[which] + term
            real.append(sums[0])
            imag.append(sums[1])
        even = (iota((width, cols), 0) & 1) == 0
        for b in range(basis_count):
            total = None
            for step in range(3):
                turn = jnp.where(even, real[step][b:b + 1], imag[step][b:b + 1])
                term = lat_tab[step].reshape(waves, width, cols) * turn[None]
                total = term if total is None else total + term
            left[pl.ds(b * out_rows, out_rows)] = total.reshape(out_rows, cols).astype(BF16)

    def latitude(group, part):
        rows = held[group, pl.ds(part * lat_rows, lat_rows)].reshape(cols, channels)
        return jnp.dot(left[...], rows, preferred_element_type=F32)

    def finish(group):
        if single_lat:
            total = latitude(group, 0)
        else:
            factors_here = tap_factors(group)
            mixed[...] = jnp.zeros(mixed.shape, F32)

            def add(part):
                lat_tables(group, part)
                build_left(part, factors_here)
                mixed[...] += latitude(group, part)

            pl.loop(0, parts)(add)
            total = mixed[...]
        total = total.astype(BF16)
        flat = jnp.concatenate([total[b * out_rows:(b + 1) * out_rows] for b in range(basis_count)], axis=1)
        weights = basis[...].reshape(basis_count * channels, channels)
        coefficients = jnp.concatenate(
            [jnp.dot(flat, weights[:, first:first + LANES], preferred_element_type=F32) for first in range(0, channels, LANES)],
            axis=1,
        )
        scaled = (coefficients.reshape(waves, width, channels) * gain[...][:, None, :]).astype(BF16)
        scaled = scaled.reshape(out_rows, channels)
        straight = jnp.dot(scaled, spectral[0], preferred_element_type=F32)
        turned = jnp.dot(scaled, spectral[1], preferred_element_type=F32).reshape(waves, width, channels)
        even = (iota((1, width, channels), 1) & 1) == 0
        turned = jnp.where(even, -pltpu.roll(turned, width - 1, 1), pltpu.roll(turned, 1, 1))
        out_ref[group] = (straight + turned.reshape(out_rows, channels)).astype(BF16)

    if single_lat:
        build_left(0, factors)
    arrivals.wait_recv()
    repeat(groups, finish)
    filt_arrivals.wait_send()
    arrivals.wait_send()


def per_device(field, tap_mask, tap_weight, basis_mix, order_slots, degree_gain, spectral_mix):
    rows_here, n_lon, channels = field.shape
    assert rows_here == 1
    basis_count = basis_mix.shape[0]
    n_lat = degree_gain.shape[0]
    n_orders = order_slots.shape[0]
    n_lat_dev = lax.axis_size("lat")
    n_ord_dev = lax.axis_size("ord")
    slots_here = n_orders // n_ord_dev
    waves = n_lat // n_lat_dev
    per_slab = min(SLAB // 2, slots_here)
    width = 2 * per_slab
    groups = slots_here // per_slab
    lat_rows = min(n_lat, COLUMNS // width)
    block_rows = min(2 * n_orders, 64)
    out_rows = waves * width
    single = groups == 1 and lat_rows == n_lat
    dims = (n_lat_dev, n_ord_dev, n_lat, n_lon, n_orders, channels, basis_count)
    vmem = pl.BlockSpec(memory_space=pltpu.VMEM)
    hbm = pl.BlockSpec(memory_space=pltpu.HBM)
    result = pl.pallas_call(
        functools.partial(kernel, dims),
        out_shape=pltpu.VMEM((groups, out_rows, channels), BF16),
        in_specs=[hbm] * 7,
        out_specs=vmem,
        scratch_shapes=[
            pltpu.VMEM(tap_mask.shape, jnp.int32),
            pltpu.VMEM(tap_weight.shape, F32),
            pltpu.VMEM((1, n_orders), jnp.int32),
            pltpu.SMEM((1, n_orders), jnp.int32),
            pltpu.VMEM((1, n_lon, channels), BF16),
            pltpu.VMEM((basis_count, channels, channels), BF16),
            pltpu.VMEM((waves, channels), F32),
            pltpu.VMEM((2, channels, channels), BF16),
            pltpu.VMEM((block_rows, n_lon), BF16),
            pltpu.VMEM((n_lat + 2, LANES), F32),
            pltpu.VMEM((n_ord_dev * groups, width, channels), BF16),
            pltpu.VMEM((groups, n_lat, width, channels), BF16),
            pltpu.VMEM((3, out_rows, lat_rows * width), F32),
            pltpu.VMEM((3, 2 * (lat_rows + 2), lat_rows * width), BF16),
            pltpu.VMEM((basis_count * out_rows, lat_rows * width), BF16),
            pltpu.VMEM((8, LANES) if single else (basis_count * out_rows, channels), F32),
            pltpu.SemaphoreType.DMA((8,)),
            pltpu.SemaphoreType.DMA((1,)),
            pltpu.SemaphoreType.DMA((1,)),
            pltpu.SemaphoreType.DMA((1,)),
            pltpu.SemaphoreType.DMA((1,)),
            pltpu.SemaphoreType.REGULAR((3 + n_lat // 2 // (1 if n_lat <= 128 else n_lat_dev),)),
        ],
        compiler_params=pltpu.CompilerParams(
            collective_id=0, has_side_effects=True, vmem_limit_bytes=63 * 1024 * 1024
        ),
    )(*[pltpu.with_memory_space_constraint(x, pltpu.HBM) for x in (tap_mask, tap_weight, order_slots.reshape(1, n_orders), field, basis_mix, degree_gain, spectral_mix)])
    result = result.reshape(groups, waves, per_slab, 2, channels)
    return jnp.swapaxes(result, 0, 1).reshape(waves, slots_here, 2, channels)


def solution(mesh):
    in_specs = (
        P(("lat", "ord"), None, None),
        P(("lat", "ord"), None, None),
        P(("lat", "ord"), None, None),
        P(),
        P(),
        P(),
        P(),
    )
    out_specs = P("lat", "ord", None, None)
    return jax.shard_map(
        per_device, mesh=mesh, in_specs=in_specs, out_specs=out_specs, check_vma=False
    )
```

```python
import functools
import math

import jax
import jax.numpy as jnp
from jax import lax
from jax.experimental import pallas as pl
from jax.experimental.pallas import tpu as pltpu
from jax.sharding import PartitionSpec as P

MESH = pl.DeviceIdType.MESH
F32 = jnp.float32
BF16 = jnp.bfloat16
SLAB = 8
COLUMNS = 256
LANES = 128


def log2(n):
    assert n & (n - 1) == 0
    return n.bit_length() - 1


def cosine(phase_int, period):
    q = phase_int & (period - 1)
    r = jnp.minimum(q, period - q)
    x = (period // 4 - r).astype(F32) * (2.0 * math.pi / period)
    x2 = x * x
    total = jnp.full_like(x, -1.0 / math.factorial(11))
    for power, sign in ((9, 1.0), (7, -1.0), (5, 1.0), (3, -1.0), (1, 1.0)):
        total = total * x2 + sign / math.factorial(power)
    return total * x


def iota(shape, dim):
    return lax.broadcasted_iota(jnp.int32, shape, dim)


def repeat(count, body):
    if count == 1:
        body(0)
    else:
        pl.loop(0, count)(body)


def kernel(
    dims,
    mask_hbm, weight_hbm, slots_hbm, field_hbm, basis_hbm, gain_hbm, spectral_hbm,
    out_ref,
    mask_ref, weight_ref, slots_ref, slots_smem, field, basis, gain, spectral, table, filt, sent, held, lat_tab, select, left, mixed,
    local_sem, filt_send, filt_recv, all_send, all_recv, ready,
):
    n_lat_dev, n_ord_dev, n_lat, n_lon, n_orders, channels, basis_count = dims
    lat_id = lax.axis_index("lat")
    ord_id = lax.axis_index("ord")
    row_id = lat_id * n_ord_dev + ord_id
    slots_here = n_orders // n_ord_dev
    waves = n_lat // n_lat_dev
    per_slab = min(SLAB // 2, slots_here)
    width = 2 * per_slab
    groups = slots_here // per_slab
    count = n_lat_dev * n_ord_dev
    lat_rows = min(n_lat, COLUMNS // width)
    parts = n_lat // lat_rows
    cols = lat_rows * width
    out_rows = waves * width

    lat_bits = log2(n_lat_dev)
    lat_mask = n_lat_dev - 1
    levels = n_ord_dev // 2
    chips = levels * n_lat_dev
    level = ord_id >> 1
    chip = level * n_lat_dev + lat_id
    leader = (ord_id & 1) == 1
    follower = (ord_id & 1) == 0
    half = levels // 2
    top = (levels - 1) * n_lat_dev
    low = level < half
    sibling = (lat_id, ord_id ^ 1)
    per_ready = 1 if chips <= 64 else n_lat_dev

    def device(other, core):
        return (other & lat_mask, ((other >> lat_bits) << 1) + core)

    def on_both(other, body):
        body(device(other, 1))
        body(device(other, 0))

    slots_copy = pltpu.make_async_copy(slots_hbm, slots_ref, local_sem.at[0])
    field_copy = pltpu.make_async_copy(field_hbm, field, local_sem.at[1])
    mask_copy = pltpu.make_async_copy(mask_hbm, mask_ref, local_sem.at[2])
    weight_copy = pltpu.make_async_copy(weight_hbm, weight_ref, local_sem.at[3])
    smem_copy = pltpu.make_async_copy(slots_hbm, slots_smem, local_sem.at[4])
    gain_copy = pltpu.make_async_copy(
        gain_hbm.at[pl.ds(pl.multiple_of(lat_id * waves, waves), waves)], gain, local_sem.at[5]
    )
    spectral_copy = pltpu.make_async_copy(spectral_hbm, spectral, local_sem.at[6])
    basis_copy = pltpu.make_async_copy(basis_hbm, basis, local_sem.at[7])
    barrier = pltpu.get_barrier_semaphore()

    def greet(target):
        pl.semaphore_signal(barrier, inc=1, device_id=target, device_id_type=MESH)

    def signal(semaphore, target):
        pl.semaphore_signal(semaphore, inc=1, device_id=target, device_id_type=MESH)

    mask_copy.start()
    weight_copy.start()
    slots_copy.start()
    field_copy.start()
    greet(sibling)
    pl.loop(chip + 1, chips)(lambda other: greet(device(other, 1)))

    @pl.when(chip == 0)
    def _():
        pl.loop(half * n_lat_dev, chips)(lambda other: greet(device(other, 0)))

    @pl.when(level == levels - 1)
    def _():
        pl.loop(0, half * n_lat_dev)(lambda other: greet(device(other, 0)))

    smem_copy.start()
    basis_copy.start()
    gain_copy.start()
    spectral_copy.start()

    early_sem, known_sem, top_sem = ready.at[chips // per_ready], ready.at[chips // per_ready + 1], ready.at[chips // per_ready + 2]

    @pl.when(jnp.logical_and(follower, jnp.logical_not(low)))
    def _():
        pl.semaphore_wait(barrier, 3)
        signal(early_sem, sibling)

    filt[pl.ds(0, 1)] = jnp.zeros((1, LANES), F32)
    filt[pl.ds(n_lat + 1, 1)] = jnp.zeros((1, LANES), F32)

    mask_copy.wait()
    weight_copy.wait()
    taps = mask_ref[0].astype(F32) * weight_ref[0]
    tap_count = taps.shape[1]
    lane = iota((basis_count, LANES), 1)
    spread = jnp.zeros((basis_count, LANES), F32)
    for tap in range(tap_count):
        spread = jnp.where(lane // basis_count == tap, taps[:, tap:tap + 1], spread)
    spread = jnp.where(lane % basis_count == iota((basis_count, LANES), 0), spread, 0.0)
    filt[pl.ds(row_id + 1, 1)] = jnp.sum(spread, axis=0, keepdims=True)

    def send_filters(target):
        pltpu.make_async_remote_copy(
            src_ref=filt.at[pl.ds(row_id + 1, 1)], dst_ref=filt.at[pl.ds(row_id + 1, 1)],
            send_sem=filt_send.at[0], recv_sem=filt_recv.at[0],
            device_id=target, device_id_type=MESH,
        ).start()

    def send_rows(target):
        pltpu.make_async_remote_copy(
            src_ref=sent.at[pl.ds(target[1] * groups, groups)], dst_ref=held.at[:, row_id],
            send_sem=all_send.at[0], recv_sem=all_recv.at[0],
            device_id=target, device_id_type=MESH,
        ).start()

    def send(target):
        send_filters(target)
        send_rows(target)


    @pl.when(jnp.logical_and(leader, jnp.logical_not(low)))
    def _():
        pl.semaphore_wait(early_sem, 1)

    @pl.when(jnp.logical_not(low))
    def _():
        send_filters(device(0, 0))
        send_filters(device(0, 1))

    slots_copy.wait()
    orders = slots_ref[...]
    block_rows = table.shape[0]

    def dft_block(start):
        row = iota((block_rows, 1), 0) + start
        found = iota((block_rows, n_orders), 1) == row >> 1
        order = jnp.sum(jnp.where(found, orders.astype(F32), 0.0), axis=1, keepdims=True).astype(jnp.int32)
        phase = order * iota((block_rows, n_lon), 1) + (n_lon // 4) * (row & 1)
        table[...] = (cosine(phase, n_lon) * (1.0 / math.sqrt(n_lon))).astype(BF16)

    single_dft = block_rows == 2 * n_orders
    if single_dft:
        dft_block(0)
    slabs = block_rows // width

    field_copy.wait()

    def transform(block):
        if not single_dft:
            dft_block(block * block_rows)
        rows = jnp.dot(table[...], field[0], preferred_element_type=F32).astype(BF16)
        sent[pl.ds(block * slabs, slabs)] = rows.reshape(slabs, width, channels)

    def send_first():
        @pl.when(jnp.logical_not(low))
        def _():
            send_rows(device(0, 0))
            send_rows(device(0, 1))

    def transform_rows(first, last):
        rows = jnp.dot(table[first:last], field[0], preferred_element_type=F32).astype(BF16)
        sent[first // width:last // width] = rows.reshape((last - first) // width, width, channels)

    first_rows = 4 * slots_here
    if single_dft and first_rows % 16 == 0 and first_rows < block_rows:
        transform_rows(0, first_rows)
        send_first()
        transform_rows(first_rows, block_rows)
    else:
        repeat(2 * n_orders // block_rows, transform)
        send_first()

    @pl.when(leader)
    def _():
        pl.semaphore_wait(barrier, 2 * chip + 1)
        signal(known_sem, sibling)
        block = chip // per_ready
        first = jnp.where(level == levels - 1, half * n_lat_dev, 0)
        pl.loop(first, chip)(lambda other: on_both(other, lambda target: signal(ready.at[block], target)))

    @pl.when(follower)
    def _():
        pl.semaphore_wait(known_sem, 1)

    pl.loop(jnp.where(low, 0, 1), chip)(lambda other: on_both(other, send))
    send(sibling)
    held[:, row_id] = sent[pl.ds(ord_id * groups, groups)]

    smem_copy.wait()

    def lane_orders(group):
        place = (iota((1, cols), 1) & (width - 1)) >> 1
        order = jnp.zeros((1, cols), jnp.int32)
        for slot in range(per_slab):
            order = jnp.where(place == slot, slots_smem[0, ord_id * slots_here + group * per_slab + slot], order)
        return order

    def lat_tables(group, part):
        order = lane_orders(group)
        col = iota((1, cols), 1)
        row = iota((out_rows, 1), 0)
        wave = (row >> log2(width)) + lat_id * waves
        same = ((row & (width - 1)) >> 1) == ((col & (width - 1)) >> 1)
        for step in range(3):
            lat = (col >> log2(width)) + part * lat_rows + 1 - step
            phase = wave * (2 * lat + 1) + jnp.where((order & 1) == 0, 0, 3 * n_lat)
            value = cosine(phase, 4 * n_lat) * math.sqrt(2.0 / n_lat)
            lat_tab[step] = jnp.where(same, value, 0.0)

    def tap_factors(group):
        order = lane_orders(group)
        row = iota((16, cols), 0)
        lon_step = (row & 7) - 2
        part_of = iota((16, cols), 1) & 1
        phase = order * lon_step + (n_lon // 4) * (part_of - (row >> 3))
        return cosine(phase, n_lon)

    window_row = iota((lat_rows + 2, cols), 0)
    window_lat = iota((lat_rows + 2, cols), 1) >> log2(width)
    for step in range(3):
        chosen = (window_row == window_lat + 2 - step).astype(F32)
        select[step] = jnp.concatenate([chosen, chosen], axis=0).astype(BF16)

    single_lat = groups == 1 and parts == 1
    if single_lat:
        lat_tables(0, 0)
        factors = tap_factors(0)

    def answer(block):
        first = jnp.maximum(chip + 1, block * per_ready)
        last = (block + 1) * per_ready

        @pl.when(jnp.logical_or(jnp.logical_not(low), block < top // per_ready))
        def _():
            pl.semaphore_wait(ready.at[block], last - first)

        pl.loop(first, last)(lambda other: on_both(other, send))

    start = (chip + 1) // per_ready
    half_block, top_block = half * n_lat_dev // per_ready, top // per_ready
    pl.loop(start, half_block)(answer)

    def answer_top():
        pl.loop(jnp.maximum(start, top_block), chips // per_ready)(answer)

    def answer_rest():
        pl.loop(jnp.maximum(start, half_block), top_block)(answer)

    top_first = jnp.logical_and(low, follower)

    @pl.when(jnp.logical_not(top_first))
    def _():
        answer_rest()

    @pl.when(jnp.logical_and(follower, low))
    def _():
        pl.semaphore_wait(barrier, 2 * n_lat_dev + 1)
        signal(top_sem, sibling)

    @pl.when(jnp.logical_and(leader, low))
    def _():
        pl.semaphore_wait(top_sem, 1)

    answer_top()

    @pl.when(top_first)
    def _():
        answer_rest()

    gain_copy.wait()
    spectral_copy.wait()
    basis_copy.wait()
    filt_arrivals = pltpu.make_async_remote_copy(
        src_ref=filt.at[pl.ds(0, count - 1)], dst_ref=filt.at[pl.ds(0, count - 1)],
        send_sem=filt_send.at[0], recv_sem=filt_recv.at[0],
        device_id=(lat_id, ord_id ^ 1), device_id_type=MESH,
    )
    arrivals = pltpu.make_async_remote_copy(
        src_ref=held.at[:, pl.ds(0, count - 1)], dst_ref=held.at[:, pl.ds(0, count - 1)],
        send_sem=all_send.at[0], recv_sem=all_recv.at[0],
        device_id=(lat_id, ord_id ^ 1), device_id_type=MESH,
    )
    filt_arrivals.wait_recv()

    def build_left(part, factors):
        window = filt[pl.ds(part * lat_rows, lat_rows + 2)]
        high = window.astype(BF16)
        low = (window - high.astype(F32)).astype(BF16)
        both = jnp.concatenate([high.astype(F32), low.astype(F32)], axis=0).T.astype(BF16)
        real, imag = [], []
        for step in range(3):
            first = 5 * step * basis_count
            wide = jnp.dot(both[first:first + 5 * basis_count], select[step], preferred_element_type=F32)
            sums = [None, None]
            for lon_step in range(5):
                values = wide[lon_step * basis_count:(lon_step + 1) * basis_count]
                for which in range(2):
                    term = values * factors[8 * which + lon_step:8 * which + lon_step + 1]
                    sums[which] = term if sums[which] is None else sums[which] + term
            real.append(sums[0])
            imag.append(sums[1])
        even = (iota((width, cols), 0) & 1) == 0
        for b in range(basis_count):
            total = None
            for step in range(3):
                turn = jnp.where(even, real[step][b:b + 1], imag[step][b:b + 1])
                term = lat_tab[step].reshape(waves, width, cols) * turn[None]
                total = term if total is None else total + term
            left[pl.ds(b * out_rows, out_rows)] = total.reshape(out_rows, cols).astype(BF16)

    def latitude(group, part):
        rows = held[group, pl.ds(part * lat_rows, lat_rows)].reshape(cols, channels)
        return jnp.dot(left[...], rows, preferred_element_type=F32)

    def finish(group):
        if single_lat:
            total = latitude(group, 0)
        else:
            factors_here = tap_factors(group)
            mixed[...] = jnp.zeros(mixed.shape, F32)

            def add(part):
                lat_tables(group, part)
                build_left(part, factors_here)
                mixed[...] += latitude(group, part)

            pl.loop(0, parts)(add)
            total = mixed[...]
        total = total.astype(BF16)
        flat = jnp.concatenate([total[b * out_rows:(b + 1) * out_rows] for b in range(basis_count)], axis=1)
        weights = basis[...].reshape(basis_count * channels, channels)
        coefficients = jnp.concatenate(
            [jnp.dot(flat, weights[:, first:first + LANES], preferred_element_type=F32) for first in range(0, channels, LANES)],
            axis=1,
        )
        scaled = (coefficients.reshape(waves, width, channels) * gain[...][:, None, :]).astype(BF16)
        scaled = scaled.reshape(out_rows, channels)
        straight = jnp.dot(scaled, spectral[0], preferred_element_type=F32)
        turned = jnp.dot(scaled, spectral[1], preferred_element_type=F32).reshape(waves, width, channels)
        even = (iota((1, width, channels), 1) & 1) == 0
        turned = jnp.where(even, -pltpu.roll(turned, width - 1, 1), pltpu.roll(turned, 1, 1))
        out_ref[group] = (straight + turned.reshape(out_rows, channels)).astype(BF16)

    if single_lat:
        build_left(0, factors)
    arrivals.wait_recv()
    repeat(groups, finish)
    filt_arrivals.wait_send()
    arrivals.wait_send()


def per_device(field, tap_mask, tap_weight, basis_mix, order_slots, degree_gain, spectral_mix):
    rows_here, n_lon, channels = field.shape
    assert rows_here == 1
    basis_count = basis_mix.shape[0]
    n_lat = degree_gain.shape[0]
    n_orders = order_slots.shape[0]
    n_lat_dev = lax.axis_size("lat")
    n_ord_dev = lax.axis_size("ord")
    slots_here = n_orders // n_ord_dev
    waves = n_lat // n_lat_dev
    per_slab = min(SLAB // 2, slots_here)
    width = 2 * per_slab
    groups = slots_here // per_slab
    lat_rows = min(n_lat, COLUMNS // width)
    block_rows = min(2 * n_orders, 64)
    out_rows = waves * width
    single = groups == 1 and lat_rows == n_lat
    dims = (n_lat_dev, n_ord_dev, n_lat, n_lon, n_orders, channels, basis_count)
    vmem = pl.BlockSpec(memory_space=pltpu.VMEM)
    hbm = pl.BlockSpec(memory_space=pltpu.HBM)
    result = pl.pallas_call(
        functools.partial(kernel, dims),
        out_shape=pltpu.VMEM((groups, out_rows, channels), BF16),
        in_specs=[hbm] * 7,
        out_specs=vmem,
        scratch_shapes=[
            pltpu.VMEM(tap_mask.shape, jnp.int32),
            pltpu.VMEM(tap_weight.shape, F32),
            pltpu.VMEM((1, n_orders), jnp.int32),
            pltpu.SMEM((1, n_orders), jnp.int32),
            pltpu.VMEM((1, n_lon, channels), BF16),
            pltpu.VMEM((basis_count, channels, channels), BF16),
            pltpu.VMEM((waves, channels), F32),
            pltpu.VMEM((2, channels, channels), BF16),
            pltpu.VMEM((block_rows, n_lon), BF16),
            pltpu.VMEM((n_lat + 2, LANES), F32),
            pltpu.VMEM((n_ord_dev * groups, width, channels), BF16),
            pltpu.VMEM((groups, n_lat, width, channels), BF16),
            pltpu.VMEM((3, out_rows, lat_rows * width), F32),
            pltpu.VMEM((3, 2 * (lat_rows + 2), lat_rows * width), BF16),
            pltpu.VMEM((basis_count * out_rows, lat_rows * width), BF16),
            pltpu.VMEM((8, LANES) if single else (basis_count * out_rows, channels), F32),
            pltpu.SemaphoreType.DMA((8,)),
            pltpu.SemaphoreType.DMA((1,)),
            pltpu.SemaphoreType.DMA((1,)),
            pltpu.SemaphoreType.DMA((1,)),
            pltpu.SemaphoreType.DMA((1,)),
            pltpu.SemaphoreType.REGULAR((3 + n_lat // 2 // (1 if n_lat <= 128 else n_lat_dev),)),
        ],
        compiler_params=pltpu.CompilerParams(
            collective_id=0, has_side_effects=True, vmem_limit_bytes=63 * 1024 * 1024
        ),
    )(*[pltpu.with_memory_space_constraint(x, pltpu.HBM) for x in (tap_mask, tap_weight, order_slots.reshape(1, n_orders), field, basis_mix, degree_gain, spectral_mix)])
    result = result.reshape(groups, waves, per_slab, 2, channels)
    return jnp.swapaxes(result, 0, 1).reshape(waves, slots_here, 2, channels)


def solution(mesh):
    in_specs = (
        P(("lat", "ord"), None, None),
        P(("lat", "ord"), None, None),
        P(("lat", "ord"), None, None),
        P(),
        P(),
        P(),
        P(),
    )
    out_specs = P("lat", "ord", None, None)
    return jax.shard_map(
        per_device, mesh=mesh, in_specs=in_specs, out_specs=out_specs, check_vma=False
    )
```

```python
import functools
import math

import jax
import jax.numpy as jnp
from jax import lax
from jax.experimental import pallas as pl
from jax.experimental.pallas import tpu as pltpu
from jax.sharding import PartitionSpec as P

MESH = pl.DeviceIdType.MESH
F32 = jnp.float32
BF16 = jnp.bfloat16
SLAB = 8
COLUMNS = 256
LANES = 128


def log2(n):
    assert n & (n - 1) == 0
    return n.bit_length() - 1


def cosine(phase_int, period):
    q = phase_int & (period - 1)
    r = jnp.minimum(q, period - q)
    x = (period // 4 - r).astype(F32) * (2.0 * math.pi / period)
    x2 = x * x
    total = jnp.full_like(x, -1.0 / math.factorial(11))
    for power, sign in ((9, 1.0), (7, -1.0), (5, 1.0), (3, -1.0), (1, 1.0)):
        total = total * x2 + sign / math.factorial(power)
    return total * x


def iota(shape, dim):
    return lax.broadcasted_iota(jnp.int32, shape, dim)


def repeat(count, body):
    if count == 1:
        body(0)
    else:
        pl.loop(0, count)(body)


def kernel(
    dims,
    mask_hbm, weight_hbm, slots_hbm, field_hbm, basis_hbm, gain_hbm, spectral_hbm,
    out_ref,
    mask_ref, weight_ref, slots_ref, slots_smem, field, basis, gain, spectral, table, filt, sent, held, lat_tab, select, left, mixed,
    local_sem, filt_send, filt_recv, all_send, all_recv, ready,
):
    n_lat_dev, n_ord_dev, n_lat, n_lon, n_orders, channels, basis_count = dims
    lat_id = lax.axis_index("lat")
    ord_id = lax.axis_index("ord")
    row_id = lat_id * n_ord_dev + ord_id
    slots_here = n_orders // n_ord_dev
    waves = n_lat // n_lat_dev
    per_slab = min(SLAB // 2, slots_here)
    width = 2 * per_slab
    groups = slots_here // per_slab
    count = n_lat_dev * n_ord_dev
    lat_rows = min(n_lat, COLUMNS // width)
    parts = n_lat // lat_rows
    cols = lat_rows * width
    out_rows = waves * width

    lat_bits = log2(n_lat_dev)
    lat_mask = n_lat_dev - 1
    levels = n_ord_dev // 2
    chips = levels * n_lat_dev
    level = ord_id >> 1
    chip = level * n_lat_dev + lat_id
    leader = (ord_id & 1) == 1
    follower = (ord_id & 1) == 0
    half = levels // 2
    top = (levels - 1) * n_lat_dev
    direct = levels - 1
    low = level < direct
    sibling = (lat_id, ord_id ^ 1)
    per_ready = 1 if chips <= 64 else n_lat_dev

    def device(other, core):
        return (other & lat_mask, ((other >> lat_bits) << 1) + core)

    def on_both(other, body):
        body(device(other, 1))
        body(device(other, 0))

    slots_copy = pltpu.make_async_copy(slots_hbm, slots_ref, local_sem.at[0])
    field_copy = pltpu.make_async_copy(field_hbm, field, local_sem.at[1])
    mask_copy = pltpu.make_async_copy(mask_hbm, mask_ref, local_sem.at[2])
    weight_copy = pltpu.make_async_copy(weight_hbm, weight_ref, local_sem.at[3])
    smem_copy = pltpu.make_async_copy(slots_hbm, slots_smem, local_sem.at[4])
    gain_copy = pltpu.make_async_copy(
        gain_hbm.at[pl.ds(pl.multiple_of(lat_id * waves, waves), waves)], gain, local_sem.at[5]
    )
    spectral_copy = pltpu.make_async_copy(spectral_hbm, spectral, local_sem.at[6])
    basis_copy = pltpu.make_async_copy(basis_hbm, basis, local_sem.at[7])
    barrier = pltpu.get_barrier_semaphore()

    def greet(target):
        pl.semaphore_signal(barrier, inc=1, device_id=target, device_id_type=MESH)

    def signal(semaphore, target):
        pl.semaphore_signal(semaphore, inc=1, device_id=target, device_id_type=MESH)

    mask_copy.start()
    weight_copy.start()
    slots_copy.start()
    field_copy.start()
    greet(sibling)
    pl.loop(chip + 1, chips)(lambda other: greet(device(other, 1)))

    @pl.when(chip == 0)
    def _():
        pl.loop(direct * n_lat_dev, chips)(lambda other: greet(device(other, 0)))

    @pl.when(level == levels - 1)
    def _():
        pl.loop(0, direct * n_lat_dev)(lambda other: greet(device(other, 0)))

    smem_copy.start()

    early_sem, known_sem, top_sem = ready.at[chips // per_ready], ready.at[chips // per_ready + 1], ready.at[chips // per_ready + 2]

    @pl.when(jnp.logical_and(follower, jnp.logical_not(low)))
    def _():
        pl.semaphore_wait(barrier, 3)
        signal(early_sem, sibling)

    filt[pl.ds(0, 1)] = jnp.zeros((1, LANES), F32)
    filt[pl.ds(n_lat + 1, 1)] = jnp.zeros((1, LANES), F32)

    mask_copy.wait()
    weight_copy.wait()
    taps = mask_ref[0].astype(F32) * weight_ref[0]
    tap_count = taps.shape[1]
    lane = iota((basis_count, LANES), 1)
    spread = jnp.zeros((basis_count, LANES), F32)
    for tap in range(tap_count):
        spread = jnp.where(lane // basis_count == tap, taps[:, tap:tap + 1], spread)
    spread = jnp.where(lane % basis_count == iota((basis_count, LANES), 0), spread, 0.0)
    filt[pl.ds(row_id + 1, 1)] = jnp.sum(spread, axis=0, keepdims=True)

    def send_filters(target):
        pltpu.make_async_remote_copy(
            src_ref=filt.at[pl.ds(row_id + 1, 1)], dst_ref=filt.at[pl.ds(row_id + 1, 1)],
            send_sem=filt_send.at[0], recv_sem=filt_recv.at[0],
            device_id=target, device_id_type=MESH,
        ).start()

    def send_rows(target):
        pltpu.make_async_remote_copy(
            src_ref=sent.at[pl.ds(target[1] * groups, groups)], dst_ref=held.at[:, row_id],
            send_sem=all_send.at[0], recv_sem=all_recv.at[0],
            device_id=target, device_id_type=MESH,
        ).start()

    def send(target):
        send_filters(target)
        send_rows(target)


    @pl.when(jnp.logical_and(leader, jnp.logical_not(low)))
    def _():
        pl.semaphore_wait(early_sem, 1)

    @pl.when(jnp.logical_not(low))
    def _():
        send_filters(device(0, 0))
        send_filters(device(0, 1))

    slots_copy.wait()
    orders = slots_ref[...]
    block_rows = table.shape[0]

    def dft_block(start):
        row = iota((block_rows, 1), 0) + start
        found = iota((block_rows, n_orders), 1) == row >> 1
        order = jnp.sum(jnp.where(found, orders.astype(F32), 0.0), axis=1, keepdims=True).astype(jnp.int32)
        phase = order * iota((block_rows, n_lon), 1) + (n_lon // 4) * (row & 1)
        table[...] = (cosine(phase, n_lon) * (1.0 / math.sqrt(n_lon))).astype(BF16)

    single_dft = block_rows == 2 * n_orders
    if single_dft:
        dft_block(0)
    slabs = block_rows // width

    field_copy.wait()

    def transform(block):
        if not single_dft:
            dft_block(block * block_rows)
        rows = jnp.dot(table[...], field[0], preferred_element_type=F32).astype(BF16)
        sent[pl.ds(block * slabs, slabs)] = rows.reshape(slabs, width, channels)

    def send_first():
        @pl.when(jnp.logical_not(low))
        def _():
            send_rows(device(0, 0))
            send_rows(device(0, 1))

    def transform_rows(first, last):
        rows = jnp.dot(table[first:last], field[0], preferred_element_type=F32).astype(BF16)
        sent[first // width:last // width] = rows.reshape((last - first) // width, width, channels)

    first_rows = 4 * slots_here
    if single_dft and first_rows % 16 == 0 and first_rows < block_rows:
        transform_rows(0, first_rows)
        send_first()
        transform_rows(first_rows, block_rows)
    else:
        repeat(2 * n_orders // block_rows, transform)
        send_first()

    basis_copy.start()
    gain_copy.start()
    spectral_copy.start()

    @pl.when(leader)
    def _():
        pl.semaphore_wait(barrier, 2 * chip + 1)
        signal(known_sem, sibling)
        block = chip // per_ready
        first = jnp.where(level == levels - 1, direct * n_lat_dev, 0)
        pl.loop(first, chip)(lambda other: on_both(other, lambda target: signal(ready.at[block], target)))

    @pl.when(follower)
    def _():
        pl.semaphore_wait(known_sem, 1)

    pl.loop(jnp.where(low, 0, 1), chip)(lambda other: on_both(other, send))
    send(sibling)
    held[:, row_id] = sent[pl.ds(ord_id * groups, groups)]

    smem_copy.wait()

    def lane_orders(group):
        place = (iota((1, cols), 1) & (width - 1)) >> 1
        order = jnp.zeros((1, cols), jnp.int32)
        for slot in range(per_slab):
            order = jnp.where(place == slot, slots_smem[0, ord_id * slots_here + group * per_slab + slot], order)
        return order

    def lat_tables(group, part):
        order = lane_orders(group)
        col = iota((1, cols), 1)
        row = iota((out_rows, 1), 0)
        wave = (row >> log2(width)) + lat_id * waves
        same = ((row & (width - 1)) >> 1) == ((col & (width - 1)) >> 1)
        for step in range(3):
            lat = (col >> log2(width)) + part * lat_rows + 1 - step
            phase = wave * (2 * lat + 1) + jnp.where((order & 1) == 0, 0, 3 * n_lat)
            value = cosine(phase, 4 * n_lat) * math.sqrt(2.0 / n_lat)
            lat_tab[step] = jnp.where(same, value, 0.0)

    def tap_factors(group):
        order = lane_orders(group)
        row = iota((16, cols), 0)
        lon_step = (row & 7) - 2
        part_of = iota((16, cols), 1) & 1
        phase = order * lon_step + (n_lon // 4) * (part_of - (row >> 3))
        return cosine(phase, n_lon)

    window_row = iota((lat_rows + 2, cols), 0)
    window_lat = iota((lat_rows + 2, cols), 1) >> log2(width)
    for step in range(3):
        chosen = (window_row == window_lat + 2 - step).astype(F32)
        select[step] = jnp.concatenate([chosen, chosen], axis=0).astype(BF16)

    single_lat = groups == 1 and parts == 1
    if single_lat:
        lat_tables(0, 0)
        factors = tap_factors(0)

    def answer(block):
        first = jnp.maximum(chip + 1, block * per_ready)
        last = (block + 1) * per_ready

        @pl.when(jnp.logical_or(jnp.logical_not(low), block < top // per_ready))
        def _():
            pl.semaphore_wait(ready.at[block], last - first)

        pl.loop(first, last)(lambda other: on_both(other, send))

    start = (chip + 1) // per_ready
    half_block, top_block = half * n_lat_dev // per_ready, top // per_ready
    pl.loop(start, half_block)(answer)

    def answer_top():
        pl.loop(jnp.maximum(start, top_block), chips // per_ready)(answer)

    def answer_rest():
        pl.loop(jnp.maximum(start, half_block), top_block)(answer)

    top_first = jnp.logical_and(low, follower)

    @pl.when(jnp.logical_not(top_first))
    def _():
        answer_rest()

    @pl.when(jnp.logical_and(follower, low))
    def _():
        pl.semaphore_wait(barrier, 2 * n_lat_dev + 1)
        signal(top_sem, sibling)

    @pl.when(jnp.logical_and(leader, low))
    def _():
        pl.semaphore_wait(top_sem, 1)

    answer_top()

    @pl.when(top_first)
    def _():
        answer_rest()

    gain_copy.wait()
    spectral_copy.wait()
    basis_copy.wait()
    filt_arrivals = pltpu.make_async_remote_copy(
        src_ref=filt.at[pl.ds(0, count - 1)], dst_ref=filt.at[pl.ds(0, count - 1)],
        send_sem=filt_send.at[0], recv_sem=filt_recv.at[0],
        device_id=(lat_id, ord_id ^ 1), device_id_type=MESH,
    )
    arrivals = pltpu.make_async_remote_copy(
        src_ref=held.at[:, pl.ds(0, count - 1)], dst_ref=held.at[:, pl.ds(0, count - 1)],
        send_sem=all_send.at[0], recv_sem=all_recv.at[0],
        device_id=(lat_id, ord_id ^ 1), device_id_type=MESH,
    )
    filt_arrivals.wait_recv()

    def build_left(part, factors):
        window = filt[pl.ds(part * lat_rows, lat_rows + 2)]
        high = window.astype(BF16)
        low = (window - high.astype(F32)).astype(BF16)
        both = jnp.concatenate([high.astype(F32), low.astype(F32)], axis=0).T.astype(BF16)
        real, imag = [], []
        for step in range(3):
            first = 5 * step * basis_count
            wide = jnp.dot(both[first:first + 5 * basis_count], select[step], preferred_element_type=F32)
            sums = [None, None]
            for lon_step in range(5):
                values = wide[lon_step * basis_count:(lon_step + 1) * basis_count]
                for which in range(2):
                    term = values * factors[8 * which + lon_step:8 * which + lon_step + 1]
                    sums[which] = term if sums[which] is None else sums[which] + term
            real.append(sums[0])
            imag.append(sums[1])
        even = (iota((width, cols), 0) & 1) == 0
        for b in range(basis_count):
            total = None
            for step in range(3):
                turn = jnp.where(even, real[step][b:b + 1], imag[step][b:b + 1])
                term = lat_tab[step].reshape(waves, width, cols) * turn[None]
                total = term if total is None else total + term
            left[pl.ds(b * out_rows, out_rows)] = total.reshape(out_rows, cols).astype(BF16)

    def latitude(group, part):
        rows = held[group, pl.ds(part * lat_rows, lat_rows)].reshape(cols, channels)
        return jnp.dot(left[...], rows, preferred_element_type=F32)

    def finish(group):
        if single_lat:
            total = latitude(group, 0)
        else:
            factors_here = tap_factors(group)
            mixed[...] = jnp.zeros(mixed.shape, F32)

            def add(part):
                lat_tables(group, part)
                build_left(part, factors_here)
                mixed[...] += latitude(group, part)

            pl.loop(0, parts)(add)
            total = mixed[...]
        total = total.astype(BF16)
        flat = jnp.concatenate([total[b * out_rows:(b + 1) * out_rows] for b in range(basis_count)], axis=1)
        weights = basis[...].reshape(basis_count * channels, channels)
        coefficients = jnp.concatenate(
            [jnp.dot(flat, weights[:, first:first + LANES], preferred_element_type=F32) for first in range(0, channels, LANES)],
            axis=1,
        )
        scaled = (coefficients.reshape(waves, width, channels) * gain[...][:, None, :]).astype(BF16)
        scaled = scaled.reshape(out_rows, channels)
        straight = jnp.dot(scaled, spectral[0], preferred_element_type=F32)
        turned = jnp.dot(scaled, spectral[1], preferred_element_type=F32).reshape(waves, width, channels)
        even = (iota((1, width, channels), 1) & 1) == 0
        turned = jnp.where(even, -pltpu.roll(turned, width - 1, 1), pltpu.roll(turned, 1, 1))
        out_ref[group] = (straight + turned.reshape(out_rows, channels)).astype(BF16)

    if single_lat:
        build_left(0, factors)
    arrivals.wait_recv()
    repeat(groups, finish)
    filt_arrivals.wait_send()
    arrivals.wait_send()


def per_device(field, tap_mask, tap_weight, basis_mix, order_slots, degree_gain, spectral_mix):
    rows_here, n_lon, channels = field.shape
    assert rows_here == 1
    basis_count = basis_mix.shape[0]
    n_lat = degree_gain.shape[0]
    n_orders = order_slots.shape[0]
    n_lat_dev = lax.axis_size("lat")
    n_ord_dev = lax.axis_size("ord")
    slots_here = n_orders // n_ord_dev
    waves = n_lat // n_lat_dev
    per_slab = min(SLAB // 2, slots_here)
    width = 2 * per_slab
    groups = slots_here // per_slab
    lat_rows = min(n_lat, COLUMNS // width)
    block_rows = min(2 * n_orders, 64)
    out_rows = waves * width
    single = groups == 1 and lat_rows == n_lat
    dims = (n_lat_dev, n_ord_dev, n_lat, n_lon, n_orders, channels, basis_count)
    vmem = pl.BlockSpec(memory_space=pltpu.VMEM)
    hbm = pl.BlockSpec(memory_space=pltpu.HBM)
    result = pl.pallas_call(
        functools.partial(kernel, dims),
        out_shape=pltpu.VMEM((groups, out_rows, channels), BF16),
        in_specs=[hbm] * 7,
        out_specs=vmem,
        scratch_shapes=[
            pltpu.VMEM(tap_mask.shape, jnp.int32),
            pltpu.VMEM(tap_weight.shape, F32),
            pltpu.VMEM((1, n_orders), jnp.int32),
            pltpu.SMEM((1, n_orders), jnp.int32),
            pltpu.VMEM((1, n_lon, channels), BF16),
            pltpu.VMEM((basis_count, channels, channels), BF16),
            pltpu.VMEM((waves, channels), F32),
            pltpu.VMEM((2, channels, channels), BF16),
            pltpu.VMEM((block_rows, n_lon), BF16),
            pltpu.VMEM((n_lat + 2, LANES), F32),
            pltpu.VMEM((n_ord_dev * groups, width, channels), BF16),
            pltpu.VMEM((groups, n_lat, width, channels), BF16),
            pltpu.VMEM((3, out_rows, lat_rows * width), F32),
            pltpu.VMEM((3, 2 * (lat_rows + 2), lat_rows * width), BF16),
            pltpu.VMEM((basis_count * out_rows, lat_rows * width), BF16),
            pltpu.VMEM((8, LANES) if single else (basis_count * out_rows, channels), F32),
            pltpu.SemaphoreType.DMA((8,)),
            pltpu.SemaphoreType.DMA((1,)),
            pltpu.SemaphoreType.DMA((1,)),
            pltpu.SemaphoreType.DMA((1,)),
            pltpu.SemaphoreType.DMA((1,)),
            pltpu.SemaphoreType.REGULAR((3 + n_lat // 2 // (1 if n_lat <= 128 else n_lat_dev),)),
        ],
        compiler_params=pltpu.CompilerParams(
            collective_id=0, has_side_effects=True, vmem_limit_bytes=63 * 1024 * 1024
        ),
    )(*[pltpu.with_memory_space_constraint(x, pltpu.HBM) for x in (tap_mask, tap_weight, order_slots.reshape(1, n_orders), field, basis_mix, degree_gain, spectral_mix)])
    result = result.reshape(groups, waves, per_slab, 2, channels)
    return jnp.swapaxes(result, 0, 1).reshape(waves, slots_here, 2, channels)


def solution(mesh):
    in_specs = (
        P(("lat", "ord"), None, None),
        P(("lat", "ord"), None, None),
        P(("lat", "ord"), None, None),
        P(),
        P(),
        P(),
        P(),
    )
    out_specs = P("lat", "ord", None, None)
    return jax.shard_map(
        per_device, mesh=mesh, in_specs=in_specs, out_specs=out_specs, check_vma=False
    )
```

```python
import functools
import math

import jax
import jax.numpy as jnp
from jax import lax
from jax.experimental import pallas as pl
from jax.experimental.pallas import tpu as pltpu
from jax.sharding import PartitionSpec as P

MESH = pl.DeviceIdType.MESH
F32 = jnp.float32
BF16 = jnp.bfloat16
SLAB = 8
COLUMNS = 256
LANES = 128


def log2(n):
    assert n & (n - 1) == 0
    return n.bit_length() - 1


def cosine(phase_int, period):
    q = phase_int & (period - 1)
    r = jnp.minimum(q, period - q)
    x = (period // 4 - r).astype(F32) * (2.0 * math.pi / period)
    x2 = x * x
    total = jnp.full_like(x, -1.0 / math.factorial(11))
    for power, sign in ((9, 1.0), (7, -1.0), (5, 1.0), (3, -1.0), (1, 1.0)):
        total = total * x2 + sign / math.factorial(power)
    return total * x


def iota(shape, dim):
    return lax.broadcasted_iota(jnp.int32, shape, dim)


def repeat(count, body):
    if count == 1:
        body(0)
    else:
        pl.loop(0, count)(body)


def kernel(
    dims,
    mask_hbm, weight_hbm, slots_hbm, field_hbm, basis_hbm, gain_hbm, spectral_hbm,
    out_ref,
    mask_ref, weight_ref, slots_ref, slots_smem, field, basis, gain, spectral, table, filt, sent, held, lat_tab, select, left, mixed,
    local_sem, filt_send, filt_recv, all_send, all_recv, ready,
):
    n_lat_dev, n_ord_dev, n_lat, n_lon, n_orders, channels, basis_count = dims
    lat_id = lax.axis_index("lat")
    ord_id = lax.axis_index("ord")
    row_id = lat_id * n_ord_dev + ord_id
    slots_here = n_orders // n_ord_dev
    waves = n_lat // n_lat_dev
    per_slab = min(SLAB // 2, slots_here)
    width = 2 * per_slab
    groups = slots_here // per_slab
    count = n_lat_dev * n_ord_dev
    lat_rows = min(n_lat, COLUMNS // width)
    parts = n_lat // lat_rows
    cols = lat_rows * width
    out_rows = waves * width

    lat_bits = log2(n_lat_dev)
    lat_mask = n_lat_dev - 1
    levels = n_ord_dev // 2
    chips = levels * n_lat_dev
    level = ord_id >> 1
    chip = level * n_lat_dev + lat_id
    leader = (ord_id & 1) == 1
    follower = (ord_id & 1) == 0
    half = levels // 2
    top = (levels - 1) * n_lat_dev
    low = level < half
    sibling = (lat_id, ord_id ^ 1)
    per_ready = 1 if chips <= 64 else n_lat_dev

    def device(other, core):
        return (other & lat_mask, ((other >> lat_bits) << 1) + core)

    def on_both(other, body):
        body(device(other, 1))
        body(device(other, 0))

    slots_copy = pltpu.make_async_copy(slots_hbm, slots_ref, local_sem.at[0])
    pieces = 2
    piece = n_lon // pieces

    def field_copy(part):
        place = pl.ds(part * piece, piece)
        return pltpu.make_async_copy(field_hbm.at[:, place], field.at[:, place], local_sem.at[8 + part])

    mask_copy = pltpu.make_async_copy(mask_hbm, mask_ref, local_sem.at[2])
    weight_copy = pltpu.make_async_copy(weight_hbm, weight_ref, local_sem.at[3])
    smem_copy = pltpu.make_async_copy(slots_hbm, slots_smem, local_sem.at[4])
    gain_copy = pltpu.make_async_copy(
        gain_hbm.at[pl.ds(pl.multiple_of(lat_id * waves, waves), waves)], gain, local_sem.at[5]
    )
    spectral_copy = pltpu.make_async_copy(spectral_hbm, spectral, local_sem.at[6])
    basis_copy = pltpu.make_async_copy(basis_hbm, basis, local_sem.at[7])
    barrier = pltpu.get_barrier_semaphore()

    def greet(target):
        pl.semaphore_signal(barrier, inc=1, device_id=target, device_id_type=MESH)

    def signal(semaphore, target):
        pl.semaphore_signal(semaphore, inc=1, device_id=target, device_id_type=MESH)

    mask_copy.start()
    weight_copy.start()
    slots_copy.start()
    for part in range(pieces):
        field_copy(part).start()
    greet(sibling)
    pl.loop(chip + 1, chips)(lambda other: greet(device(other, 1)))

    @pl.when(chip == 0)
    def _():
        pl.loop(half * n_lat_dev, chips)(lambda other: greet(device(other, 0)))

    @pl.when(level == levels - 1)
    def _():
        pl.loop(0, half * n_lat_dev)(lambda other: greet(device(other, 0)))

    smem_copy.start()
    basis_copy.start()
    gain_copy.start()
    spectral_copy.start()

    early_sem, known_sem, top_sem = ready.at[chips // per_ready], ready.at[chips // per_ready + 1], ready.at[chips // per_ready + 2]

    @pl.when(jnp.logical_and(follower, jnp.logical_not(low)))
    def _():
        pl.semaphore_wait(barrier, 3)
        signal(early_sem, sibling)

    filt[pl.ds(0, 1)] = jnp.zeros((1, LANES), F32)
    filt[pl.ds(n_lat + 1, 1)] = jnp.zeros((1, LANES), F32)

    mask_copy.wait()
    weight_copy.wait()
    taps = mask_ref[0].astype(F32) * weight_ref[0]
    tap_count = taps.shape[1]
    lane = iota((basis_count, LANES), 1)
    spread = jnp.zeros((basis_count, LANES), F32)
    for tap in range(tap_count):
        spread = jnp.where(lane // basis_count == tap, taps[:, tap:tap + 1], spread)
    spread = jnp.where(lane % basis_count == iota((basis_count, LANES), 0), spread, 0.0)
    filt[pl.ds(row_id + 1, 1)] = jnp.sum(spread, axis=0, keepdims=True)

    def send_filters(target):
        pltpu.make_async_remote_copy(
            src_ref=filt.at[pl.ds(row_id + 1, 1)], dst_ref=filt.at[pl.ds(row_id + 1, 1)],
            send_sem=filt_send.at[0], recv_sem=filt_recv.at[0],
            device_id=target, device_id_type=MESH,
        ).start()

    def send_rows(target):
        pltpu.make_async_remote_copy(
            src_ref=sent.at[pl.ds(target[1] * groups, groups)], dst_ref=held.at[:, row_id],
            send_sem=all_send.at[0], recv_sem=all_recv.at[0],
            device_id=target, device_id_type=MESH,
        ).start()

    def send(target):
        send_filters(target)
        send_rows(target)


    @pl.when(jnp.logical_and(leader, jnp.logical_not(low)))
    def _():
        pl.semaphore_wait(early_sem, 1)

    @pl.when(jnp.logical_not(low))
    def _():
        send_filters(device(0, 0))
        send_filters(device(0, 1))

    slots_copy.wait()
    orders = slots_ref[...]
    block_rows = table.shape[0]

    def dft_block(start):
        row = iota((block_rows, 1), 0) + start
        found = iota((block_rows, n_orders), 1) == row >> 1
        order = jnp.sum(jnp.where(found, orders.astype(F32), 0.0), axis=1, keepdims=True).astype(jnp.int32)
        phase = order * iota((block_rows, n_lon), 1) + (n_lon // 4) * (row & 1)
        table[...] = (cosine(phase, n_lon) * (1.0 / math.sqrt(n_lon))).astype(BF16)

    single_dft = block_rows == 2 * n_orders
    if single_dft:
        dft_block(0)
    slabs = block_rows // width

    for part in range(pieces):
        field_copy(part).wait()

    def transform(block):
        if not single_dft:
            dft_block(block * block_rows)
        rows = jnp.dot(table[...], field[0], preferred_element_type=F32).astype(BF16)
        sent[pl.ds(block * slabs, slabs)] = rows.reshape(slabs, width, channels)

    def send_first():
        @pl.when(jnp.logical_not(low))
        def _():
            send_rows(device(0, 0))
            send_rows(device(0, 1))

    def transform_rows(first, last):
        rows = jnp.dot(table[first:last], field[0], preferred_element_type=F32).astype(BF16)
        sent[first // width:last // width] = rows.reshape((last - first) // width, width, channels)

    first_rows = 4 * slots_here
    if single_dft and first_rows % 16 == 0 and first_rows < block_rows:
        transform_rows(0, first_rows)
        send_first()
        transform_rows(first_rows, block_rows)
    else:
        repeat(2 * n_orders // block_rows, transform)
        send_first()

    @pl.when(leader)
    def _():
        pl.semaphore_wait(barrier, 2 * chip + 1)
        signal(known_sem, sibling)
        block = chip // per_ready
        first = jnp.where(level == levels - 1, half * n_lat_dev, 0)
        pl.loop(first, chip)(lambda other: on_both(other, lambda target: signal(ready.at[block], target)))

    @pl.when(follower)
    def _():
        pl.semaphore_wait(known_sem, 1)

    pl.loop(jnp.where(low, 0, 1), chip)(lambda other: on_both(other, send))
    send(sibling)
    held[:, row_id] = sent[pl.ds(ord_id * groups, groups)]

    smem_copy.wait()

    def lane_orders(group):
        place = (iota((1, cols), 1) & (width - 1)) >> 1
        order = jnp.zeros((1, cols), jnp.int32)
        for slot in range(per_slab):
            order = jnp.where(place == slot, slots_smem[0, ord_id * slots_here + group * per_slab + slot], order)
        return order

    def lat_tables(group, part):
        order = lane_orders(group)
        col = iota((1, cols), 1)
        row = iota((out_rows, 1), 0)
        wave = (row >> log2(width)) + lat_id * waves
        same = ((row & (width - 1)) >> 1) == ((col & (width - 1)) >> 1)
        for step in range(3):
            lat = (col >> log2(width)) + part * lat_rows + 1 - step
            phase = wave * (2 * lat + 1) + jnp.where((order & 1) == 0, 0, 3 * n_lat)
            value = cosine(phase, 4 * n_lat) * math.sqrt(2.0 / n_lat)
            lat_tab[step] = jnp.where(same, value, 0.0)

    def tap_factors(group):
        order = lane_orders(group)
        row = iota((16, cols), 0)
        lon_step = (row & 7) - 2
        part_of = iota((16, cols), 1) & 1
        phase = order * lon_step + (n_lon // 4) * (part_of - (row >> 3))
        return cosine(phase, n_lon)

    window_row = iota((lat_rows + 2, cols), 0)
    window_lat = iota((lat_rows + 2, cols), 1) >> log2(width)
    for step in range(3):
        chosen = (window_row == window_lat + 2 - step).astype(F32)
        select[step] = jnp.concatenate([chosen, chosen], axis=0).astype(BF16)

    single_lat = groups == 1 and parts == 1
    if single_lat:
        lat_tables(0, 0)
        factors = tap_factors(0)

    def answer(block):
        first = jnp.maximum(chip + 1, block * per_ready)
        last = (block + 1) * per_ready

        @pl.when(jnp.logical_or(jnp.logical_not(low), block < top // per_ready))
        def _():
            pl.semaphore_wait(ready.at[block], last - first)

        pl.loop(first, last)(lambda other: on_both(other, send))

    start = (chip + 1) // per_ready
    half_block, top_block = half * n_lat_dev // per_ready, top // per_ready
    pl.loop(start, half_block)(answer)

    def answer_top():
        pl.loop(jnp.maximum(start, top_block), chips // per_ready)(answer)

    def answer_rest():
        pl.loop(jnp.maximum(start, half_block), top_block)(answer)

    top_first = jnp.logical_and(low, follower)

    @pl.when(jnp.logical_not(top_first))
    def _():
        answer_rest()

    @pl.when(jnp.logical_and(follower, low))
    def _():
        pl.semaphore_wait(barrier, 2 * n_lat_dev + 1)
        signal(top_sem, sibling)

    @pl.when(jnp.logical_and(leader, low))
    def _():
        pl.semaphore_wait(top_sem, 1)

    answer_top()

    @pl.when(top_first)
    def _():
        answer_rest()

    gain_copy.wait()
    spectral_copy.wait()
    basis_copy.wait()
    filt_arrivals = pltpu.make_async_remote_copy(
        src_ref=filt.at[pl.ds(0, count - 1)], dst_ref=filt.at[pl.ds(0, count - 1)],
        send_sem=filt_send.at[0], recv_sem=filt_recv.at[0],
        device_id=(lat_id, ord_id ^ 1), device_id_type=MESH,
    )
    arrivals = pltpu.make_async_remote_copy(
        src_ref=held.at[:, pl.ds(0, count - 1)], dst_ref=held.at[:, pl.ds(0, count - 1)],
        send_sem=all_send.at[0], recv_sem=all_recv.at[0],
        device_id=(lat_id, ord_id ^ 1), device_id_type=MESH,
    )
    filt_arrivals.wait_recv()

    def build_left(part, factors):
        window = filt[pl.ds(part * lat_rows, lat_rows + 2)]
        high = window.astype(BF16)
        low = (window - high.astype(F32)).astype(BF16)
        both = jnp.concatenate([high.astype(F32), low.astype(F32)], axis=0).T.astype(BF16)
        real, imag = [], []
        for step in range(3):
            first = 5 * step * basis_count
            wide = jnp.dot(both[first:first + 5 * basis_count], select[step], preferred_element_type=F32)
            sums = [None, None]
            for lon_step in range(5):
                values = wide[lon_step * basis_count:(lon_step + 1) * basis_count]
                for which in range(2):
                    term = values * factors[8 * which + lon_step:8 * which + lon_step + 1]
                    sums[which] = term if sums[which] is None else sums[which] + term
            real.append(sums[0])
            imag.append(sums[1])
        even = (iota((width, cols), 0) & 1) == 0
        for b in range(basis_count):
            total = None
            for step in range(3):
                turn = jnp.where(even, real[step][b:b + 1], imag[step][b:b + 1])
                term = lat_tab[step].reshape(waves, width, cols) * turn[None]
                total = term if total is None else total + term
            left[pl.ds(b * out_rows, out_rows)] = total.reshape(out_rows, cols).astype(BF16)

    def latitude(group, part):
        rows = held[group, pl.ds(part * lat_rows, lat_rows)].reshape(cols, channels)
        return jnp.dot(left[...], rows, preferred_element_type=F32)

    def finish(group):
        if single_lat:
            total = latitude(group, 0)
        else:
            factors_here = tap_factors(group)
            mixed[...] = jnp.zeros(mixed.shape, F32)

            def add(part):
                lat_tables(group, part)
                build_left(part, factors_here)
                mixed[...] += latitude(group, part)

            pl.loop(0, parts)(add)
            total = mixed[...]
        total = total.astype(BF16)
        flat = jnp.concatenate([total[b * out_rows:(b + 1) * out_rows] for b in range(basis_count)], axis=1)
        weights = basis[...].reshape(basis_count * channels, channels)
        coefficients = jnp.concatenate(
            [jnp.dot(flat, weights[:, first:first + LANES], preferred_element_type=F32) for first in range(0, channels, LANES)],
            axis=1,
        )
        scaled = (coefficients.reshape(waves, width, channels) * gain[...][:, None, :]).astype(BF16)
        scaled = scaled.reshape(out_rows, channels)
        straight = jnp.dot(scaled, spectral[0], preferred_element_type=F32)
        turned = jnp.dot(scaled, spectral[1], preferred_element_type=F32).reshape(waves, width, channels)
        even = (iota((1, width, channels), 1) & 1) == 0
        turned = jnp.where(even, -pltpu.roll(turned, width - 1, 1), pltpu.roll(turned, 1, 1))
        out_ref[group] = (straight + turned.reshape(out_rows, channels)).astype(BF16)

    if single_lat:
        build_left(0, factors)
    arrivals.wait_recv()
    repeat(groups, finish)
    filt_arrivals.wait_send()
    arrivals.wait_send()


def per_device(field, tap_mask, tap_weight, basis_mix, order_slots, degree_gain, spectral_mix):
    rows_here, n_lon, channels = field.shape
    assert rows_here == 1
    basis_count = basis_mix.shape[0]
    n_lat = degree_gain.shape[0]
    n_orders = order_slots.shape[0]
    n_lat_dev = lax.axis_size("lat")
    n_ord_dev = lax.axis_size("ord")
    slots_here = n_orders // n_ord_dev
    waves = n_lat // n_lat_dev
    per_slab = min(SLAB // 2, slots_here)
    width = 2 * per_slab
    groups = slots_here // per_slab
    lat_rows = min(n_lat, COLUMNS // width)
    block_rows = min(2 * n_orders, 64)
    out_rows = waves * width
    single = groups == 1 and lat_rows == n_lat
    dims = (n_lat_dev, n_ord_dev, n_lat, n_lon, n_orders, channels, basis_count)
    vmem = pl.BlockSpec(memory_space=pltpu.VMEM)
    hbm = pl.BlockSpec(memory_space=pltpu.HBM)
    result = pl.pallas_call(
        functools.partial(kernel, dims),
        out_shape=pltpu.VMEM((groups, out_rows, channels), BF16),
        in_specs=[hbm] * 7,
        out_specs=vmem,
        scratch_shapes=[
            pltpu.VMEM(tap_mask.shape, jnp.int32),
            pltpu.VMEM(tap_weight.shape, F32),
            pltpu.VMEM((1, n_orders), jnp.int32),
            pltpu.SMEM((1, n_orders), jnp.int32),
            pltpu.VMEM((1, n_lon, channels), BF16),
            pltpu.VMEM((basis_count, channels, channels), BF16),
            pltpu.VMEM((waves, channels), F32),
            pltpu.VMEM((2, channels, channels), BF16),
            pltpu.VMEM((block_rows, n_lon), BF16),
            pltpu.VMEM((n_lat + 2, LANES), F32),
            pltpu.VMEM((n_ord_dev * groups, width, channels), BF16),
            pltpu.VMEM((groups, n_lat, width, channels), BF16),
            pltpu.VMEM((3, out_rows, lat_rows * width), F32),
            pltpu.VMEM((3, 2 * (lat_rows + 2), lat_rows * width), BF16),
            pltpu.VMEM((basis_count * out_rows, lat_rows * width), BF16),
            pltpu.VMEM((8, LANES) if single else (basis_count * out_rows, channels), F32),
            pltpu.SemaphoreType.DMA((10,)),
            pltpu.SemaphoreType.DMA((1,)),
            pltpu.SemaphoreType.DMA((1,)),
            pltpu.SemaphoreType.DMA((1,)),
            pltpu.SemaphoreType.DMA((1,)),
            pltpu.SemaphoreType.REGULAR((3 + n_lat // 2 // (1 if n_lat <= 128 else n_lat_dev),)),
        ],
        compiler_params=pltpu.CompilerParams(
            collective_id=0, has_side_effects=True, vmem_limit_bytes=63 * 1024 * 1024
        ),
    )(*[pltpu.with_memory_space_constraint(x, pltpu.HBM) for x in (tap_mask, tap_weight, order_slots.reshape(1, n_orders), field, basis_mix, degree_gain, spectral_mix)])
    result = result.reshape(groups, waves, per_slab, 2, channels)
    return jnp.swapaxes(result, 0, 1).reshape(waves, slots_here, 2, channels)


def solution(mesh):
    in_specs = (
        P(("lat", "ord"), None, None),
        P(("lat", "ord"), None, None),
        P(("lat", "ord"), None, None),
        P(),
        P(),
        P(),
        P(),
    )
    out_specs = P("lat", "ord", None, None)
    return jax.shard_map(
        per_device, mesh=mesh, in_specs=in_specs, out_specs=out_specs, check_vma=False
    )
```

```python
import functools
import math

import jax
import jax.numpy as jnp
from jax import lax
from jax.experimental import pallas as pl
from jax.experimental.pallas import tpu as pltpu
from jax.sharding import PartitionSpec as P

MESH = pl.DeviceIdType.MESH
F32 = jnp.float32
BF16 = jnp.bfloat16
SLAB = 8
COLUMNS = 256
LANES = 128


def log2(n):
    assert n & (n - 1) == 0
    return n.bit_length() - 1


def cosine(phase_int, period):
    q = phase_int & (period - 1)
    r = jnp.minimum(q, period - q)
    x = (period // 4 - r).astype(F32) * (2.0 * math.pi / period)
    x2 = x * x
    total = jnp.full_like(x, -1.0 / math.factorial(11))
    for power, sign in ((9, 1.0), (7, -1.0), (5, 1.0), (3, -1.0), (1, 1.0)):
        total = total * x2 + sign / math.factorial(power)
    return total * x


def iota(shape, dim):
    return lax.broadcasted_iota(jnp.int32, shape, dim)


def repeat(count, body):
    if count == 1:
        body(0)
    else:
        pl.loop(0, count)(body)


def kernel(
    dims,
    mask_hbm, weight_hbm, slots_hbm, field_hbm, basis_hbm, gain_hbm, spectral_hbm,
    out_ref,
    mask_ref, weight_ref, slots_ref, slots_smem, field, basis, gain, spectral, table, filt, sent, held, lat_tab, select, left, mixed,
    local_sem, filt_send, filt_recv, all_send, all_recv, ready,
):
    n_lat_dev, n_ord_dev, n_lat, n_lon, n_orders, channels, basis_count = dims
    lat_id = lax.axis_index("lat")
    ord_id = lax.axis_index("ord")
    row_id = lat_id * n_ord_dev + ord_id
    slots_here = n_orders // n_ord_dev
    waves = n_lat // n_lat_dev
    per_slab = min(SLAB // 2, slots_here)
    width = 2 * per_slab
    groups = slots_here // per_slab
    count = n_lat_dev * n_ord_dev
    lat_rows = min(n_lat, COLUMNS // width)
    parts = n_lat // lat_rows
    cols = lat_rows * width
    out_rows = waves * width

    lat_bits = log2(n_lat_dev)
    lat_mask = n_lat_dev - 1
    levels = n_ord_dev // 2
    chips = levels * n_lat_dev
    level = ord_id >> 1
    chip = level * n_lat_dev + lat_id
    leader = (ord_id & 1) == 1
    follower = (ord_id & 1) == 0
    half = levels // 2
    top = (levels - 1) * n_lat_dev
    low = level < half
    sibling = (lat_id, ord_id ^ 1)
    per_ready = 1 if chips <= 64 else n_lat_dev

    def device(other, core):
        return (other & lat_mask, ((other >> lat_bits) << 1) + core)

    def on_both(other, body):
        body(device(other, 1))
        body(device(other, 0))

    slots_copy = pltpu.make_async_copy(slots_hbm, slots_ref, local_sem.at[0])
    pieces = 2
    piece = n_lon // pieces

    def field_copy(part):
        place = pl.ds(part * piece, piece)
        return pltpu.make_async_copy(field_hbm.at[:, place], field.at[:, place], local_sem.at[8 + part])

    mask_copy = pltpu.make_async_copy(mask_hbm, mask_ref, local_sem.at[2])
    weight_copy = pltpu.make_async_copy(weight_hbm, weight_ref, local_sem.at[3])
    smem_copy = pltpu.make_async_copy(slots_hbm, slots_smem, local_sem.at[4])
    gain_copy = pltpu.make_async_copy(
        gain_hbm.at[pl.ds(pl.multiple_of(lat_id * waves, waves), waves)], gain, local_sem.at[5]
    )
    spectral_copy = pltpu.make_async_copy(spectral_hbm, spectral, local_sem.at[6])
    basis_copy = pltpu.make_async_copy(basis_hbm, basis, local_sem.at[7])
    barrier = pltpu.get_barrier_semaphore()

    def greet(target):
        pl.semaphore_signal(barrier, inc=1, device_id=target, device_id_type=MESH)

    def signal(semaphore, target):
        pl.semaphore_signal(semaphore, inc=1, device_id=target, device_id_type=MESH)

    mask_copy.start()
    weight_copy.start()
    slots_copy.start()
    for part in range(pieces):
        field_copy(part).start()
    greet(sibling)
    pl.loop(chip + 1, chips)(lambda other: greet(device(other, 1)))

    @pl.when(chip == 0)
    def _():
        pl.loop(half * n_lat_dev, chips)(lambda other: greet(device(other, 0)))

    @pl.when(level == levels - 1)
    def _():
        pl.loop(0, half * n_lat_dev)(lambda other: greet(device(other, 0)))

    smem_copy.start()
    basis_copy.start()
    gain_copy.start()
    spectral_copy.start()

    early_sem, known_sem, top_sem = ready.at[chips // per_ready], ready.at[chips // per_ready + 1], ready.at[chips // per_ready + 2]

    @pl.when(jnp.logical_and(follower, jnp.logical_not(low)))
    def _():
        pl.semaphore_wait(barrier, 3)
        signal(early_sem, sibling)

    filt[pl.ds(0, 1)] = jnp.zeros((1, LANES), F32)
    filt[pl.ds(n_lat + 1, 1)] = jnp.zeros((1, LANES), F32)

    mask_copy.wait()
    weight_copy.wait()
    taps = mask_ref[0].astype(F32) * weight_ref[0]
    tap_count = taps.shape[1]
    lane = iota((basis_count, LANES), 1)
    spread = jnp.zeros((basis_count, LANES), F32)
    for tap in range(tap_count):
        spread = jnp.where(lane // basis_count == tap, taps[:, tap:tap + 1], spread)
    spread = jnp.where(lane % basis_count == iota((basis_count, LANES), 0), spread, 0.0)
    filt[pl.ds(row_id + 1, 1)] = jnp.sum(spread, axis=0, keepdims=True)

    def send_filters(target):
        pltpu.make_async_remote_copy(
            src_ref=filt.at[pl.ds(row_id + 1, 1)], dst_ref=filt.at[pl.ds(row_id + 1, 1)],
            send_sem=filt_send.at[0], recv_sem=filt_recv.at[0],
            device_id=target, device_id_type=MESH,
        ).start()

    def send_rows(target):
        pltpu.make_async_remote_copy(
            src_ref=sent.at[pl.ds(target[1] * groups, groups)], dst_ref=held.at[:, row_id],
            send_sem=all_send.at[0], recv_sem=all_recv.at[0],
            device_id=target, device_id_type=MESH,
        ).start()

    def send(target):
        send_filters(target)
        send_rows(target)


    @pl.when(jnp.logical_and(leader, jnp.logical_not(low)))
    def _():
        pl.semaphore_wait(early_sem, 1)

    @pl.when(jnp.logical_not(low))
    def _():
        send_filters(device(0, 0))
        send_filters(device(0, 1))

    slots_copy.wait()
    orders = slots_ref[...]
    block_rows = table.shape[0]

    def dft_block(start):
        row = iota((block_rows, 1), 0) + start
        found = iota((block_rows, n_orders), 1) == row >> 1
        order = jnp.sum(jnp.where(found, orders.astype(F32), 0.0), axis=1, keepdims=True).astype(jnp.int32)
        phase = order * iota((block_rows, n_lon), 1) + (n_lon // 4) * (row & 1)
        table[...] = (cosine(phase, n_lon) * (1.0 / math.sqrt(n_lon))).astype(BF16)

    single_dft = block_rows == 2 * n_orders
    if single_dft:
        dft_block(0)
    slabs = block_rows // width

    for part in range(pieces):
        field_copy(part).wait()

    def transform(block):
        if not single_dft:
            dft_block(block * block_rows)
        rows = jnp.dot(table[...], field[0], preferred_element_type=F32).astype(BF16)
        sent[pl.ds(block * slabs, slabs)] = rows.reshape(slabs, width, channels)

    def send_first():
        @pl.when(jnp.logical_not(low))
        def _():
            send_rows(device(0, 0))
            send_rows(device(0, 1))

    def transform_rows(first, last):
        rows = jnp.dot(table[first:last], field[0], preferred_element_type=F32).astype(BF16)
        sent[first // width:last // width] = rows.reshape((last - first) // width, width, channels)

    first_rows = 4 * slots_here
    if single_dft and first_rows % 16 == 0 and first_rows < block_rows:
        transform_rows(0, first_rows)
        send_first()
        transform_rows(first_rows, block_rows)
    else:
        repeat(2 * n_orders // block_rows, transform)
        send_first()

    @pl.when(leader)
    def _():
        pl.semaphore_wait(barrier, 2 * chip + 1)
        signal(known_sem, sibling)
        block = chip // per_ready
        first = jnp.where(level == levels - 1, half * n_lat_dev, 0)
        pl.loop(first, chip)(lambda other: on_both(other, lambda target: signal(ready.at[block], target)))

    @pl.when(follower)
    def _():
        pl.semaphore_wait(known_sem, 1)

    pl.loop(jnp.where(low, 0, 1), chip)(lambda other: on_both(other, send))
    send(sibling)
    held[:, row_id] = sent[pl.ds(ord_id * groups, groups)]

    smem_copy.wait()

    def lane_orders(group):
        place = (iota((1, cols), 1) & (width - 1)) >> 1
        order = jnp.zeros((1, cols), jnp.int32)
        for slot in range(per_slab):
            order = jnp.where(place == slot, slots_smem[0, ord_id * slots_here + group * per_slab + slot], order)
        return order

    def lat_tables(group, part):
        order = lane_orders(group)
        col = iota((1, cols), 1)
        row = iota((out_rows, 1), 0)
        wave = (row >> log2(width)) + lat_id * waves
        same = ((row & (width - 1)) >> 1) == ((col & (width - 1)) >> 1)
        for step in range(3):
            lat = (col >> log2(width)) + part * lat_rows + 1 - step
            phase = wave * (2 * lat + 1) + jnp.where((order & 1) == 0, 0, 3 * n_lat)
            value = cosine(phase, 4 * n_lat) * math.sqrt(2.0 / n_lat)
            lat_tab[step] = jnp.where(same, value, 0.0)

    def tap_factors(group):
        order = lane_orders(group)
        row = iota((16, cols), 0)
        lon_step = (row & 7) - 2
        part_of = iota((16, cols), 1) & 1
        phase = order * lon_step + (n_lon // 4) * (part_of - (row >> 3))
        return cosine(phase, n_lon)

    window_row = iota((lat_rows + 2, cols), 0)
    window_lat = iota((lat_rows + 2, cols), 1) >> log2(width)
    for step in range(3):
        chosen = (window_row == window_lat + 2 - step).astype(F32)
        select[step] = chosen.astype(BF16)

    single_lat = groups == 1 and parts == 1
    if single_lat:
        lat_tables(0, 0)
        factors = tap_factors(0)

    def answer(block):
        first = jnp.maximum(chip + 1, block * per_ready)
        last = (block + 1) * per_ready

        @pl.when(jnp.logical_or(jnp.logical_not(low), block < top // per_ready))
        def _():
            pl.semaphore_wait(ready.at[block], last - first)

        pl.loop(first, last)(lambda other: on_both(other, send))

    start = (chip + 1) // per_ready
    half_block, top_block = half * n_lat_dev // per_ready, top // per_ready
    pl.loop(start, half_block)(answer)

    def answer_top():
        pl.loop(jnp.maximum(start, top_block), chips // per_ready)(answer)

    def answer_rest():
        pl.loop(jnp.maximum(start, half_block), top_block)(answer)

    top_first = jnp.logical_and(low, follower)

    @pl.when(jnp.logical_not(top_first))
    def _():
        answer_rest()

    @pl.when(jnp.logical_and(follower, low))
    def _():
        pl.semaphore_wait(barrier, 2 * n_lat_dev + 1)
        signal(top_sem, sibling)

    @pl.when(jnp.logical_and(leader, low))
    def _():
        pl.semaphore_wait(top_sem, 1)

    answer_top()

    @pl.when(top_first)
    def _():
        answer_rest()

    gain_copy.wait()
    spectral_copy.wait()
    basis_copy.wait()
    filt_arrivals = pltpu.make_async_remote_copy(
        src_ref=filt.at[pl.ds(0, count - 1)], dst_ref=filt.at[pl.ds(0, count - 1)],
        send_sem=filt_send.at[0], recv_sem=filt_recv.at[0],
        device_id=(lat_id, ord_id ^ 1), device_id_type=MESH,
    )
    arrivals = pltpu.make_async_remote_copy(
        src_ref=held.at[:, pl.ds(0, count - 1)], dst_ref=held.at[:, pl.ds(0, count - 1)],
        send_sem=all_send.at[0], recv_sem=all_recv.at[0],
        device_id=(lat_id, ord_id ^ 1), device_id_type=MESH,
    )
    filt_arrivals.wait_recv()

    def build_left(part, factors):
        window = filt[pl.ds(part * lat_rows, lat_rows + 2)]
        both = window.T.astype(BF16)
        real, imag = [], []
        for step in range(3):
            first = 5 * step * basis_count
            wide = jnp.dot(both[first:first + 5 * basis_count], select[step], preferred_element_type=F32)
            sums = [None, None]
            for lon_step in range(5):
                values = wide[lon_step * basis_count:(lon_step + 1) * basis_count]
                for which in range(2):
                    term = values * factors[8 * which + lon_step:8 * which + lon_step + 1]
                    sums[which] = term if sums[which] is None else sums[which] + term
            real.append(sums[0])
            imag.append(sums[1])
        even = (iota((width, cols), 0) & 1) == 0
        for b in range(basis_count):
            total = None
            for step in range(3):
                turn = jnp.where(even, real[step][b:b + 1], imag[step][b:b + 1])
                term = lat_tab[step].reshape(waves, width, cols) * turn[None]
                total = term if total is None else total + term
            left[pl.ds(b * out_rows, out_rows)] = total.reshape(out_rows, cols).astype(BF16)

    def latitude(group, part):
        rows = held[group, pl.ds(part * lat_rows, lat_rows)].reshape(cols, channels)
        return jnp.dot(left[...], rows, preferred_element_type=F32)

    def finish(group):
        if single_lat:
            total = latitude(group, 0)
        else:
            factors_here = tap_factors(group)
            mixed[...] = jnp.zeros(mixed.shape, F32)

            def add(part):
                lat_tables(group, part)
                build_left(part, factors_here)
                mixed[...] += latitude(group, part)

            pl.loop(0, parts)(add)
            total = mixed[...]
        total = total.astype(BF16)
        flat = jnp.concatenate([total[b * out_rows:(b + 1) * out_rows] for b in range(basis_count)], axis=1)
        weights = basis[...].reshape(basis_count * channels, channels)
        coefficients = jnp.concatenate(
            [jnp.dot(flat, weights[:, first:first + LANES], preferred_element_type=F32) for first in range(0, channels, LANES)],
            axis=1,
        )
        scaled = (coefficients.reshape(waves, width, channels) * gain[...][:, None, :]).astype(BF16)
        scaled = scaled.reshape(out_rows, channels)
        straight = jnp.dot(scaled, spectral[0], preferred_element_type=F32)
        turned = jnp.dot(scaled, spectral[1], preferred_element_type=F32).reshape(waves, width, channels)
        even = (iota((1, width, channels), 1) & 1) == 0
        turned = jnp.where(even, -pltpu.roll(turned, width - 1, 1), pltpu.roll(turned, 1, 1))
        out_ref[group] = (straight + turned.reshape(out_rows, channels)).astype(BF16)

    if single_lat:
        build_left(0, factors)
    arrivals.wait_recv()
    repeat(groups, finish)
    filt_arrivals.wait_send()
    arrivals.wait_send()


def per_device(field, tap_mask, tap_weight, basis_mix, order_slots, degree_gain, spectral_mix):
    rows_here, n_lon, channels = field.shape
    assert rows_here == 1
    basis_count = basis_mix.shape[0]
    n_lat = degree_gain.shape[0]
    n_orders = order_slots.shape[0]
    n_lat_dev = lax.axis_size("lat")
    n_ord_dev = lax.axis_size("ord")
    slots_here = n_orders // n_ord_dev
    waves = n_lat // n_lat_dev
    per_slab = min(SLAB // 2, slots_here)
    width = 2 * per_slab
    groups = slots_here // per_slab
    lat_rows = min(n_lat, COLUMNS // width)
    block_rows = min(2 * n_orders, 64)
    out_rows = waves * width
    single = groups == 1 and lat_rows == n_lat
    dims = (n_lat_dev, n_ord_dev, n_lat, n_lon, n_orders, channels, basis_count)
    vmem = pl.BlockSpec(memory_space=pltpu.VMEM)
    hbm = pl.BlockSpec(memory_space=pltpu.HBM)
    result = pl.pallas_call(
        functools.partial(kernel, dims),
        out_shape=pltpu.VMEM((groups, out_rows, channels), BF16),
        in_specs=[hbm] * 7,
        out_specs=vmem,
        scratch_shapes=[
            pltpu.VMEM(tap_mask.shape, jnp.int32),
            pltpu.VMEM(tap_weight.shape, F32),
            pltpu.VMEM((1, n_orders), jnp.int32),
            pltpu.SMEM((1, n_orders), jnp.int32),
            pltpu.VMEM((1, n_lon, channels), BF16),
            pltpu.VMEM((basis_count, channels, channels), BF16),
            pltpu.VMEM((waves, channels), F32),
            pltpu.VMEM((2, channels, channels), BF16),
            pltpu.VMEM((block_rows, n_lon), BF16),
            pltpu.VMEM((n_lat + 2, LANES), F32),
            pltpu.VMEM((n_ord_dev * groups, width, channels), BF16),
            pltpu.VMEM((groups, n_lat, width, channels), BF16),
            pltpu.VMEM((3, out_rows, lat_rows * width), F32),
            pltpu.VMEM((3, lat_rows + 2, lat_rows * width), BF16),
            pltpu.VMEM((basis_count * out_rows, lat_rows * width), BF16),
            pltpu.VMEM((8, LANES) if single else (basis_count * out_rows, channels), F32),
            pltpu.SemaphoreType.DMA((10,)),
            pltpu.SemaphoreType.DMA((1,)),
            pltpu.SemaphoreType.DMA((1,)),
            pltpu.SemaphoreType.DMA((1,)),
            pltpu.SemaphoreType.DMA((1,)),
            pltpu.SemaphoreType.REGULAR((3 + n_lat // 2 // (1 if n_lat <= 128 else n_lat_dev),)),
        ],
        compiler_params=pltpu.CompilerParams(
            collective_id=0, has_side_effects=True, vmem_limit_bytes=63 * 1024 * 1024
        ),
    )(*[pltpu.with_memory_space_constraint(x, pltpu.HBM) for x in (tap_mask, tap_weight, order_slots.reshape(1, n_orders), field, basis_mix, degree_gain, spectral_mix)])
    result = result.reshape(groups, waves, per_slab, 2, channels)
    return jnp.swapaxes(result, 0, 1).reshape(waves, slots_here, 2, channels)


def solution(mesh):
    in_specs = (
        P(("lat", "ord"), None, None),
        P(("lat", "ord"), None, None),
        P(("lat", "ord"), None, None),
        P(),
        P(),
        P(),
        P(),
    )
    out_specs = P("lat", "ord", None, None)
    return jax.shard_map(
        per_device, mesh=mesh, in_specs=in_specs, out_specs=out_specs, check_vma=False
    )
```
